32 devices in a mesh: grp: 2 (over y), tm: 4 (over z), row: 4 (over x, core).
Axes of the slice: x: 2, y: 2, z: 4, core: 2. Of those that a mesh axis runs over, the one named last changes fastest.
Arguments:
- terminal: bfloat16 [8, 2, 2048, 2048], P(('grp', 'tm'), None, None, 'row'), parts along dimension 0, may hold values from -12 to 12, as said below
- controls: float32 [8, 2], P(('grp', 'tm')), parts along dimension 0, may hold values from -3 to 3
- ham_blocks: bfloat16 [2, 64, 2, 32, 32], replicated, may hold values from -0.5 to 0.5
- ham_cols: int32 [2, 64], replicated, may hold values from 0 to 63, each once within a row
- jump_blocks: bfloat16 [64, 2, 32, 32], replicated, may hold values from -0.75 to 0.75
- jump_cols: int32 [2, 64], replicated, may hold values from 0 to 63, each once within a row
Outputs:
- new_cpoint: bfloat16 [8, 2, 2048, 2048], P(('grp', 'tm'), None, None, 'row'), parts along dimension 0
- new_fpoint: bfloat16 [8, 2, 2048, 2048], P(('grp', 'tm'), None, None, 'row'), parts along dimension 0
The draws below stay inside these ranges and needn't reach their ends.
There are 2 independent parts, one for each index of `grp`. The reference program is written for one: setup_inputs(seed, part) draws one part's arguments, and reference() takes and returns one part's arrays. A program takes and returns all parts, laid end to end along the dimension named above; an argument that names none is the same for every part. Nothing has to cross between parts.
Inputs may be any that keep to these rules, and one draw needn't show every extreme that they name: `terminal`: every interval's state is Hermitian: the real part is symmetric and the imaginary part antisymmetric. Each row of ham_cols names every block column once. Each row of jump_cols names every block column once.
All inputs are finite; a program needn't handle non-finite values.
Results may differ from the reference program's by a relative error of at most 0.0041.
Values may be sent and summed in bfloat16 or wider, within the bound.
No kernel may reach another device: no remote copies, remote signals or barrier semaphores. Data moves between devices by JAX's collectives and lax.ppermute only.
A program may use at most 192 MiB of HBM per device.

```python
import jax
import jax.numpy as jnp
from jax import lax

NDIM = 2048
NBLK = 64
KH = 2
KJ = 2
CF = 2
BS = 32
NINT = 4


def draw_terminal(key, part):
    key = jax.random.fold_in(key, 11)
    key_one, key_two = jax.random.split(key)
    full_shape = (NINT, NDIM, NDIM)
    sample_one = jax.random.normal(key_one, full_shape, jnp.float32)
    sample_two = jax.random.normal(key_two, full_shape, jnp.float32)
    real_part = (sample_one + jnp.swapaxes(sample_one, 1, 2)) * 0.7071
    imag_part = (sample_two - jnp.swapaxes(sample_two, 1, 2)) * 0.7071
    return jnp.stack([real_part, imag_part], axis=1).astype(jnp.bfloat16)


def block_scale(key, dims, cuts, smallest, largest):
    level = 1.0
    for position, shards_of in cuts:
        heights = jax.random.uniform(jax.random.fold_in(jax.random.fold_in(key, 6), position), (shards_of,), jnp.float32, smallest / len(cuts), largest / len(cuts))
        level = level * jnp.repeat(jnp.exp(heights), dims[position] // shards_of).reshape((-1,) + (1,) * (len(dims) - 1 - position))
    return level


def normal_values(stream_key, shape, deviation, bound, cuts=(), dtype=jnp.bfloat16):
    array = jax.random.normal(stream_key, shape, jnp.float32) * deviation
    if len(cuts) > 0:
        array = block_scale(stream_key, shape, cuts, -0.22, 0.18) * array
    return jnp.clip(array, min=-bound, max=bound).astype(dtype)


def setup_inputs(seed: int = 0, part: int = 0) -> dict:
    keys = jax.random.split(jax.random.key(seed), 7)
    part_splits = jax.random.split(jax.random.fold_in(keys[6], part), 7)
    terminal = draw_terminal(jax.random.fold_in(jax.random.fold_in(keys[6], part), 71), part)
    controls = normal_values(part_splits[1], (NINT, CF), 1.0, 3.0, ((0, 4),), jnp.float32)
    ham_blocks = normal_values(keys[2], (2, NBLK, KH, BS, BS), (2 * KH * BS) ** -0.5, 0.5)
    ham_cols = jax.vmap(lambda own: jax.random.permutation(own, NBLK))(jax.random.split(keys[3], KH)).reshape((KH, NBLK)).astype(jnp.int32)
    jump_blocks = normal_values(keys[4], (NBLK, KJ, BS, BS), (KJ * BS) ** -0.5, 0.75)
    jump_cols = jax.vmap(lambda own: jax.random.permutation(own, NBLK))(jax.random.split(keys[5], KJ)).reshape((KJ, NBLK)).astype(jnp.int32)
    return dict(terminal=terminal, controls=controls, ham_blocks=ham_blocks, ham_cols=ham_cols, jump_blocks=jump_blocks, jump_cols=jump_cols)


time_step = 0.2


def apply_left(values, pattern, slab):
    count = values.shape[0]
    size = values.shape[2]
    columns = slab.shape[1]
    grid = slab.astype(jnp.float32).reshape(count, size, columns)
    picked = grid[pattern]
    product = jnp.einsum("bkij,kbjn->bin", values.astype(jnp.float32), picked, precision=lax.Precision.HIGHEST)
    return product.reshape(count * size, columns)


def apply_right(values, inverse, slab):
    count = values.shape[0]
    size = values.shape[2]
    columns = slab.shape[1]
    grid = slab.astype(jnp.float32).reshape(count, size, columns)
    turned = jnp.stack([values[:, layer][inverse[layer]] for layer in range(values.shape[1])], axis=0)
    picked = grid[inverse]
    product = jnp.einsum("kcji,kcjn->cin", turned.astype(jnp.float32), picked, precision=lax.Precision.HIGHEST)
    return product.reshape(count * size, columns)


def adjoint_step(real_part, imag_part, control, drift, steer, ham_cols, ham_inv, jump, jump_cols, jump_inv):
    width = real_part.shape[1]
    coeffs = (drift + control * steer).astype(jnp.bfloat16)
    stacked = jnp.concatenate([real_part.astype(jnp.bfloat16), imag_part.astype(jnp.bfloat16)], axis=1)
    ham = apply_left(coeffs, ham_cols, stacked) + apply_right(coeffs, ham_inv, stacked)
    pushed = apply_left(jump, jump_cols, stacked).astype(jnp.bfloat16)
    pulled_all = apply_right(jump, jump_inv, jnp.concatenate([pushed, stacked], axis=1))
    loss = pulled_all[:, :2 * width]
    pulled = pulled_all[:, 2 * width:].astype(jnp.bfloat16)
    sym_part = -ham[:, width:] - 0.5 * loss[:, :width]
    skew_part = ham[:, :width] - 0.5 * loss[:, width:]
    back = apply_right(jump, jump_inv, jnp.concatenate([pulled[:, :width].T, pulled[:, width:].T], axis=1))
    sym_round = lax.optimization_barrier(sym_part.astype(jnp.bfloat16))
    skew_round = lax.optimization_barrier(skew_part.astype(jnp.bfloat16))
    new_real = real_part + time_step * (sym_part + sym_round.T.astype(jnp.float32) + back[:, :width])
    new_imag = imag_part + time_step * (skew_part - skew_round.T.astype(jnp.float32) - back[:, width:])
    return new_real, new_imag


def reference(terminal, controls, ham_blocks, ham_cols, jump_blocks, jump_cols):
    drift = ham_blocks[0].astype(jnp.float32)
    steer = ham_blocks[1].astype(jnp.float32)
    ham_inv = jnp.argsort(ham_cols, axis=1).astype(jnp.int32)
    jump_inv = jnp.argsort(jump_cols, axis=1).astype(jnp.int32)

    def sweep(pair):
        state, control_row = pair
        real_part = state[0].astype(jnp.float32)
        imag_part = state[1].astype(jnp.float32)
        real_part, imag_part = adjoint_step(real_part, imag_part, control_row[CF - 1], drift, steer, ham_cols, ham_inv, jump_blocks, jump_cols, jump_inv)
        inner = jnp.stack([real_part, imag_part], axis=0).astype(jnp.bfloat16)
        real_part, imag_part = adjoint_step(real_part, imag_part, control_row[0], drift, steer, ham_cols, ham_inv, jump_blocks, jump_cols, jump_inv)
        start = jnp.stack([real_part, imag_part], axis=0).astype(jnp.bfloat16)
        return inner, start

    new_fpoint, cstart = lax.map(sweep, (terminal, controls))
    new_cpoint = jnp.concatenate([cstart[1:], terminal[NINT - 1:]], axis=0)
    return new_cpoint, new_fpoint
```

```python
import functools

import jax
import jax.numpy as jnp
from jax import lax
from jax.experimental import pallas as pl
from jax.experimental.pallas import tpu as pltpu
from jax.sharding import PartitionSpec as P

time_step = 0.2
F32 = jnp.float32
BF16 = jnp.bfloat16


def shifted_down(block, axis):
    route = [(i, i - 1) for i in range(1, lax.axis_size(axis))]
    return lax.ppermute(block, axis, route)


def operator_tables(ham_blocks, ham_cols, jump_blocks, jump_cols, amplitudes):
    count = ham_cols.shape[1]
    size = ham_blocks.shape[-1]
    layers_h, layers_j = ham_cols.shape[0], jump_cols.shape[0]
    places = jnp.arange(count, dtype=jnp.int32)
    hit_h = ham_cols[:, None, :] == places[None, :, None]
    hit_j = jump_cols[:, None, :] == places[None, :, None]
    inv_h = jnp.sum(jnp.where(hit_h, places, 0), axis=2)
    inv_j = jnp.sum(jnp.where(hit_j, places, 0), axis=2)
    pick_h = hit_h.astype(BF16)
    pick_j = hit_j.astype(BF16)

    turned = [
        jnp.einsum("cb,bij->cji", pick_j[k], jump_blocks[:, k], preferred_element_type=F32).astype(BF16)
        for k in range(layers_j)
    ]
    jump_row = jnp.concatenate(turned, axis=2)
    rows_k, blocks_k = [places], [None]
    for k in range(layers_j):
        for other in range(layers_j):
            met = jnp.einsum("cb,bij->cij", pick_j[k], jump_blocks[:, other], preferred_element_type=F32).astype(BF16)
            block = -0.5 * jnp.einsum("cij,cjl->cil", turned[k], met, preferred_element_type=F32)
            if other == k:
                blocks_k[0] = block if blocks_k[0] is None else blocks_k[0] + block
            else:
                blocks_k.append(block)
                rows_k.append(jnp.sum(jnp.where(hit_j[k], jump_cols[other], 0), axis=1))
    decay = jnp.concatenate(blocks_k, axis=2).astype(BF16)

    drift = ham_blocks[0].astype(F32)
    steer = ham_blocks[1].astype(F32)
    plus, minus = [], []
    for amplitude in amplitudes:
        coeffs = (drift + amplitude * steer).astype(BF16)
        parts = [coeffs[:, k] for k in range(layers_h)]
        parts += [
            jnp.einsum("cb,bij->cji", pick_h[k], coeffs[:, k], preferred_element_type=F32).astype(BF16)
            for k in range(layers_h)
        ]
        ham = jnp.concatenate(parts, axis=2)
        plus.append(jnp.concatenate([ham, decay], axis=2))
        minus.append(jnp.concatenate([-ham, decay], axis=2))
    rows = jnp.concatenate([ham_cols, inv_h, jnp.stack(rows_k), inv_j], axis=0).astype(jnp.int32) * size
    return rows, jump_row, plus, minus


class Step:
    def __init__(self, rows, counts, size, plus, minus, jump):
        self.rows, self.counts, self.size = rows, counts, size
        self.plus, self.minus, self.jump = plus, minus, jump

    def take(self, ref, kind, c, cols):
        first = sum(self.counts[:kind])
        return [
            ref[pl.ds(pl.multiple_of(self.rows[first + k, c], self.size), self.size), cols]
            for k in range(self.counts[kind])
        ]

    def ham(self, table, c, ham_ref, decay_ref, cols):
        met = jnp.concatenate(self.take(ham_ref, 0, c, cols) + self.take(decay_ref, 1, c, cols), axis=0)
        return jnp.dot(table[c], met, preferred_element_type=F32)

    def pull(self, c, ref, cols):
        met = jnp.concatenate(self.take(ref, 2, c, cols), axis=0)
        return jnp.dot(self.jump[c], met, preferred_element_type=F32)


def turned_tile(tile):
    n = tile.shape[1]
    eye = (lax.broadcasted_iota(jnp.int32, (n, n), 0) == lax.broadcasted_iota(jnp.int32, (n, n), 1)).astype(BF16)
    return lax.dot_general(eye, tile, (((1,), (1,)), ((), ())), preferred_element_type=F32).astype(BF16)


def turn_whole(source, target, tile):
    n = source.shape[0] // tile

    @pl.loop(0, n)
    def _(i):
        near = pl.ds(pl.multiple_of(i * tile, tile), tile)
        for j in range(n):
            far = pl.ds(j * tile, tile)
            target[far, near] = turned_tile(source[near, far])


def turn_whole_in_place(ref, tile):
    n = ref.shape[0] // tile
    for i in range(n):
        near = pl.ds(i * tile, tile)
        ref[near, near] = turned_tile(ref[near, near])

        @pl.loop(i + 1, n)
        def _(j):
            far = pl.ds(pl.multiple_of(j * tile, tile), tile)
            upper = turned_tile(ref[near, far])
            lower = turned_tile(ref[far, near])
            ref[far, near] = upper
            ref[near, far] = lower


def whole_step(step, c_ref, d_ref, r_ref, x_ref, c_new, tile):
    n = c_ref.shape[0]
    count = n // step.size

    @pl.loop(0, count)
    def _(c):
        own = pl.ds(pl.multiple_of(c * step.size, step.size), step.size)
        for s in range(n // tile):
            cols = pl.ds(s * tile, tile)
            r_ref[own, cols] = step.ham(step.minus, c, c_ref, d_ref, cols).astype(BF16)
            x_ref[own, cols] = step.pull(c, d_ref, cols).astype(BF16)

    turn_whole_in_place(r_ref, tile)
    turn_whole_in_place(x_ref, tile)

    @pl.loop(0, count)
    def _(c):
        own = pl.ds(pl.multiple_of(c * step.size, step.size), step.size)
        for s in range(n // tile):
            cols = pl.ds(s * tile, tile)
            change = step.ham(step.plus, c, d_ref, c_ref, cols) + step.pull(c, x_ref, cols)
            change = change + r_ref[own, cols].astype(F32)
            c_new[own, cols] = (c_ref[own, cols].astype(F32) + time_step * change).astype(BF16)

    turn_whole(c_new, r_ref, tile)


def own_step(step, start, width, c_ref, d_ref, flat, turned, tile, base, out):
    n = c_ref.shape[0]
    part = min(tile, width)

    @pl.loop(0, width // step.size)
    def _(t):
        c = start // step.size + t
        for s in range(n // tile):
            cols = pl.ds(s * tile, tile)
            products = (
                step.ham(step.minus, c, c_ref, d_ref, cols),
                step.ham(step.plus, c, d_ref, c_ref, cols),
                step.pull(c, d_ref, cols),
                step.pull(c, c_ref, cols),
            )
            for k, product in enumerate(products):
                flat[pl.ds(pl.multiple_of(k * width + t * step.size, step.size), step.size), cols] = product.astype(BF16)

    @pl.loop(0, n // part)
    def _(i):
        near = pl.ds(pl.multiple_of(i * part, part), part)
        for j in range(4 * width // part):
            far = pl.ds(j * part, part)
            turned[near, far] = turned_tile(flat[far, near])

    @pl.loop(0, n // step.size)
    def _(c):
        own = pl.ds(pl.multiple_of(c * step.size, step.size), step.size)
        for s in range(width // part):
            cols = pl.ds(pl.multiple_of(start + s * part, part), part)
            of = [pl.ds(k * width + s * part, part) for k in range(4)]
            first = step.ham(step.plus, c, d_ref, c_ref, cols) + step.pull(c, turned, of[2])
            second = step.ham(step.minus, c, c_ref, d_ref, cols) + step.pull(c, turned, of[3])
            first = first + turned[own, of[0]].astype(F32)
            second = second + turned[own, of[1]].astype(F32)
            real, imag = base(own, cols, pl.ds(s * part, part))
            out[0, 0, own, pl.ds(s * part, part)] = (real + 0.5 * time_step * (first + second)).astype(BF16)
            out[0, 1, own, pl.ds(s * part, part)] = (imag + 0.5 * time_step * (first - second)).astype(BF16)


def inner_kernel(counts, tile, rows, place, c_hbm, terminal, plus, minus, jump, out, c_ref, d_ref, flat, turned, sem):
    load = pltpu.make_async_copy(c_hbm, c_ref, sem)
    load.start()
    load.wait()
    turn_whole(c_ref, d_ref, tile)
    step = Step(rows, counts, plus.shape[1], plus, minus, jump)

    def base(own, _, cols):
        return terminal[0, 0, own, cols].astype(F32), terminal[0, 1, own, cols].astype(F32)

    own_step(step, place[0], out.shape[3], c_ref, d_ref, flat, turned, tile, base, out)


def start_kernel(
    counts, tile, rows, place, c_hbm, terminal, plus_one, minus_one, plus_two, minus_two, jump, out,
    c_ref, d_ref, r_ref, x_ref, c_new, sem,
):
    @pl.when(place[1] == 1)
    def _():
        keep = pltpu.make_async_copy(terminal, out, sem)
        keep.start()
        keep.wait()

    @pl.when(place[1] == 0)
    def _():
        load = pltpu.make_async_copy(c_hbm, c_ref, sem)
        load.start()
        load.wait()
        turn_whole(c_ref, d_ref, tile)
        size = plus_one.shape[1]
        whole_step(Step(rows, counts, size, plus_one, minus_one, jump), c_ref, d_ref, r_ref, x_ref, c_new, tile)

        def base(own, cols, _):
            first, second = c_new[own, cols].astype(F32), r_ref[own, cols].astype(F32)
            return 0.5 * (first + second), 0.5 * (first - second)

        step = Step(rows, counts, size, plus_two, minus_two, jump)
        own_step(step, place[0], out.shape[3], c_new, r_ref, x_ref, c_ref, tile, base, out)


def on_device(terminal, controls, ham_blocks, ham_cols, jump_blocks, jump_cols):
    n, width = terminal.shape[2], terminal.shape[3]
    tile = 256
    mixed = (terminal[0, 0].astype(F32) + terminal[0, 1].astype(F32)).astype(BF16)
    mixed_next = shifted_down(mixed, "tm")
    controls_next = shifted_down(controls, "tm")
    whole = lax.all_gather(mixed, "row", axis=1, tiled=True)
    whole_next = lax.all_gather(mixed_next, "row", axis=1, tiled=True)

    rows, jump_row, plus, minus = operator_tables(
        ham_blocks, ham_cols, jump_blocks, jump_cols, (controls[0, 1], controls_next[0, 1], controls_next[0, 0])
    )
    counts = (2 * ham_cols.shape[0], rows.shape[0] - 2 * ham_cols.shape[0] - jump_cols.shape[0], jump_cols.shape[0])
    is_last = lax.axis_index("tm") == lax.axis_size("tm") - 1
    place = jnp.stack([lax.axis_index("row") * width, is_last.astype(jnp.int32)]).astype(jnp.int32)

    smem = pl.BlockSpec(memory_space=pltpu.SMEM)
    vmem = pl.BlockSpec(memory_space=pltpu.VMEM)
    anywhere = pl.BlockSpec(memory_space=pl.ANY)
    square = pltpu.VMEM((n, n), BF16)
    params = pltpu.CompilerParams(vmem_limit_bytes=60 * 2**20)
    out_shape = jax.ShapeDtypeStruct(terminal.shape, BF16)
    new_fpoint = pl.pallas_call(
        functools.partial(inner_kernel, counts, tile),
        out_shape=out_shape,
        in_specs=[smem, smem, anywhere, vmem, vmem, vmem, vmem],
        out_specs=vmem,
        scratch_shapes=[square, square, pltpu.VMEM((4 * width, n), BF16), pltpu.VMEM((n, 4 * width), BF16), pltpu.SemaphoreType.DMA],
        compiler_params=params,
        cost_estimate=pl.CostEstimate(flops=2 * 10**10, bytes_accessed=16 * 2**20, transcendentals=0),
        name="inner_point",
    )(rows, place, whole, terminal, plus[0], minus[0], jump_row)
    new_cpoint = pl.pallas_call(
        functools.partial(start_kernel, counts, tile),
        out_shape=out_shape,
        in_specs=[smem, smem, anywhere, anywhere, vmem, vmem, vmem, vmem, vmem],
        out_specs=vmem,
        scratch_shapes=[square] * 5 + [pltpu.SemaphoreType.DMA],
        compiler_params=params,
        cost_estimate=pl.CostEstimate(flops=6 * 10**10, bytes_accessed=16 * 2**20, transcendentals=0),
        name="left_end",
    )(rows, place, whole_next, terminal, plus[1], minus[1], plus[2], minus[2], jump_row)
    return (new_cpoint, new_fpoint)


def solution(mesh):
    in_specs = (P(("grp", "tm"), None, None, "row"), P(("grp", "tm"), None), P(), P(), P(), P())
    out_specs = (P(("grp", "tm"), None, None, "row"), P(("grp", "tm"), None, None, "row"))
    return jax.shard_map(
        on_device, mesh=mesh, in_specs=in_specs, out_specs=out_specs, check_vma=False
    )
```

```python
import functools

import jax
import jax.numpy as jnp
from jax import lax
from jax.experimental import pallas as pl
from jax.experimental.pallas import tpu as pltpu
from jax.sharding import PartitionSpec as P

time_step = 0.2
F32 = jnp.float32
BF16 = jnp.bfloat16


def shifted_down(block, axis):
    route = [(i, i - 1) for i in range(1, lax.axis_size(axis))]
    return lax.ppermute(block, axis, route)


def table_kernel(ham_cols, jump_cols, amplitudes, ham, jump, rows, jump_row, *tables):
    layers_h, count = ham_cols.shape
    layers_j = jump_cols.shape[0]
    size = ham.shape[-1]
    crossed = [(k, other) for k in range(layers_j) for other in range(layers_j) if k != other]
    first_k = 2 * layers_h
    first_j = first_k + 1 + len(crossed)

    @pl.loop(0, count)
    def _(b):
        for k in range(layers_h):
            rows[k, b] = ham_cols[k, b] * size
            rows[layers_h + k, ham_cols[k, b]] = b * size
        for k in range(layers_j):
            rows[first_j + k, jump_cols[k, b]] = b * size

    @pl.loop(0, count, unroll=2)
    def _(c):
        came_h = [rows[layers_h + k, c] // size for k in range(layers_h)]
        came_j = [rows[first_j + k, c] // size for k in range(layers_j)]
        rows[first_k, c] = c * size
        for at, (k, other) in enumerate(crossed):
            rows[first_k + 1 + at, c] = jump_cols[other, came_j[k]] * size

        def ham_row(term):
            parts = [ham[term, c, k].astype(F32) for k in range(layers_h)]
            parts += [ham[term, came_h[k], k].astype(F32).T for k in range(layers_h)]
            return jnp.concatenate(parts, axis=1)

        turned = [jump[came_j[k], k].astype(F32).T.astype(BF16) for k in range(layers_j)]
        jump_row[c] = jnp.concatenate(turned, axis=1)
        square = sum(
            jnp.dot(turned[k], jump[came_j[k], k], preferred_element_type=F32) for k in range(layers_j)
        )
        blocks = [square] + [
            jnp.dot(turned[k], jump[came_j[k], other], preferred_element_type=F32) for k, other in crossed
        ]
        decay = -0.5 * jnp.concatenate(blocks, axis=1)
        drift, steer = ham_row(0), ham_row(1)
        for at in range(len(tables) // 2):
            coeffs = drift + amplitudes[at] * steer
            tables[2 * at][c] = jnp.concatenate([coeffs, decay], axis=1).astype(BF16)
            tables[2 * at + 1][c] = jnp.concatenate([-coeffs, decay], axis=1).astype(BF16)


def operator_tables(ham_blocks, ham_cols, jump_blocks, jump_cols, amplitudes):
    layers_h, count = ham_cols.shape
    layers_j = jump_cols.shape[0]
    size = ham_blocks.shape[-1]
    layers_k = 1 + layers_j * (layers_j - 1)
    smem = pl.BlockSpec(memory_space=pltpu.SMEM)
    vmem = pl.BlockSpec(memory_space=pltpu.VMEM)
    table = jax.ShapeDtypeStruct((count, size, (2 * layers_h + layers_k) * size), BF16)
    number = amplitudes.shape[0]
    rows, jump_row, *tables = pl.pallas_call(
        table_kernel,
        out_shape=[
            jax.ShapeDtypeStruct((2 * layers_h + layers_k + layers_j, count), jnp.int32),
            jax.ShapeDtypeStruct((count, size, layers_j * size), BF16),
        ] + [table] * (2 * number),
        in_specs=[smem, smem, smem, vmem, vmem],
        out_specs=[smem, vmem] + [vmem] * (2 * number),
        compiler_params=pltpu.CompilerParams(vmem_limit_bytes=60 * 2**20),
        cost_estimate=pl.CostEstimate(flops=10**9, bytes_accessed=10 * 2**20, transcendentals=0),
        name="operator_tables",
    )(ham_cols, jump_cols, amplitudes, ham_blocks, jump_blocks)
    return (2 * layers_h, layers_k, layers_j), rows, jump_row, tables[0::2], tables[1::2]


class Step:
    def __init__(self, rows, counts, size, plus, minus, jump):
        self.rows, self.counts, self.size = rows, counts, size
        self.plus, self.minus, self.jump = plus, minus, jump

    def take(self, ref, kind, c, cols):
        first = sum(self.counts[:kind])
        return [
            ref[pl.ds(pl.multiple_of(self.rows[first + k, c], self.size), self.size), cols]
            for k in range(self.counts[kind])
        ]

    def ham(self, table, c, ham_ref, decay_ref, cols):
        met = jnp.concatenate(self.take(ham_ref, 0, c, cols) + self.take(decay_ref, 1, c, cols), axis=0)
        return jnp.dot(table[c], met, preferred_element_type=F32)

    def pull(self, c, ref, cols):
        met = jnp.concatenate(self.take(ref, 2, c, cols), axis=0)
        return jnp.dot(self.jump[c], met, preferred_element_type=F32)


def turned_tile(tile):
    return tile.T


def turn_whole(source, target, tile):
    n = source.shape[0] // tile

    @pl.loop(0, n)
    def _(i):
        near = pl.ds(pl.multiple_of(i * tile, tile), tile)
        for j in range(n):
            far = pl.ds(j * tile, tile)
            target[far, near] = turned_tile(source[near, far])


def turn_whole_in_place(ref, tile):
    n = ref.shape[0] // tile
    for i in range(n):
        near = pl.ds(i * tile, tile)
        ref[near, near] = turned_tile(ref[near, near])

        @pl.loop(i + 1, n)
        def _(j):
            far = pl.ds(pl.multiple_of(j * tile, tile), tile)
            upper = turned_tile(ref[near, far])
            lower = turned_tile(ref[far, near])
            ref[far, near] = upper
            ref[near, far] = lower


def whole_step(step, c_ref, d_ref, r_ref, x_ref, c_new, tile):
    n = c_ref.shape[0]
    count = n // step.size

    @pl.loop(0, count)
    def _(c):
        own = pl.ds(pl.multiple_of(c * step.size, step.size), step.size)
        for s in range(n // tile):
            cols = pl.ds(s * tile, tile)
            r_ref[own, cols] = step.ham(step.minus, c, c_ref, d_ref, cols).astype(BF16)
            x_ref[own, cols] = step.pull(c, d_ref, cols).astype(BF16)

    turn_whole_in_place(r_ref, tile)
    turn_whole_in_place(x_ref, tile)

    @pl.loop(0, count)
    def _(c):
        own = pl.ds(pl.multiple_of(c * step.size, step.size), step.size)
        for s in range(n // tile):
            cols = pl.ds(s * tile, tile)
            change = step.ham(step.plus, c, d_ref, c_ref, cols) + step.pull(c, x_ref, cols)
            change = change + r_ref[own, cols].astype(F32)
            c_new[own, cols] = (c_ref[own, cols].astype(F32) + time_step * change).astype(BF16)

    turn_whole(c_new, r_ref, tile)


def own_step(step, start, width, c_ref, d_ref, flat, turned, tile, base, out):
    n = c_ref.shape[0]
    part = min(tile, width)

    @pl.loop(0, width // step.size)
    def _(t):
        c = start // step.size + t
        for s in range(n // tile):
            cols = pl.ds(s * tile, tile)
            products = (
                step.ham(step.minus, c, c_ref, d_ref, cols),
                step.ham(step.plus, c, d_ref, c_ref, cols),
                step.pull(c, d_ref, cols),
                step.pull(c, c_ref, cols),
            )
            for k, product in enumerate(products):
                flat[pl.ds(pl.multiple_of(k * width + t * step.size, step.size), step.size), cols] = product.astype(BF16)

    @pl.loop(0, n // part)
    def _(i):
        near = pl.ds(pl.multiple_of(i * part, part), part)
        for j in range(4 * width // part):
            far = pl.ds(j * part, part)
            turned[near, far] = turned_tile(flat[far, near])

    @pl.loop(0, n // step.size)
    def _(c):
        own = pl.ds(pl.multiple_of(c * step.size, step.size), step.size)
        for s in range(width // part):
            cols = pl.ds(pl.multiple_of(start + s * part, part), part)
            of = [pl.ds(k * width + s * part, part) for k in range(4)]
            first = step.ham(step.plus, c, d_ref, c_ref, cols) + step.pull(c, turned, of[2])
            second = step.ham(step.minus, c, c_ref, d_ref, cols) + step.pull(c, turned, of[3])
            first = first + turned[own, of[0]].astype(F32)
            second = second + turned[own, of[1]].astype(F32)
            real, imag = base(own, cols, pl.ds(s * part, part))
            out[0, 0, own, pl.ds(s * part, part)] = (real + 0.5 * time_step * (first + second)).astype(BF16)
            out[0, 1, own, pl.ds(s * part, part)] = (imag + 0.5 * time_step * (first - second)).astype(BF16)


def inner_kernel(counts, tile, rows, place, c_hbm, terminal, plus, minus, jump, out, c_ref, d_ref, flat, turned, sem):
    load = pltpu.make_async_copy(c_hbm, c_ref, sem)
    load.start()
    load.wait()
    turn_whole(c_ref, d_ref, tile)
    step = Step(rows, counts, plus.shape[1], plus, minus, jump)

    def base(own, _, cols):
        return terminal[0, 0, own, cols].astype(F32), terminal[0, 1, own, cols].astype(F32)

    own_step(step, place[0], out.shape[3], c_ref, d_ref, flat, turned, tile, base, out)


def start_kernel(
    counts, tile, rows, place, c_hbm, terminal, plus_one, minus_one, plus_two, minus_two, jump, out,
    c_ref, d_ref, r_ref, x_ref, c_new, sem,
):
    @pl.when(place[1] == 1)
    def _():
        keep = pltpu.make_async_copy(terminal, out, sem)
        keep.start()
        keep.wait()

    @pl.when(place[1] == 0)
    def _():
        load = pltpu.make_async_copy(c_hbm, c_ref, sem)
        load.start()
        load.wait()
        turn_whole(c_ref, d_ref, tile)
        size = plus_one.shape[1]
        whole_step(Step(rows, counts, size, plus_one, minus_one, jump), c_ref, d_ref, r_ref, x_ref, c_new, tile)

        def base(own, cols, _):
            first, second = c_new[own, cols].astype(F32), r_ref[own, cols].astype(F32)
            return 0.5 * (first + second), 0.5 * (first - second)

        step = Step(rows, counts, size, plus_two, minus_two, jump)
        own_step(step, place[0], out.shape[3], c_new, r_ref, x_ref, c_ref, tile, base, out)


def on_device(terminal, controls, ham_blocks, ham_cols, jump_blocks, jump_cols):
    n, width = terminal.shape[2], terminal.shape[3]
    tile = 256
    mixed = (terminal[0, 0].astype(F32) + terminal[0, 1].astype(F32)).astype(BF16)
    mixed_next = shifted_down(mixed, "tm")
    controls_next = shifted_down(controls, "tm")
    whole = lax.all_gather(mixed, "row", axis=1, tiled=True)
    whole_next = lax.all_gather(mixed_next, "row", axis=1, tiled=True)

    amplitudes = jnp.stack([controls[0, 1], controls_next[0, 1], controls_next[0, 0]])
    counts, rows, jump_row, plus, minus = operator_tables(ham_blocks, ham_cols, jump_blocks, jump_cols, amplitudes)
    is_last = lax.axis_index("tm") == lax.axis_size("tm") - 1
    place = jnp.stack([lax.axis_index("row") * width, is_last.astype(jnp.int32)]).astype(jnp.int32)

    smem = pl.BlockSpec(memory_space=pltpu.SMEM)
    vmem = pl.BlockSpec(memory_space=pltpu.VMEM)
    anywhere = pl.BlockSpec(memory_space=pl.ANY)
    square = pltpu.VMEM((n, n), BF16)
    params = pltpu.CompilerParams(vmem_limit_bytes=60 * 2**20)
    out_shape = jax.ShapeDtypeStruct(terminal.shape, BF16)
    new_fpoint = pl.pallas_call(
        functools.partial(inner_kernel, counts, tile),
        out_shape=out_shape,
        in_specs=[smem, smem, anywhere, vmem, vmem, vmem, vmem],
        out_specs=vmem,
        scratch_shapes=[square, square, pltpu.VMEM((4 * width, n), BF16), pltpu.VMEM((n, 4 * width), BF16), pltpu.SemaphoreType.DMA],
        compiler_params=params,
        cost_estimate=pl.CostEstimate(flops=2 * 10**10, bytes_accessed=16 * 2**20, transcendentals=0),
        name="inner_point",
    )(rows, place, whole, terminal, plus[0], minus[0], jump_row)
    new_cpoint = pl.pallas_call(
        functools.partial(start_kernel, counts, tile),
        out_shape=out_shape,
        in_specs=[smem, smem, anywhere, anywhere, vmem, vmem, vmem, vmem, vmem],
        out_specs=vmem,
        scratch_shapes=[square] * 5 + [pltpu.SemaphoreType.DMA],
        compiler_params=params,
        cost_estimate=pl.CostEstimate(flops=6 * 10**10, bytes_accessed=16 * 2**20, transcendentals=0),
        name="left_end",
    )(rows, place, whole_next, terminal, plus[1], minus[1], plus[2], minus[2], jump_row)
    return (new_cpoint, new_fpoint)


def solution(mesh):
    in_specs = (P(("grp", "tm"), None, None, "row"), P(("grp", "tm"), None), P(), P(), P(), P())
    out_specs = (P(("grp", "tm"), None, None, "row"), P(("grp", "tm"), None, None, "row"))
    return jax.shard_map(
        on_device, mesh=mesh, in_specs=in_specs, out_specs=out_specs, check_vma=False
    )
```

```python
import functools

import jax
import jax.numpy as jnp
from jax import lax
from jax.experimental import pallas as pl
from jax.experimental.pallas import tpu as pltpu
from jax.sharding import PartitionSpec as P

time_step = 0.2
F32 = jnp.float32
BF16 = jnp.bfloat16


def shifted_down(block, axis):
    route = [(i, i - 1) for i in range(1, lax.axis_size(axis))]
    return lax.ppermute(block, axis, route)


def table_kernel(ham_cols, jump_cols, amplitudes, ham, jump, rows, jump_row, *tables):
    layers_h, count = ham_cols.shape
    layers_j = jump_cols.shape[0]
    size = ham.shape[-1]
    crossed = [(k, other) for k in range(layers_j) for other in range(layers_j) if k != other]
    first_k = 2 * layers_h
    first_j = first_k + 1 + len(crossed)

    @pl.loop(0, count)
    def _(b):
        for k in range(layers_h):
            rows[k, b] = ham_cols[k, b] * size
            rows[layers_h + k, ham_cols[k, b]] = b * size
        for k in range(layers_j):
            rows[first_j + k, jump_cols[k, b]] = b * size

    @pl.loop(0, count, unroll=2)
    def _(c):
        came_h = [rows[layers_h + k, c] // size for k in range(layers_h)]
        came_j = [rows[first_j + k, c] // size for k in range(layers_j)]
        rows[first_k, c] = c * size
        for at, (k, other) in enumerate(crossed):
            rows[first_k + 1 + at, c] = jump_cols[other, came_j[k]] * size

        def ham_row(term):
            parts = [ham[term, c, k].astype(F32) for k in range(layers_h)]
            parts += [ham[term, came_h[k], k].astype(F32).T for k in range(layers_h)]
            return jnp.concatenate(parts, axis=1)

        turned = [jump[came_j[k], k].astype(F32).T.astype(BF16) for k in range(layers_j)]
        jump_row[c] = jnp.concatenate(turned, axis=1)
        square = sum(
            jnp.dot(turned[k], jump[came_j[k], k], preferred_element_type=F32) for k in range(layers_j)
        )
        blocks = [square] + [
            jnp.dot(turned[k], jump[came_j[k], other], preferred_element_type=F32) for k, other in crossed
        ]
        decay = -0.5 * jnp.concatenate(blocks, axis=1)
        drift, steer = ham_row(0), ham_row(1)
        for at in range(len(tables) // 2):
            coeffs = drift + amplitudes[at] * steer
            tables[2 * at][c] = jnp.concatenate([coeffs, decay], axis=1).astype(BF16)
            tables[2 * at + 1][c] = jnp.concatenate([-coeffs, decay], axis=1).astype(BF16)


def operator_tables(ham_blocks, ham_cols, jump_blocks, jump_cols, amplitudes):
    layers_h, count = ham_cols.shape
    layers_j = jump_cols.shape[0]
    size = ham_blocks.shape[-1]
    layers_k = 1 + layers_j * (layers_j - 1)
    smem = pl.BlockSpec(memory_space=pltpu.SMEM)
    vmem = pl.BlockSpec(memory_space=pltpu.VMEM)
    table = jax.ShapeDtypeStruct((count, size, (2 * layers_h + layers_k) * size), BF16)
    number = amplitudes.shape[0]
    rows, jump_row, *tables = pl.pallas_call(
        table_kernel,
        out_shape=[
            jax.ShapeDtypeStruct((2 * layers_h + layers_k + layers_j, count), jnp.int32),
            jax.ShapeDtypeStruct((count, size, layers_j * size), BF16),
        ] + [table] * (2 * number),
        in_specs=[smem, smem, smem, vmem, vmem],
        out_specs=[smem, vmem] + [vmem] * (2 * number),
        compiler_params=pltpu.CompilerParams(vmem_limit_bytes=60 * 2**20),
        cost_estimate=pl.CostEstimate(flops=10**9, bytes_accessed=10 * 2**20, transcendentals=0),
        name="operator_tables",
    )(ham_cols, jump_cols, amplitudes, ham_blocks, jump_blocks)
    return (2 * layers_h, layers_k, layers_j), rows, jump_row, tables[0::2], tables[1::2]


class Step:
    def __init__(self, rows, counts, size, plus, minus, jump):
        self.rows, self.counts, self.size = rows, counts, size
        self.plus, self.minus, self.jump = plus, minus, jump

    def take(self, ref, kind, c, cols):
        first = sum(self.counts[:kind])
        return [
            ref[pl.ds(pl.multiple_of(self.rows[first + k, c], self.size), self.size), cols]
            for k in range(self.counts[kind])
        ]

    def ham(self, table, c, ham_ref, decay_ref, cols):
        met = jnp.concatenate(self.take(ham_ref, 0, c, cols) + self.take(decay_ref, 1, c, cols), axis=0)
        return jnp.dot(table[c], met, preferred_element_type=F32)

    def pull(self, c, ref, cols):
        met = jnp.concatenate(self.take(ref, 2, c, cols), axis=0)
        return jnp.dot(self.jump[c], met, preferred_element_type=F32)


def turned_tile(tile):
    return tile.T


def turn_whole(source, target, tile):
    n = source.shape[0] // tile

    @pl.loop(0, n)
    def _(i):
        near = pl.ds(pl.multiple_of(i * tile, tile), tile)
        for j in range(n):
            far = pl.ds(j * tile, tile)
            target[far, near] = turned_tile(source[near, far])


def assemble(place, near, near_pair, far, far_pair, c_ref, d_ref, stage, sems, tile):
    half, width = far.shape
    here, there = place[2], half - place[2]
    own, pair = place[3], width - place[3]
    chip_rows, other_rows = (pl.ds(pl.multiple_of(first, half), half) for first in (here, there))

    def cols(first):
        return pl.ds(pl.multiple_of(first, width), width)

    copies = [
        (near.at[0], c_ref.at[chip_rows, cols(here + own)]),
        (near_pair.at[0], c_ref.at[chip_rows, cols(here + pair)]),
        (far, c_ref.at[other_rows, cols(there + own)]),
        (far_pair, c_ref.at[other_rows, cols(there + pair)]),
    ]
    for k in range(2):
        copies.append((near.at[1 + k], stage.at[pl.ds(k * half, half), cols(own)]))
        copies.append((near_pair.at[1 + k], stage.at[pl.ds(k * half, half), cols(pair)]))
    copies = [pltpu.make_async_copy(a, b, sems.at[k]) for k, (a, b) in enumerate(copies)]
    for copy in copies:
        copy.start()
    for copy in copies:
        copy.wait()

    def part(first, k):
        return pl.ds(pl.multiple_of(first + k * tile, tile), tile)

    @pl.loop(0, half // tile)
    def _(i):
        for first in (0, half):
            for j in range(half // tile):
                d_ref[part(first, j), part(first, i)] = c_ref[part(first, i), part(first, j)].T
        for j in range(half // tile):
            real = stage[part(0, i), part(0, j)].astype(F32)
            imag = stage[part(half, i), part(0, j)].astype(F32)
            total, less = (real + imag).astype(BF16), (real - imag).astype(BF16)
            c_ref[part(there, i), part(here, j)] = total
            d_ref[part(there, i), part(here, j)] = less
            c_ref[part(here, j), part(there, i)] = less.T
            d_ref[part(here, j), part(there, i)] = total.T


def own_step(step, start, width, c_ref, d_ref, flat, turned, tile, base, out):
    n = c_ref.shape[0]
    part = min(tile, width)

    @pl.loop(0, width // step.size)
    def _(t):
        c = start // step.size + t
        for s in range(n // tile):
            cols = pl.ds(s * tile, tile)
            products = (
                step.ham(step.minus, c, c_ref, d_ref, cols),
                step.ham(step.plus, c, d_ref, c_ref, cols),
                step.pull(c, d_ref, cols),
                step.pull(c, c_ref, cols),
            )
            for k, product in enumerate(products):
                flat[pl.ds(pl.multiple_of(k * width + t * step.size, step.size), step.size), cols] = product.astype(BF16)

    @pl.loop(0, n // part)
    def _(i):
        near = pl.ds(pl.multiple_of(i * part, part), part)
        for j in range(4 * width // part):
            far = pl.ds(j * part, part)
            turned[near, far] = turned_tile(flat[far, near])

    @pl.loop(0, n // step.size)
    def _(c):
        own = pl.ds(pl.multiple_of(c * step.size, step.size), step.size)
        for s in range(width // part):
            cols = pl.ds(pl.multiple_of(start + s * part, part), part)
            of = [pl.ds(k * width + s * part, part) for k in range(4)]
            first = step.ham(step.plus, c, d_ref, c_ref, cols) + step.pull(c, turned, of[2])
            second = step.ham(step.minus, c, c_ref, d_ref, cols) + step.pull(c, turned, of[3])
            first = first + turned[own, of[0]].astype(F32)
            second = second + turned[own, of[1]].astype(F32)
            real, imag = base(own, cols, pl.ds(s * part, part))
            out[0, 0, own, pl.ds(s * part, part)] = (real + 0.5 * time_step * (first + second)).astype(BF16)
            out[0, 1, own, pl.ds(s * part, part)] = (imag + 0.5 * time_step * (first - second)).astype(BF16)


def fill(place, pieces, c_ref, d_ref, flat, sems, tile):
    if len(pieces) == 1:
        load = pltpu.make_async_copy(pieces[0], c_ref, sems.at[0])
        load.start()
        load.wait()
        turn_whole(c_ref, d_ref, tile)
    else:
        assemble(place, *pieces, c_ref, d_ref, flat, sems, tile)


def inner_kernel(counts, tile, rows, place, terminal, plus, minus, jump, *refs):
    *pieces, out, c_ref, d_ref, flat, turned, sems = refs
    fill(place, pieces, c_ref, d_ref, flat, sems, tile)
    step = Step(rows, counts, plus.shape[1], plus, minus, jump)

    def base(own, _, cols):
        return terminal[0, 0, own, cols].astype(F32), terminal[0, 1, own, cols].astype(F32)

    own_step(step, place[0], out.shape[3], c_ref, d_ref, flat, turned, tile, base, out)


def start_kernel(counts, tile, rows, place, terminal, plus, minus, jump, *refs):
    *pieces, out, c_ref, d_ref, flat, turned, sems = refs

    @pl.when(place[1] == 1)
    def _():
        keep = pltpu.make_async_copy(terminal, out, sems.at[0])
        keep.start()
        keep.wait()

    @pl.when(place[1] == 0)
    def _():
        fill(place, pieces, c_ref, d_ref, flat, sems, tile)
        step = Step(rows, counts, plus.shape[1], plus, minus, jump)

        def base(own, cols, _):
            first, second = c_ref[own, cols].astype(F32), d_ref[own, cols].astype(F32)
            return 0.5 * (first + second), 0.5 * (first - second)

        own_step(step, place[0], out.shape[3], c_ref, d_ref, flat, turned, tile, base, out)


def swapped(block, bit):
    return lax.ppermute(block, "row", [(i, i ^ bit) for i in range(lax.axis_size("row"))])


def on_device(terminal, controls, ham_blocks, ham_cols, jump_blocks, jump_cols):
    n, width = terminal.shape[2], terminal.shape[3]
    tile = 256
    two_chips = lax.axis_size("row") == 4
    row = lax.axis_index("row")
    here = row // 2 * 2 * width
    controls_next = shifted_down(controls, "tm")
    is_last = lax.axis_index("tm") == lax.axis_size("tm") - 1
    place = jnp.stack([row * width, is_last.astype(jnp.int32), here, row % 2 * width]).astype(jnp.int32)
    amplitudes = jnp.stack([controls[0, 1], controls_next[0, 0]])
    counts, rows, jump_row, plus, minus = operator_tables(ham_blocks, ham_cols, jump_blocks, jump_cols, amplitudes)

    def packed(state):
        mine = lax.dynamic_slice_in_dim(state[0], here, 2 * width, 1).astype(F32)
        rest = lax.dynamic_slice_in_dim(state[0], 2 * width - here, 2 * width, 1)
        return (mine[0] + mine[1]).astype(BF16)[None], rest

    def gathered(mixed, rest):
        near = jnp.concatenate([mixed, rest], axis=0)
        far = swapped(mixed[0], 2)
        return [near, swapped(near, 1), far, swapped(far, 1)]

    def whole(state):
        return (state[0, 0].astype(F32) + state[0, 1].astype(F32)).astype(BF16)

    smem = pl.BlockSpec(memory_space=pltpu.SMEM)
    vmem = pl.BlockSpec(memory_space=pltpu.VMEM)
    anywhere = pl.BlockSpec(memory_space=pl.ANY)

    def step_call(kernel, name, state_spec, k, pieces):
        return pl.pallas_call(
            functools.partial(kernel, counts, tile),
            out_shape=jax.ShapeDtypeStruct(terminal.shape, BF16),
            in_specs=[smem, smem, state_spec, vmem, vmem, vmem] + [anywhere] * len(pieces),
            out_specs=vmem,
            scratch_shapes=[
                pltpu.VMEM((n, n), BF16),
                pltpu.VMEM((n, n), BF16),
                pltpu.VMEM((4 * width, n), BF16),
                pltpu.VMEM((n, 4 * width), BF16),
                pltpu.SemaphoreType.DMA((8,)),
            ],
            compiler_params=pltpu.CompilerParams(vmem_limit_bytes=60 * 2**20),
            cost_estimate=pl.CostEstimate(flops=2 * 10**10, bytes_accessed=16 * 2**20, transcendentals=0),
            name=name,
        )(rows, place, terminal, plus[k], minus[k], jump_row, *pieces)

    if two_chips:
        pieces = gathered(*packed(terminal))
    else:
        pieces = [lax.all_gather(whole(terminal), "row", axis=1, tiled=True)]
    new_fpoint = step_call(inner_kernel, "inner_point", vmem, 0, pieces)
    if two_chips:
        mixed, rest = packed(new_fpoint)
        pieces = gathered(shifted_down(mixed, "tm"), shifted_down(rest, "tm"))
    else:
        pieces = [lax.all_gather(shifted_down(whole(new_fpoint), "tm"), "row", axis=1, tiled=True)]
    new_cpoint = step_call(start_kernel, "left_end", anywhere, 1, pieces)
    return (new_cpoint, new_fpoint)


def solution(mesh):
    in_specs = (P(("grp", "tm"), None, None, "row"), P(("grp", "tm"), None), P(), P(), P(), P())
    out_specs = (P(("grp", "tm"), None, None, "row"), P(("grp", "tm"), None, None, "row"))
    return jax.shard_map(
        on_device, mesh=mesh, in_specs=in_specs, out_specs=out_specs, check_vma=False
    )
```

```python
import functools

import jax
import jax.numpy as jnp
from jax import lax
from jax.experimental import pallas as pl
from jax.experimental.pallas import tpu as pltpu
from jax.sharding import PartitionSpec as P

time_step = 0.2
F32 = jnp.float32
BF16 = jnp.bfloat16


def shifted_down(block, axis):
    route = [(i, i - 1) for i in range(1, lax.axis_size(axis))]
    return lax.ppermute(block, axis, route)


def table_kernel(ham_cols, jump_cols, amplitudes, ham, jump, rows, jump_row, *tables):
    layers_h, count = ham_cols.shape
    layers_j = jump_cols.shape[0]
    size = ham.shape[-1]
    crossed = [(k, other) for k in range(layers_j) for other in range(layers_j) if k != other]
    first_k = 2 * layers_h
    first_j = first_k + 1 + len(crossed)

    @pl.loop(0, count)
    def _(b):
        for k in range(layers_h):
            rows[k, b] = ham_cols[k, b] * size
            rows[layers_h + k, ham_cols[k, b]] = b * size
        for k in range(layers_j):
            rows[first_j + k, jump_cols[k, b]] = b * size

    @pl.loop(0, count, unroll=2)
    def _(c):
        came_h = [rows[layers_h + k, c] // size for k in range(layers_h)]
        came_j = [rows[first_j + k, c] // size for k in range(layers_j)]
        rows[first_k, c] = c * size
        for at, (k, other) in enumerate(crossed):
            rows[first_k + 1 + at, c] = jump_cols[other, came_j[k]] * size

        def ham_row(term):
            parts = [ham[term, c, k].astype(F32) for k in range(layers_h)]
            parts += [ham[term, came_h[k], k].astype(F32).T for k in range(layers_h)]
            return jnp.concatenate(parts, axis=1)

        turned = [jump[came_j[k], k].astype(F32).T.astype(BF16) for k in range(layers_j)]
        jump_row[c] = jnp.concatenate(turned, axis=1)
        square = sum(
            jnp.dot(turned[k], jump[came_j[k], k], preferred_element_type=F32) for k in range(layers_j)
        )
        blocks = [square] + [
            jnp.dot(turned[k], jump[came_j[k], other], preferred_element_type=F32) for k, other in crossed
        ]
        decay = -0.5 * jnp.concatenate(blocks, axis=1)
        drift, steer = ham_row(0), ham_row(1)
        for at in range(len(tables) // 2):
            coeffs = drift + amplitudes[at] * steer
            tables[2 * at][c] = jnp.concatenate([coeffs, decay], axis=1).astype(BF16)
            tables[2 * at + 1][c] = jnp.concatenate([-coeffs, decay], axis=1).astype(BF16)


def operator_tables(ham_blocks, ham_cols, jump_blocks, jump_cols, amplitudes):
    layers_h, count = ham_cols.shape
    layers_j = jump_cols.shape[0]
    size = ham_blocks.shape[-1]
    layers_k = 1 + layers_j * (layers_j - 1)
    smem = pl.BlockSpec(memory_space=pltpu.SMEM)
    vmem = pl.BlockSpec(memory_space=pltpu.VMEM)
    table = jax.ShapeDtypeStruct((count, size, (2 * layers_h + layers_k) * size), BF16)
    number = amplitudes.shape[0]
    rows, jump_row, *tables = pl.pallas_call(
        table_kernel,
        out_shape=[
            jax.ShapeDtypeStruct((2 * layers_h + layers_k + layers_j, count), jnp.int32),
            jax.ShapeDtypeStruct((count, size, layers_j * size), BF16),
        ] + [table] * (2 * number),
        in_specs=[smem, smem, smem, vmem, vmem],
        out_specs=[smem, vmem] + [vmem] * (2 * number),
        compiler_params=pltpu.CompilerParams(vmem_limit_bytes=60 * 2**20),
        cost_estimate=pl.CostEstimate(flops=10**9, bytes_accessed=10 * 2**20, transcendentals=0),
        name="operator_tables",
    )(ham_cols, jump_cols, amplitudes, ham_blocks, jump_blocks)
    return (2 * layers_h, layers_k, layers_j), rows, jump_row, tables[0::2], tables[1::2]


class Step:
    def __init__(self, rows, counts, size, plus, minus, jump):
        self.rows, self.counts, self.size = rows, counts, size
        self.plus, self.minus, self.jump = plus, minus, jump

    def take(self, ref, kind, c, cols):
        first = sum(self.counts[:kind])
        return [
            ref[pl.ds(pl.multiple_of(self.rows[first + k, c], self.size), self.size), cols]
            for k in range(self.counts[kind])
        ]

    def ham(self, table, c, ham_ref, decay_ref, cols):
        met = jnp.concatenate(self.take(ham_ref, 0, c, cols) + self.take(decay_ref, 1, c, cols), axis=0)
        return jnp.dot(table[c], met, preferred_element_type=F32)

    def pull(self, c, ref, cols):
        met = jnp.concatenate(self.take(ref, 2, c, cols), axis=0)
        return jnp.dot(self.jump[c], met, preferred_element_type=F32)


def turned_tile(tile):
    return tile.T


def turn_whole(source, target, tile):
    n = source.shape[0] // tile

    @pl.loop(0, n)
    def _(i):
        near = pl.ds(pl.multiple_of(i * tile, tile), tile)
        for j in range(n):
            far = pl.ds(j * tile, tile)
            target[far, near] = turned_tile(source[near, far])


def load_all(copies, sems):
    copies = [pltpu.make_async_copy(source, target, sems.at[k]) for k, (source, target) in enumerate(copies)]
    for copy in copies:
        copy.start()
    for copy in copies:
        copy.wait()


def part_of(first, k, tile):
    return pl.ds(pl.multiple_of(first + k * tile, tile), tile)


def assemble_first(place, near, near_pair, far, far_pair, c_ref, d_ref, stage, sems, tile):
    half, width = far.shape
    here, there = place[2], half - place[2]
    own, pair = place[3], width - place[3]
    n = 2 * half
    other_rows = pl.ds(pl.multiple_of(there, half), half)

    def cols(first):
        return pl.ds(pl.multiple_of(first, width), width)

    copies = [
        (far, c_ref.at[other_rows, cols(there + own)]),
        (far_pair, c_ref.at[other_rows, cols(there + pair)]),
    ]
    for k in range(2):
        copies.append((near.at[0, k], stage.at[:, cols(k * half + own)]))
        copies.append((near_pair.at[0, k], stage.at[:, cols(k * half + pair)]))
    load_all(copies, sems)

    def near_tile(rows, j):
        real = stage[rows, pl.ds(j * tile, tile)].astype(F32)
        imag = stage[rows, pl.ds(half + j * tile, tile)].astype(F32)
        total, less = (real + imag).astype(BF16), (real - imag).astype(BF16)
        c_ref[rows, part_of(here, j, tile)] = total
        d_ref[rows, part_of(here, j, tile)] = less
        return total, less

    @pl.loop(0, half // tile)
    def _(i):
        for j in range(half // tile):
            near_tile(part_of(here, i, tile), j)
            total, less = near_tile(part_of(there, i, tile), j)
            c_ref[part_of(here, j, tile), part_of(there, i, tile)] = less.T
            d_ref[part_of(here, j, tile), part_of(there, i, tile)] = total.T
            turned = c_ref[part_of(there, i, tile), part_of(there, j, tile)].T
            d_ref[part_of(there, j, tile), part_of(there, i, tile)] = turned


def assemble_second(place, near, near_pair, far, far_pair, c_ref, d_ref, stage, sems, tile):
    depth, width = near[0].shape
    half = 2 * width
    chunks = half // depth
    here, there = place[2], half - place[2]
    own, pair = place[3], width - place[3]

    def block(rows, cols):
        return pl.ds(pl.multiple_of(rows, depth), depth), pl.ds(pl.multiple_of(cols, width), width)

    copies = []
    for pieces, chip, core in ((near, here, own), (near_pair, here, pair), (far, there, own), (far_pair, there, pair)):
        for k in range(chunks):
            copies.append((pieces[k], c_ref.at[block(chip + k * depth, chip + core)]))
            copies.append((pieces[chunks + k], stage.at[block(chip + k * depth, core)]))
    load_all(copies, sems)

    @pl.loop(0, half // tile)
    def _(i):
        for j in range(half // tile):
            for first in (0, half):
                d_ref[part_of(first, j, tile), part_of(first, i, tile)] = c_ref[
                    part_of(first, i, tile), part_of(first, j, tile)
                ].T
            low = stage[part_of(0, i, tile), part_of(0, j, tile)]
            high = stage[part_of(half, j, tile), part_of(0, i, tile)]
            low_turned, high_turned = low.T.astype(F32), high.T.astype(F32)
            low, high = low.astype(F32), high.astype(F32)
            c_ref[part_of(half, i, tile), part_of(0, j, tile)] = (low - high_turned).astype(BF16)
            d_ref[part_of(half, i, tile), part_of(0, j, tile)] = (low + high_turned).astype(BF16)
            c_ref[part_of(0, j, tile), part_of(half, i, tile)] = (low_turned + high).astype(BF16)
            d_ref[part_of(0, j, tile), part_of(half, i, tile)] = (low_turned - high).astype(BF16)


def own_step(step, start, width, c_ref, d_ref, flat, turned, tile, base, out, parts):
    n = c_ref.shape[0]
    part = min(tile, width)

    @pl.loop(0, width // step.size)
    def _(t):
        c = start // step.size + t
        for s in range(n // tile):
            cols = pl.ds(s * tile, tile)
            products = (
                step.ham(step.minus, c, c_ref, d_ref, cols),
                step.ham(step.plus, c, d_ref, c_ref, cols),
                step.pull(c, d_ref, cols),
                step.pull(c, c_ref, cols),
            )
            for k, product in enumerate(products):
                flat[pl.ds(pl.multiple_of(k * width + t * step.size, step.size), step.size), cols] = product.astype(BF16)

    @pl.loop(0, n // part)
    def _(i):
        near = pl.ds(pl.multiple_of(i * part, part), part)
        for j in range(4 * width // part):
            far = pl.ds(j * part, part)
            turned[near, far] = turned_tile(flat[far, near])

    def finish(first, count, pass_on):
        @pl.loop(0, count)
        def _(t):
            c = first // step.size + t
            own = pl.ds(pl.multiple_of(c * step.size, step.size), step.size)
            for s in range(width // part):
                cols = pl.ds(pl.multiple_of(start + s * part, part), part)
                to = pl.ds(s * part, part)
                of = [pl.ds(k * width + s * part, part) for k in range(4)]
                change = step.ham(step.plus, c, d_ref, c_ref, cols) + step.pull(c, turned, of[2])
                second = step.ham(step.minus, c, c_ref, d_ref, cols) + step.pull(c, turned, of[3])
                change = change + turned[own, of[0]].astype(F32)
                second = second + turned[own, of[1]].astype(F32)
                real, imag = base(own, cols, to)
                real = real + 0.5 * time_step * (change + second)
                imag = imag + 0.5 * time_step * (change - second)
                out[0, 0, own, to] = real.astype(BF16)
                out[0, 1, own, to] = imag.astype(BF16)
                if pass_on is not None:
                    pass_on(pl.ds(pl.multiple_of(t * step.size, step.size), step.size), to, real, imag)

    for first, count, pass_on in parts:
        finish(first, count, pass_on)


def fill_whole(piece, c_ref, d_ref, sems, tile):
    load_all([(piece, c_ref)], sems)
    turn_whole(c_ref, d_ref, tile)


def inner_kernel(counts, tile, number, rows, place, terminal, plus, minus, jump, *refs):
    pieces, refs = refs[:number], refs[number:]
    *outs, c_ref, d_ref, flat, turned, sems = refs
    out, passed = outs[0], outs[1:]
    n, width = out.shape[2], out.shape[3]
    size = plus.shape[1]
    if number == 1:
        fill_whole(pieces[0], c_ref, d_ref, sems, tile)
        parts = [(0, n // size, None)]
    else:
        assemble_first(place, *pieces, c_ref, d_ref, flat, sems, tile)
        depth = passed[0].shape[0]
        half, chunks = 2 * width, 2 * width // depth
        parts = []

        def send_mixed(target, rows, cols, real, imag):
            target[rows, cols] = (real + imag).astype(BF16)

        def send_one(target, rows, cols, real, imag):
            target[rows, cols] = jnp.where(place[2] == 0, real, imag).astype(BF16)

        for k in range(chunks):
            parts.append((place[2] + k * depth, depth // size, functools.partial(send_mixed, passed[k])))
        for k in range(chunks):
            target = passed[chunks + k]
            parts.append((half - place[2] + k * depth, depth // size, functools.partial(send_one, target)))
    step = Step(rows, counts, size, plus, minus, jump)

    def base(own, _, cols):
        return terminal[0, 0, own, cols].astype(F32), terminal[0, 1, own, cols].astype(F32)

    own_step(step, place[0], width, c_ref, d_ref, flat, turned, tile, base, out, parts)


def start_kernel(counts, tile, number, rows, place, terminal, plus, minus, jump, *refs):
    pieces, refs = refs[:number], refs[number:]
    out, c_ref, d_ref, flat, turned, sems = refs
    size = plus.shape[1]

    @pl.when(place[1] == 1)
    def _():
        load_all([(terminal, out)], sems)

    @pl.when(place[1] == 0)
    def _():
        if number == 1:
            fill_whole(pieces[0], c_ref, d_ref, sems, tile)
        else:
            each = number // 4
            groups = [pieces[k * each : (k + 1) * each] for k in range(4)]
            assemble_second(place, *groups, c_ref, d_ref, flat, sems, tile)
        step = Step(rows, counts, size, plus, minus, jump)

        def base(own, cols, _):
            first, second = c_ref[own, cols].astype(F32), d_ref[own, cols].astype(F32)
            return 0.5 * (first + second), 0.5 * (first - second)

        parts = [(0, out.shape[2] // size, None)]
        own_step(step, place[0], out.shape[3], c_ref, d_ref, flat, turned, tile, base, out, parts)


def swapped(block, bit):
    return lax.ppermute(block, "row", [(i, i ^ bit) for i in range(lax.axis_size("row"))])


def on_device(terminal, controls, ham_blocks, ham_cols, jump_blocks, jump_cols):
    n, width = terminal.shape[2], terminal.shape[3]
    tile = 256
    row = lax.axis_index("row")
    here = row // 2 * 2 * width
    controls_next = shifted_down(controls, "tm")
    is_last = lax.axis_index("tm") == lax.axis_size("tm") - 1
    place = jnp.stack([row * width, is_last.astype(jnp.int32), here, row % 2 * width]).astype(jnp.int32)
    amplitudes = jnp.stack([controls[0, 1], controls_next[0, 0]])
    counts, rows, jump_row, plus, minus = operator_tables(ham_blocks, ham_cols, jump_blocks, jump_cols, amplitudes)

    smem = pl.BlockSpec(memory_space=pltpu.SMEM)
    vmem = pl.BlockSpec(memory_space=pltpu.VMEM)
    anywhere = pl.BlockSpec(memory_space=pl.ANY)
    whole_out = jax.ShapeDtypeStruct(terminal.shape, BF16)

    def step_call(kernel, name, state_spec, k, pieces, passed):
        return pl.pallas_call(
            functools.partial(kernel, counts, tile, len(pieces)),
            out_shape=[whole_out] + passed,
            in_specs=[smem, smem, state_spec, vmem, vmem, vmem] + [anywhere] * len(pieces),
            out_specs=[vmem] * (1 + len(passed)),
            scratch_shapes=[
                pltpu.VMEM((n, n), BF16),
                pltpu.VMEM((n, n), BF16),
                pltpu.VMEM((max(4 * width, n), n), BF16),
                pltpu.VMEM((n, 4 * width), BF16),
                pltpu.SemaphoreType.DMA((max(len(pieces), 6),)),
            ],
            compiler_params=pltpu.CompilerParams(vmem_limit_bytes=60 * 2**20),
            cost_estimate=pl.CostEstimate(flops=2 * 10**10, bytes_accessed=16 * 2**20, transcendentals=0),
            name=name,
        )(rows, place, terminal, plus[k], minus[k], jump_row, *pieces)

    if lax.axis_size("row") == 4:
        near_pair = swapped(terminal, 1)
        mine = lax.dynamic_slice_in_dim(terminal[0], here, 2 * width, 1).astype(F32)
        far = swapped((mine[0] + mine[1]).astype(BF16), 2)
        far, rows = lax.optimization_barrier((far, rows))
        chunk = jax.ShapeDtypeStruct((width, width), BF16)
        new_fpoint, *sent = step_call(
            inner_kernel, "inner_point", vmem, 0, [terminal, near_pair, far, swapped(far, 1)], [chunk] * 4
        )
        near, far = [], []
        for k, piece in enumerate(sent):
            if k >= 2:
                piece, _ = lax.optimization_barrier((piece, near[k - 2]))
            near.append(shifted_down(piece, "tm"))
            far.append(swapped(near[k], 2))
        pieces = near + [swapped(piece, 1) for piece in near] + far + [swapped(piece, 1) for piece in far]
        (new_cpoint,) = step_call(start_kernel, "left_end", anywhere, 1, pieces, [])
    else:

        def gathered(mixed):
            return [lax.all_gather(mixed, "row", axis=1, tiled=True)]

        def mixture(state):
            return (state[0, 0].astype(F32) + state[0, 1].astype(F32)).astype(BF16)

        (new_fpoint,) = step_call(inner_kernel, "inner_point", vmem, 0, gathered(mixture(terminal)), [])
        pieces = gathered(shifted_down(mixture(new_fpoint), "tm"))
        (new_cpoint,) = step_call(start_kernel, "left_end", anywhere, 1, pieces, [])
    return (new_cpoint, new_fpoint)


def solution(mesh):
    in_specs = (P(("grp", "tm"), None, None, "row"), P(("grp", "tm"), None), P(), P(), P(), P())
    out_specs = (P(("grp", "tm"), None, None, "row"), P(("grp", "tm"), None, None, "row"))
    return jax.shard_map(
        on_device, mesh=mesh, in_specs=in_specs, out_specs=out_specs, check_vma=False
    )
```

```python
import functools

import jax
import jax.numpy as jnp
from jax import lax
from jax.experimental import pallas as pl
from jax.experimental.pallas import tpu as pltpu
from jax.sharding import PartitionSpec as P

time_step = 0.2
F32 = jnp.float32
BF16 = jnp.bfloat16


def shifted_down(block, axis):
    route = [(i, i - 1) for i in range(1, lax.axis_size(axis))]
    return lax.ppermute(block, axis, route)


def table_kernel(ham_cols, jump_cols, amplitudes, ham, jump, rows, jump_row, *tables):
    layers_h, count = ham_cols.shape
    layers_j = jump_cols.shape[0]
    size = ham.shape[-1]
    crossed = [(k, other) for k in range(layers_j) for other in range(layers_j) if k != other]
    first_k = 2 * layers_h
    first_j = first_k + 1 + len(crossed)

    @pl.loop(0, count)
    def _(b):
        for k in range(layers_h):
            rows[k, b] = ham_cols[k, b] * size
            rows[layers_h + k, ham_cols[k, b]] = b * size
        for k in range(layers_j):
            rows[first_j + k, jump_cols[k, b]] = b * size

    @pl.loop(0, count, unroll=2)
    def _(c):
        came_h = [rows[layers_h + k, c] // size for k in range(layers_h)]
        came_j = [rows[first_j + k, c] // size for k in range(layers_j)]
        rows[first_k, c] = c * size
        for at, (k, other) in enumerate(crossed):
            rows[first_k + 1 + at, c] = jump_cols[other, came_j[k]] * size

        def ham_row(term):
            parts = [ham[term, c, k].astype(F32) for k in range(layers_h)]
            parts += [ham[term, came_h[k], k].astype(F32).T for k in range(layers_h)]
            return jnp.concatenate(parts, axis=1)

        turned = [jump[came_j[k], k].astype(F32).T.astype(BF16) for k in range(layers_j)]
        jump_row[c] = jnp.concatenate(turned, axis=1)
        square = sum(
            jnp.dot(turned[k], jump[came_j[k], k], preferred_element_type=F32) for k in range(layers_j)
        )
        blocks = [square] + [
            jnp.dot(turned[k], jump[came_j[k], other], preferred_element_type=F32) for k, other in crossed
        ]
        decay = -0.5 * jnp.concatenate(blocks, axis=1)
        drift, steer = ham_row(0), ham_row(1)
        for at in range(len(tables) // 2):
            coeffs = drift + amplitudes[at] * steer
            tables[2 * at][c] = jnp.concatenate([coeffs, decay], axis=1).astype(BF16)
            tables[2 * at + 1][c] = jnp.concatenate([-coeffs, decay], axis=1).astype(BF16)


def operator_tables(ham_blocks, ham_cols, jump_blocks, jump_cols, amplitudes):
    layers_h, count = ham_cols.shape
    layers_j = jump_cols.shape[0]
    size = ham_blocks.shape[-1]
    layers_k = 1 + layers_j * (layers_j - 1)
    smem = pl.BlockSpec(memory_space=pltpu.SMEM)
    vmem = pl.BlockSpec(memory_space=pltpu.VMEM)
    table = jax.ShapeDtypeStruct((count, size, (2 * layers_h + layers_k) * size), BF16)
    number = amplitudes.shape[0]
    rows, jump_row, *tables = pl.pallas_call(
        table_kernel,
        out_shape=[
            jax.ShapeDtypeStruct((2 * layers_h + layers_k + layers_j, count), jnp.int32),
            jax.ShapeDtypeStruct((count, size, layers_j * size), BF16),
        ] + [table] * (2 * number),
        in_specs=[smem, smem, smem, vmem, vmem],
        out_specs=[smem, vmem] + [vmem] * (2 * number),
        compiler_params=pltpu.CompilerParams(vmem_limit_bytes=60 * 2**20),
        cost_estimate=pl.CostEstimate(flops=10**9, bytes_accessed=10 * 2**20, transcendentals=0),
        name="operator_tables",
    )(ham_cols, jump_cols, amplitudes, ham_blocks, jump_blocks)
    return (2 * layers_h, layers_k, layers_j), rows, jump_row, tables[0::2], tables[1::2]


class Step:
    def __init__(self, rows, counts, size, plus, minus, jump):
        self.rows, self.counts, self.size = rows, counts, size
        self.plus, self.minus, self.jump = plus, minus, jump

    def take(self, ref, kind, c, cols):
        first = sum(self.counts[:kind])
        return [
            ref[pl.ds(pl.multiple_of(self.rows[first + k, c], self.size), self.size), cols]
            for k in range(self.counts[kind])
        ]

    def ham(self, table, c, ham_ref, decay_ref, cols):
        met = jnp.concatenate(self.take(ham_ref, 0, c, cols) + self.take(decay_ref, 1, c, cols), axis=0)
        return jnp.dot(table[c], met, preferred_element_type=F32)

    def pull(self, c, ref, cols):
        met = jnp.concatenate(self.take(ref, 2, c, cols), axis=0)
        return jnp.dot(self.jump[c], met, preferred_element_type=F32)


def turned_tile(tile):
    return tile.T


def turn_whole(source, target, tile):
    n = source.shape[0] // tile

    @pl.loop(0, n)
    def _(i):
        near = pl.ds(pl.multiple_of(i * tile, tile), tile)
        for j in range(n):
            far = pl.ds(j * tile, tile)
            target[far, near] = turned_tile(source[near, far])


def load_all(copies, sems):
    copies = [pltpu.make_async_copy(source, target, sems.at[k]) for k, (source, target) in enumerate(copies)]
    for copy in copies:
        copy.start()
    for copy in copies:
        copy.wait()


def part_of(first, k, tile):
    return pl.ds(pl.multiple_of(first + k * tile, tile), tile)


def assemble_first(place, near, near_pair, far, far_pair, c_ref, d_ref, stage, other, sems, tile):
    half, width = far.shape
    here, there = place[2], half - place[2]
    own, pair = place[3], width - place[3]

    def cols(first):
        return pl.ds(pl.multiple_of(first, width), width)

    copies = [
        (far, other.at[pl.ds(0, half), cols(own)]),
        (far_pair, other.at[pl.ds(0, half), cols(pair)]),
    ]
    for k in range(2):
        copies.append((near.at[0, k], stage.at[:, cols(k * half + own)]))
        copies.append((near_pair.at[0, k], stage.at[:, cols(k * half + pair)]))
    load_all(copies, sems)

    def mixed(rows, j):
        real = stage[rows, pl.ds(j * tile, tile)].astype(F32)
        imag = stage[rows, pl.ds(half + j * tile, tile)].astype(F32)
        return (real + imag).astype(BF16), (real - imag).astype(BF16)

    @pl.loop(0, half // tile)
    def _(i):
        here_i, there_i = part_of(here, i, tile), part_of(there, i, tile)
        for j in range(half // tile):
            here_j, there_j = part_of(here, j, tile), part_of(there, j, tile)
            total, less = mixed(there_i, j)
            c_ref[there_i, here_j] = total
            d_ref[there_i, here_j] = less
            c_ref[here_j, there_i] = less.T
            d_ref[here_j, there_i] = total.T
            block = other[part_of(0, i, tile), pl.ds(j * tile, tile)]
            c_ref[there_i, there_j] = block
            d_ref[there_j, there_i] = block.T
            total, less = mixed(here_i, j)
            c_ref[here_i, here_j] = total
            d_ref[here_i, here_j] = less


def assemble_second(place, spans, near, near_pair, far, far_pair, c_ref, d_ref, stage, other, sems, tile):
    width = near[0].shape[1]
    half = 2 * width
    here, there = place[2], half - place[2]
    own, pair = place[3], width - place[3]
    copies = []
    for pieces, chip, core in ((near, here, own), (near_pair, here, pair), (far, there, own), (far_pair, there, pair)):
        for piece, (first, depth) in zip(pieces, spans):
            target = other if first < half else stage
            rows = pl.ds(pl.multiple_of(chip + first % half, depth), depth)
            copies.append((piece, target.at[rows, pl.ds(pl.multiple_of(core, width), width)]))
    load_all(copies, sems)

    @pl.loop(0, half // tile)
    def _(i):
        for j in range(half // tile):
            for first in (0, half):
                block = other[part_of(first, i, tile), pl.ds(j * tile, tile)]
                c_ref[part_of(first, i, tile), part_of(first, j, tile)] = block
                d_ref[part_of(first, j, tile), part_of(first, i, tile)] = block.T
            low = stage[part_of(0, i, tile), part_of(0, j, tile)]
            high = stage[part_of(half, j, tile), part_of(0, i, tile)]
            low_turned, high_turned = low.T.astype(F32), high.T.astype(F32)
            low, high = low.astype(F32), high.astype(F32)
            c_ref[part_of(half, i, tile), part_of(0, j, tile)] = (low - high_turned).astype(BF16)
            d_ref[part_of(half, i, tile), part_of(0, j, tile)] = (low + high_turned).astype(BF16)
            c_ref[part_of(0, j, tile), part_of(half, i, tile)] = (low_turned + high).astype(BF16)
            d_ref[part_of(0, j, tile), part_of(half, i, tile)] = (low_turned - high).astype(BF16)


def own_step(step, start, width, c_ref, d_ref, turned, tile, base, out, parts):
    n = c_ref.shape[0]
    part = min(tile, width)
    products = (
        lambda c, cols: step.ham(step.minus, c, c_ref, d_ref, cols),
        lambda c, cols: step.ham(step.plus, c, d_ref, c_ref, cols),
        lambda c, cols: step.pull(c, d_ref, cols),
        lambda c, cols: step.pull(c, c_ref, cols),
    )

    @pl.loop(0, width // part)
    def _(g):
        first = start // step.size + g * (part // step.size)

        @pl.loop(0, n // tile)
        def _(s):
            cols = part_of(0, s, tile)
            for k, product in enumerate(products):
                rows = [product(first + u, cols).astype(BF16) for u in range(part // step.size)]
                turned[cols, part_of(k * width, g, part)] = jnp.concatenate(rows, axis=0).T

    def finish(first, count, pass_on):
        @pl.loop(0, count, unroll=4)
        def _(t):
            c = first // step.size + t
            own = pl.ds(pl.multiple_of(c * step.size, step.size), step.size)
            for s in range(width // part):
                cols = pl.ds(pl.multiple_of(start + s * part, part), part)
                to = pl.ds(s * part, part)
                of = [pl.ds(k * width + s * part, part) for k in range(4)]
                change = step.ham(step.plus, c, d_ref, c_ref, cols) + step.pull(c, turned, of[2])
                second = step.ham(step.minus, c, c_ref, d_ref, cols) + step.pull(c, turned, of[3])
                change = change + turned[own, of[0]].astype(F32)
                second = second + turned[own, of[1]].astype(F32)
                real, imag = base(own, cols, to)
                real = real + 0.5 * time_step * (change + second)
                imag = imag + 0.5 * time_step * (change - second)
                out[0, 0, own, to] = real.astype(BF16)
                out[0, 1, own, to] = imag.astype(BF16)
                if pass_on is not None:
                    pass_on(pl.ds(pl.multiple_of(t * step.size, step.size), step.size), to, real, imag)

    for first, count, pass_on in parts:
        finish(first, count, pass_on)


def fill_whole(piece, c_ref, d_ref, sems, tile):
    load_all([(piece, c_ref)], sems)
    turn_whole(c_ref, d_ref, tile)


def inner_kernel(counts, tile, spans, number, rows, place, terminal, plus, minus, jump, *refs):
    pieces, refs = refs[:number], refs[number:]
    *outs, c_ref, d_ref, stage, turned, sems = refs
    out, passed = outs[0], outs[1:]
    n, width = out.shape[2], out.shape[3]
    size = plus.shape[1]
    half = 2 * width
    if number == 1:
        fill_whole(pieces[0], c_ref, d_ref, sems, tile)
        parts = [(0, n // size, None)]
    else:
        assemble_first(place, *pieces, c_ref, d_ref, stage, turned, sems, tile)

        def send_mixed(rows, cols, real, imag):
            stage[rows, cols] = (real + imag).astype(BF16)

        def send_one(rows, cols, real, imag):
            below = pl.ds(pl.multiple_of(half + rows.start, size), size)
            stage[below, cols] = jnp.where(place[2] == 0, real, imag).astype(BF16)

        parts = [(place[2], half // size, send_mixed), (half - place[2], half // size, send_one)]
    step = Step(rows, counts, size, plus, minus, jump)

    def base(own, _, cols):
        return terminal[0, 0, own, cols].astype(F32), terminal[0, 1, own, cols].astype(F32)

    own_step(step, place[0], width, c_ref, d_ref, turned, tile, base, out, parts)
    if passed:
        load_all([(stage.at[pl.ds(*span), pl.ds(0, width)], to) for span, to in zip(spans, passed)], sems)


def start_kernel(counts, tile, spans, number, rows, place, terminal, plus, minus, jump, *refs):
    pieces, refs = refs[:number], refs[number:]
    out, c_ref, d_ref, stage, turned, sems = refs
    size = plus.shape[1]

    @pl.when(place[1] == 1)
    def _():
        load_all([(terminal, out)], sems)

    @pl.when(place[1] == 0)
    def _():
        if number == 1:
            fill_whole(pieces[0], c_ref, d_ref, sems, tile)
        else:
            each = len(spans)
            groups = [pieces[k * each : (k + 1) * each] for k in range(4)]
            assemble_second(place, spans, *groups, c_ref, d_ref, stage, turned, sems, tile)
        step = Step(rows, counts, size, plus, minus, jump)

        def base(own, cols, _):
            first, second = c_ref[own, cols].astype(F32), d_ref[own, cols].astype(F32)
            return 0.5 * (first + second), 0.5 * (first - second)

        parts = [(0, out.shape[2] // size, None)]
        own_step(step, place[0], out.shape[3], c_ref, d_ref, turned, tile, base, out, parts)


def swapped(block, bit):
    return lax.ppermute(block, "row", [(i, i ^ bit) for i in range(lax.axis_size("row"))])


def on_device(terminal, controls, ham_blocks, ham_cols, jump_blocks, jump_cols):
    n, width = terminal.shape[2], terminal.shape[3]
    tile = 256
    row = lax.axis_index("row")
    here = row // 2 * 2 * width
    controls_next = shifted_down(controls, "tm")
    is_last = lax.axis_index("tm") == lax.axis_size("tm") - 1
    place = jnp.stack([row * width, is_last.astype(jnp.int32), here, row % 2 * width]).astype(jnp.int32)
    amplitudes = jnp.stack([controls[0, 1], controls_next[0, 0]])
    counts, rows, jump_row, plus, minus = operator_tables(ham_blocks, ham_cols, jump_blocks, jump_cols, amplitudes)

    smem = pl.BlockSpec(memory_space=pltpu.SMEM)
    vmem = pl.BlockSpec(memory_space=pltpu.VMEM)
    anywhere = pl.BlockSpec(memory_space=pl.ANY)
    whole_out = jax.ShapeDtypeStruct(terminal.shape, BF16)
    spans, reached = [], 0
    for depth in (width // 2, width // 2, width, width, width // 2, width // 2):
        spans.append((reached, depth))
        reached += depth

    def step_call(kernel, name, state_spec, k, pieces, passed):
        return pl.pallas_call(
            functools.partial(kernel, counts, tile, spans, len(pieces)),
            out_shape=[whole_out] + passed,
            in_specs=[smem, smem, state_spec, vmem, vmem, vmem] + [anywhere] * len(pieces),
            out_specs=[vmem] + [anywhere] * len(passed),
            scratch_shapes=[
                pltpu.VMEM((n, n), BF16),
                pltpu.VMEM((n, n), BF16),
                pltpu.VMEM((n, n), BF16),
                pltpu.VMEM((n, 4 * width), BF16),
                pltpu.SemaphoreType.DMA((max(len(pieces), 6),)),
            ],
            compiler_params=pltpu.CompilerParams(vmem_limit_bytes=60 * 2**20),
            cost_estimate=pl.CostEstimate(flops=2 * 10**10, bytes_accessed=16 * 2**20, transcendentals=0),
            name=name,
        )(rows, place, terminal, plus[k], minus[k], jump_row, *pieces)

    if lax.axis_size("row") == 4:
        near_pair = swapped(terminal, 1)
        mine = lax.dynamic_slice_in_dim(terminal[0], here, 2 * width, 1).astype(F32)
        far = swapped((mine[0] + mine[1]).astype(BF16), 2)
        far, rows = lax.optimization_barrier((far, rows))
        chunks = [jax.ShapeDtypeStruct((depth, width), BF16) for _, depth in spans]
        new_fpoint, *sent = step_call(
            inner_kernel, "inner_point", vmem, 0, [terminal, near_pair, far, swapped(far, 1)], chunks
        )
        near, far = [], []
        for k, piece in enumerate(sent):
            if k >= 2:
                piece, _ = lax.optimization_barrier((piece, near[k - 2]))
            near.append(shifted_down(piece, "tm"))
            far.append(swapped(near[k], 2))
        pieces = near + [swapped(piece, 1) for piece in near] + far + [swapped(piece, 1) for piece in far]
        (new_cpoint,) = step_call(start_kernel, "left_end", anywhere, 1, pieces, [])
    else:

        def gathered(mixed):
            return [lax.all_gather(mixed, "row", axis=1, tiled=True)]

        def mixture(state):
            return (state[0, 0].astype(F32) + state[0, 1].astype(F32)).astype(BF16)

        (new_fpoint,) = step_call(inner_kernel, "inner_point", vmem, 0, gathered(mixture(terminal)), [])
        pieces = gathered(shifted_down(mixture(new_fpoint), "tm"))
        (new_cpoint,) = step_call(start_kernel, "left_end", anywhere, 1, pieces, [])
    return (new_cpoint, new_fpoint)


def solution(mesh):
    in_specs = (P(("grp", "tm"), None, None, "row"), P(("grp", "tm"), None), P(), P(), P(), P())
    out_specs = (P(("grp", "tm"), None, None, "row"), P(("grp", "tm"), None, None, "row"))
    return jax.shard_map(
        on_device, mesh=mesh, in_specs=in_specs, out_specs=out_specs, check_vma=False
    )
```

```python
import functools

import jax
import jax.numpy as jnp
from jax import lax
from jax.experimental import pallas as pl
from jax.experimental.pallas import tpu as pltpu
from jax.sharding import PartitionSpec as P

time_step = 0.2
F32 = jnp.float32
BF16 = jnp.bfloat16


def shifted_down(block, axis):
    route = [(i, i - 1) for i in range(1, lax.axis_size(axis))]
    return lax.ppermute(block, axis, route)


def table_kernel(ham_cols, jump_cols, amplitudes, ham, jump, rows, jump_row, *tables):
    layers_h, count = ham_cols.shape
    layers_j = jump_cols.shape[0]
    size = ham.shape[-1]
    crossed = [(k, other) for k in range(layers_j) for other in range(layers_j) if k != other]
    first_k = 2 * layers_h
    first_j = first_k + 1 + len(crossed)

    @pl.loop(0, count)
    def _(b):
        for k in range(layers_h):
            rows[k, b] = ham_cols[k, b] * size
            rows[layers_h + k, ham_cols[k, b]] = b * size
        for k in range(layers_j):
            rows[first_j + k, jump_cols[k, b]] = b * size

    @pl.loop(0, count, unroll=2)
    def _(c):
        came_h = [rows[layers_h + k, c] // size for k in range(layers_h)]
        came_j = [rows[first_j + k, c] // size for k in range(layers_j)]
        rows[first_k, c] = c * size
        for at, (k, other) in enumerate(crossed):
            rows[first_k + 1 + at, c] = jump_cols[other, came_j[k]] * size

        def ham_row(term):
            parts = [ham[term, c, k].astype(F32) for k in range(layers_h)]
            parts += [ham[term, came_h[k], k].astype(F32).T for k in range(layers_h)]
            return jnp.concatenate(parts, axis=1)

        turned = [jump[came_j[k], k].astype(F32).T.astype(BF16) for k in range(layers_j)]
        jump_row[c] = jnp.concatenate(turned, axis=1)
        square = sum(
            jnp.dot(turned[k], jump[came_j[k], k], preferred_element_type=F32) for k in range(layers_j)
        )
        blocks = [square] + [
            jnp.dot(turned[k], jump[came_j[k], other], preferred_element_type=F32) for k, other in crossed
        ]
        decay = -0.5 * jnp.concatenate(blocks, axis=1)
        drift, steer = ham_row(0), ham_row(1)
        for at in range(len(tables) // 2):
            coeffs = drift + amplitudes[at] * steer
            tables[2 * at][c] = jnp.concatenate([coeffs, decay], axis=1).astype(BF16)
            tables[2 * at + 1][c] = jnp.concatenate([-coeffs, decay], axis=1).astype(BF16)


def operator_tables(ham_blocks, ham_cols, jump_blocks, jump_cols, amplitudes):
    layers_h, count = ham_cols.shape
    layers_j = jump_cols.shape[0]
    size = ham_blocks.shape[-1]
    layers_k = 1 + layers_j * (layers_j - 1)
    smem = pl.BlockSpec(memory_space=pltpu.SMEM)
    vmem = pl.BlockSpec(memory_space=pltpu.VMEM)
    table = jax.ShapeDtypeStruct((count, size, (2 * layers_h + layers_k) * size), BF16)
    number = amplitudes.shape[0]
    rows, jump_row, *tables = pl.pallas_call(
        table_kernel,
        out_shape=[
            jax.ShapeDtypeStruct((2 * layers_h + layers_k + layers_j, count), jnp.int32),
            jax.ShapeDtypeStruct((count, size, layers_j * size), BF16),
        ] + [table] * (2 * number),
        in_specs=[smem, smem, smem, vmem, vmem],
        out_specs=[smem, vmem] + [vmem] * (2 * number),
        compiler_params=pltpu.CompilerParams(vmem_limit_bytes=60 * 2**20),
        cost_estimate=pl.CostEstimate(flops=1, bytes_accessed=1, transcendentals=0),
        name="operator_tables",
    )(ham_cols, jump_cols, amplitudes, ham_blocks, jump_blocks)
    return (2 * layers_h, layers_k, layers_j), rows, jump_row, tables[0::2], tables[1::2]


class Step:
    def __init__(self, rows, counts, size, plus, minus, jump):
        self.rows, self.counts, self.size = rows, counts, size
        self.plus, self.minus, self.jump = plus, minus, jump

    def take(self, ref, kind, c, cols):
        first = sum(self.counts[:kind])
        return [
            ref[pl.ds(pl.multiple_of(self.rows[first + k, c], self.size), self.size), cols]
            for k in range(self.counts[kind])
        ]

    def ham(self, table, c, ham_ref, decay_ref, cols):
        met = jnp.concatenate(self.take(ham_ref, 0, c, cols) + self.take(decay_ref, 1, c, cols), axis=0)
        return jnp.dot(table[c], met, preferred_element_type=F32)

    def pull(self, c, ref, cols):
        met = jnp.concatenate(self.take(ref, 2, c, cols), axis=0)
        return jnp.dot(self.jump[c], met, preferred_element_type=F32)


def turn_whole(source, target, tile):
    n = source.shape[0] // tile

    @pl.loop(0, n)
    def _(i):
        near = pl.ds(pl.multiple_of(i * tile, tile), tile)
        for j in range(n):
            far = pl.ds(j * tile, tile)
            target[far, near] = source[near, far].T


def load_all(copies, sems):
    copies = [pltpu.make_async_copy(source, target, sems.at[k]) for k, (source, target) in enumerate(copies)]
    for copy in copies:
        copy.start()
    for copy in copies:
        copy.wait()


def part_of(first, k, tile):
    return pl.ds(pl.multiple_of(first + k * tile, tile), tile)


def assemble_first(place, near, near_pair, far, far_pair, c_ref, d_ref, stage, other, sems, tile):
    half, width = far.shape
    here, there = place[2], half - place[2]
    own, pair = place[3], width - place[3]

    def cols(first):
        return pl.ds(pl.multiple_of(first, width), width)

    copies = [
        (far, other.at[pl.ds(0, half), cols(own)]),
        (far_pair, other.at[pl.ds(0, half), cols(pair)]),
    ]
    for k in range(2):
        copies.append((near.at[0, k], stage.at[:, cols(k * half + own)]))
        copies.append((near_pair.at[0, k], stage.at[:, cols(k * half + pair)]))
    load_all(copies, sems)

    def mixed(rows, j):
        real = stage[rows, pl.ds(j * tile, tile)].astype(F32)
        imag = stage[rows, pl.ds(half + j * tile, tile)].astype(F32)
        return (real + imag).astype(BF16), (real - imag).astype(BF16)

    @pl.loop(0, half // tile)
    def _(i):
        here_i, there_i = part_of(here, i, tile), part_of(there, i, tile)
        for j in range(half // tile):
            here_j, there_j = part_of(here, j, tile), part_of(there, j, tile)
            total, less = mixed(there_i, j)
            c_ref[there_i, here_j] = total
            d_ref[there_i, here_j] = less
            c_ref[here_j, there_i] = less.T
            d_ref[here_j, there_i] = total.T
            block = other[part_of(0, i, tile), pl.ds(j * tile, tile)]
            c_ref[there_i, there_j] = block
            d_ref[there_j, there_i] = block.T
            total, less = mixed(here_i, j)
            c_ref[here_i, here_j] = total
            d_ref[here_i, here_j] = less


def assemble_next(place, near, near_pair, far, far_pair, c_ref, d_ref, stage, other, sems, tile):
    half, width = far.shape
    here, there = place[2], half - place[2]
    copies = []
    for pieces, last, core in ((near, far, place[3]), (near_pair, far_pair, width - place[3])):
        for k, piece in enumerate((*pieces, last)):
            target = other if k in (0, 3) else stage
            to = pl.ds(pl.multiple_of((0, 0, half, half)[k] + core, width), width)
            copies.append((piece, target.at[pl.ds(0, half), to]))
    load_all(copies, sems)

    @pl.loop(0, half // tile)
    def _(i):
        rows = part_of(0, i, tile)
        here_i, there_i = part_of(here, i, tile), part_of(there, i, tile)
        for j in range(half // tile):
            here_j, there_j = part_of(here, j, tile), part_of(there, j, tile)
            real = stage[rows, pl.ds(j * tile, tile)].astype(F32)
            imag = stage[rows, pl.ds(half + j * tile, tile)].astype(F32)
            total, less = (real + imag).astype(BF16), (real - imag).astype(BF16)
            c_ref[there_i, here_j] = total
            d_ref[there_i, here_j] = less
            c_ref[here_j, there_i] = less.T
            d_ref[here_j, there_i] = total.T
            block = other[rows, pl.ds(j * tile, tile)]
            c_ref[here_i, here_j] = block
            d_ref[here_j, here_i] = block.T
            block = other[rows, pl.ds(half + j * tile, tile)]
            c_ref[there_i, there_j] = block
            d_ref[there_j, there_i] = block.T


def whole_step(step, c_ref, d_ref, r_ref, x_ref, c_new, d_new, tile):
    n = c_ref.shape[0]
    count = tile // step.size
    products = (
        (r_ref, lambda c, cols: step.ham(step.minus, c, c_ref, d_ref, cols)),
        (x_ref, lambda c, cols: step.pull(c, d_ref, cols)),
    )

    @pl.loop(0, n // tile)
    def _(g):
        @pl.loop(0, n // tile, unroll=2)
        def _(s):
            cols = part_of(0, s, tile)
            for target, product in products:
                rows = [product(g * count + u, cols).astype(BF16) for u in range(count)]
                target[cols, part_of(0, g, tile)] = jnp.concatenate(rows, axis=0).T

    @pl.loop(0, n // tile)
    def _(g):
        @pl.loop(0, n // tile, unroll=2)
        def _(s):
            cols = part_of(0, s, tile)
            made = []
            for u in range(count):
                c = g * count + u
                own = pl.ds(pl.multiple_of(c * step.size, step.size), step.size)
                change = step.ham(step.plus, c, d_ref, c_ref, cols) + step.pull(c, x_ref, cols)
                change = change + r_ref[own, cols].astype(F32)
                made.append((c_ref[own, cols].astype(F32) + time_step * change).astype(BF16))
                c_new[own, cols] = made[u]
            d_new[cols, part_of(0, g, tile)] = jnp.concatenate(made, axis=0).T


def own_step(step, start, width, c_ref, d_ref, turned, tile, base, out):
    n = c_ref.shape[0]
    part = min(tile, width)
    products = (
        lambda c, cols: step.ham(step.minus, c, c_ref, d_ref, cols),
        lambda c, cols: step.ham(step.plus, c, d_ref, c_ref, cols),
        lambda c, cols: step.pull(c, d_ref, cols),
        lambda c, cols: step.pull(c, c_ref, cols),
    )

    @pl.loop(0, width // part)
    def _(g):
        first = start // step.size + g * (part // step.size)

        @pl.loop(0, n // tile)
        def _(s):
            cols = part_of(0, s, tile)
            for k, product in enumerate(products):
                rows = [product(first + u, cols).astype(BF16) for u in range(part // step.size)]
                turned[cols, part_of(k * width, g, part)] = jnp.concatenate(rows, axis=0).T

    @pl.loop(0, n // step.size, unroll=4)
    def _(c):
        own = pl.ds(pl.multiple_of(c * step.size, step.size), step.size)
        for s in range(width // part):
            cols = pl.ds(pl.multiple_of(start + s * part, part), part)
            to = pl.ds(s * part, part)
            of = [pl.ds(k * width + s * part, part) for k in range(4)]
            change = step.ham(step.plus, c, d_ref, c_ref, cols) + step.pull(c, turned, of[2])
            second = step.ham(step.minus, c, c_ref, d_ref, cols) + step.pull(c, turned, of[3])
            change = change + turned[own, of[0]].astype(F32)
            second = second + turned[own, of[1]].astype(F32)
            real, imag = base(own, cols, to)
            out[0, 0, own, to] = (real + 0.5 * time_step * (change + second)).astype(BF16)
            out[0, 1, own, to] = (imag + 0.5 * time_step * (change - second)).astype(BF16)


def fill_whole(piece, c_ref, d_ref, sems, tile):
    load_all([(piece, c_ref)], sems)
    turn_whole(c_ref, d_ref, tile)


def inner_kernel(counts, tile, number, rows, place, terminal, plus, minus, jump, *refs):
    pieces, refs = refs[:number], refs[number:]
    out, c_ref, d_ref, stage, turned, sems = refs
    if number == 1:
        fill_whole(pieces[0], c_ref, d_ref, sems, tile)
    else:
        assemble_first(place, *pieces, c_ref, d_ref, stage, turned, sems, tile)
    step = Step(rows, counts, plus.shape[1], plus, minus, jump)

    def base(own, _, cols):
        return terminal[0, 0, own, cols].astype(F32), terminal[0, 1, own, cols].astype(F32)

    own_step(step, place[0], out.shape[3], c_ref, d_ref, turned, tile, base, out)


def start_kernel(counts, tile, number, rows, place, terminal, plus, minus, jump, plus_two, minus_two, *refs):
    pieces, refs = refs[:number], refs[number:]
    out, c_ref, d_ref, r_ref, x_ref, c_new, d_new, sems = refs
    size = plus.shape[1]

    @pl.when(place[1] == 1)
    def _():
        load_all([(terminal, out)], sems)

    @pl.when(place[1] == 0)
    def _():
        if number == 1:
            fill_whole(pieces[0], c_ref, d_ref, sems, tile)
        else:
            near, near_pair = pieces[0:3], pieces[3:6]
            assemble_next(place, near, near_pair, *pieces[6:], c_ref, d_ref, r_ref, x_ref, sems, tile)
        whole_step(Step(rows, counts, size, plus, minus, jump), c_ref, d_ref, r_ref, x_ref, c_new, d_new, tile)

        def base(own, cols, _):
            first, second = c_new[own, cols].astype(F32), d_new[own, cols].astype(F32)
            return 0.5 * (first + second), 0.5 * (first - second)

        step = Step(rows, counts, size, plus_two, minus_two, jump)
        own_step(step, place[0], out.shape[3], c_new, d_new, r_ref, tile, base, out)


def swapped(block, bit):
    return lax.ppermute(block, "row", [(i, i ^ bit) for i in range(lax.axis_size("row"))])


def on_device(terminal, controls, ham_blocks, ham_cols, jump_blocks, jump_cols):
    n, width = terminal.shape[2], terminal.shape[3]
    tile = 256
    row = lax.axis_index("row")
    here = row // 2 * 2 * width
    controls_next = shifted_down(controls, "tm")
    is_last = lax.axis_index("tm") == lax.axis_size("tm") - 1
    place = jnp.stack([row * width, is_last.astype(jnp.int32), here, row % 2 * width]).astype(jnp.int32)
    amplitudes = jnp.stack([controls[0, 1], controls_next[0, 1], controls_next[0, 0]])
    counts, rows, jump_row, plus, minus = operator_tables(ham_blocks, ham_cols, jump_blocks, jump_cols, amplitudes)

    smem = pl.BlockSpec(memory_space=pltpu.SMEM)
    vmem = pl.BlockSpec(memory_space=pltpu.VMEM)
    anywhere = pl.BlockSpec(memory_space=pl.ANY)
    square = pltpu.VMEM((n, n), BF16)

    def step_call(kernel, name, state_spec, squares, tables, pieces):
        return pl.pallas_call(
            functools.partial(kernel, counts, tile, len(pieces)),
            out_shape=jax.ShapeDtypeStruct(terminal.shape, BF16),
            in_specs=[smem, smem, state_spec] + [vmem] * len(tables) + [anywhere] * len(pieces),
            out_specs=vmem,
            scratch_shapes=[square] * squares + [pltpu.SemaphoreType.DMA((max(len(pieces), 6),))],
            compiler_params=pltpu.CompilerParams(vmem_limit_bytes=60 * 2**20),
            cost_estimate=pl.CostEstimate(flops=1, bytes_accessed=1, transcendentals=0),
            name=name,
        )(rows, place, terminal, *tables, *pieces)

    first = [plus[0], minus[0], jump_row]
    second = [plus[1], minus[1], jump_row, plus[2], minus[2]]
    if lax.axis_size("row") == 4:
        near_pair = swapped(terminal, 1)
        mine = lax.dynamic_slice_in_dim(terminal[0], here, 2 * width, 1).astype(F32)
        mixed = (mine[0] + mine[1]).astype(BF16)
        apart = lax.dynamic_slice_in_dim(terminal[0], 2 * width - here, 2 * width, 1)
        far = swapped(mixed, 2)
        mixed, real, imag, _ = lax.optimization_barrier((mixed, apart[0], apart[1], controls_next))
        near = [shifted_down(piece, "tm") for piece in (mixed, real, imag)]
        far, rows, near[0] = lax.optimization_barrier((far, rows, near[0]))
        far_next = swapped(near[0], 2)
        new_fpoint = step_call(inner_kernel, "inner_point", vmem, 4, first, [terminal, near_pair, far, swapped(far, 1)])
        pair = [swapped(near[0], 1)]
        near[1], near[2], far_next, new_fpoint = lax.optimization_barrier((near[1], near[2], far_next, new_fpoint))
        pair += [swapped(piece, 1) for piece in near[1:]]
        pieces = near + pair + [far_next, swapped(far_next, 1)]
    else:
        mixed = (terminal[0, 0].astype(F32) + terminal[0, 1].astype(F32)).astype(BF16)

        def gathered(piece):
            return [lax.all_gather(piece, "row", axis=1, tiled=True)]

        new_fpoint = step_call(inner_kernel, "inner_point", vmem, 4, first, gathered(mixed))
        pieces = gathered(shifted_down(mixed, "tm"))
    new_cpoint = step_call(start_kernel, "left_end", anywhere, 6, second, pieces)
    return (new_cpoint, new_fpoint)


def solution(mesh):
    in_specs = (P(("grp", "tm"), None, None, "row"), P(("grp", "tm"), None), P(), P(), P(), P())
    out_specs = (P(("grp", "tm"), None, None, "row"), P(("grp", "tm"), None, None, "row"))
    return jax.shard_map(
        on_device, mesh=mesh, in_specs=in_specs, out_specs=out_specs, check_vma=False
    )
```

```python
import functools

import jax
import jax.numpy as jnp
from jax import lax
from jax.experimental import pallas as pl
from jax.experimental.pallas import tpu as pltpu
from jax.sharding import PartitionSpec as P

time_step = 0.2
F32 = jnp.float32
BF16 = jnp.bfloat16


def shifted_down(block, axis):
    route = [(i, i - 1) for i in range(1, lax.axis_size(axis))]
    return lax.ppermute(block, axis, route)


def table_kernel(which, ham_cols, jump_cols, controls, controls_next, ham, jump, rows, jump_row, *tables):
    layers_h, count = ham_cols.shape
    layers_j = jump_cols.shape[0]
    size = ham.shape[-1]
    crossed = [(k, other) for k in range(layers_j) for other in range(layers_j) if k != other]
    first_k = 2 * layers_h
    first_j = first_k + 1 + len(crossed)

    @pl.loop(0, count)
    def _(b):
        for k in range(layers_h):
            rows[k, b] = ham_cols[k, b] * size
            rows[layers_h + k, ham_cols[k, b]] = b * size
        for k in range(layers_j):
            rows[first_j + k, jump_cols[k, b]] = b * size

    @pl.loop(0, count, unroll=8)
    def _(c):
        came_h = [rows[layers_h + k, c] // size for k in range(layers_h)]
        came_j = [rows[first_j + k, c] // size for k in range(layers_j)]
        rows[first_k, c] = c * size
        for at, (k, other) in enumerate(crossed):
            rows[first_k + 1 + at, c] = jump_cols[other, came_j[k]] * size

        def ham_row(term):
            parts = [ham[term, c, k].astype(F32) for k in range(layers_h)]
            parts += [ham[term, came_h[k], k].astype(F32).T for k in range(layers_h)]
            return jnp.concatenate(parts, axis=1)

        turned = [jump[came_j[k], k].astype(F32).T.astype(BF16) for k in range(layers_j)]
        jump_row[c] = jnp.concatenate(turned, axis=1)
        square = sum(
            jnp.dot(turned[k], jump[came_j[k], k], preferred_element_type=F32) for k in range(layers_j)
        )
        blocks = [square] + [
            jnp.dot(turned[k], jump[came_j[k], other], preferred_element_type=F32) for k, other in crossed
        ]
        decay = -0.5 * jnp.concatenate(blocks, axis=1)
        drift, steer = ham_row(0), ham_row(1)
        for at, (later, fine) in enumerate(which):
            amplitude = (controls, controls_next)[later][0, fine]
            coeffs = drift + amplitude * steer
            tables[2 * at][c] = jnp.concatenate([coeffs, decay], axis=1).astype(BF16)
            tables[2 * at + 1][c] = jnp.concatenate([-coeffs, decay], axis=1).astype(BF16)


def operator_tables(which, ham_blocks, ham_cols, jump_blocks, jump_cols, controls, controls_next):
    layers_h, count = ham_cols.shape
    layers_j = jump_cols.shape[0]
    size = ham_blocks.shape[-1]
    layers_k = 1 + layers_j * (layers_j - 1)
    smem = pl.BlockSpec(memory_space=pltpu.SMEM)
    vmem = pl.BlockSpec(memory_space=pltpu.VMEM)
    table = jax.ShapeDtypeStruct((count, size, (2 * layers_h + layers_k) * size), BF16)
    number = len(which)
    rows, jump_row, *tables = pl.pallas_call(
        functools.partial(table_kernel, which),
        out_shape=[
            jax.ShapeDtypeStruct((2 * layers_h + layers_k + layers_j, count), jnp.int32),
            jax.ShapeDtypeStruct((count, size, layers_j * size), BF16),
        ] + [table] * (2 * number),
        in_specs=[smem, smem, smem, smem, vmem, vmem],
        out_specs=[smem, vmem] + [vmem] * (2 * number),
        compiler_params=pltpu.CompilerParams(vmem_limit_bytes=60 * 2**20),
        cost_estimate=pl.CostEstimate(flops=1, bytes_accessed=1, transcendentals=0),
        name="operator_tables",
    )(ham_cols, jump_cols, controls, controls_next, ham_blocks, jump_blocks)
    return (2 * layers_h, layers_k, layers_j), rows, jump_row, tables[0::2], tables[1::2]


class Step:
    def __init__(self, rows, counts, size, plus, minus, jump):
        self.rows, self.counts, self.size = rows, counts, size
        self.plus, self.minus, self.jump = plus, minus, jump

    def take(self, ref, kind, c, cols):
        first = sum(self.counts[:kind])
        return [
            ref[pl.ds(pl.multiple_of(self.rows[first + k, c], self.size), self.size), cols]
            for k in range(self.counts[kind])
        ]

    def ham(self, table, c, ham_ref, decay_ref, cols):
        met = jnp.concatenate(self.take(ham_ref, 0, c, cols) + self.take(decay_ref, 1, c, cols), axis=0)
        return jnp.dot(table[c], met, preferred_element_type=F32)

    def pull(self, c, ref, cols):
        met = jnp.concatenate(self.take(ref, 2, c, cols), axis=0)
        return jnp.dot(self.jump[c], met, preferred_element_type=F32)


def turn_whole(source, target, tile):
    n = source.shape[0] // tile

    @pl.loop(0, n)
    def _(i):
        near = pl.ds(pl.multiple_of(i * tile, tile), tile)
        for j in range(n):
            far = pl.ds(j * tile, tile)
            target[far, near] = source[near, far].T


def load_all(copies, sems):
    copies = [pltpu.make_async_copy(source, target, sems.at[k]) for k, (source, target) in enumerate(copies)]
    for copy in copies:
        copy.start()
    for copy in copies:
        copy.wait()


def part_of(first, k, tile):
    return pl.ds(pl.multiple_of(first + k * tile, tile), tile)


def assemble_first(place, near, near_pair, far, far_pair, c_ref, d_ref, stage, other, sems, tile):
    half, width = far.shape
    here, there = place[2], half - place[2]
    own, pair = place[3], width - place[3]

    def cols(first):
        return pl.ds(pl.multiple_of(first, width), width)

    copies = [
        (far, other.at[pl.ds(0, half), cols(own)]),
        (far_pair, other.at[pl.ds(0, half), cols(pair)]),
    ]
    for k in range(2):
        copies.append((near.at[0, k], stage.at[:, cols(k * half + own)]))
        copies.append((near_pair.at[0, k], stage.at[:, cols(k * half + pair)]))
    load_all(copies, sems)

    def mixed(rows, j):
        real = stage[rows, pl.ds(j * tile, tile)].astype(F32)
        imag = stage[rows, pl.ds(half + j * tile, tile)].astype(F32)
        return (real + imag).astype(BF16), (real - imag).astype(BF16)

    @pl.loop(0, half // tile)
    def _(i):
        here_i, there_i = part_of(here, i, tile), part_of(there, i, tile)
        for j in range(half // tile):
            here_j, there_j = part_of(here, j, tile), part_of(there, j, tile)
            total, less = mixed(there_i, j)
            c_ref[there_i, here_j] = total
            d_ref[there_i, here_j] = less
            c_ref[here_j, there_i] = less.T
            d_ref[here_j, there_i] = total.T
            block = other[part_of(0, i, tile), pl.ds(j * tile, tile)]
            c_ref[there_i, there_j] = block
            d_ref[there_j, there_i] = block.T
            total, less = mixed(here_i, j)
            c_ref[here_i, here_j] = total
            d_ref[here_i, here_j] = less


def assemble_next(place, pieces, c_ref, d_ref, stage, other, sems, tile):
    half, width = pieces[0].shape
    here, there = place[2], half - place[2]
    copies = []
    for (near, apart, far), core in ((pieces[:3], place[3]), (pieces[3:], width - place[3])):
        low = pl.ds(pl.multiple_of(core, width), width)
        high = pl.ds(pl.multiple_of(half + core, width), width)
        rows = pl.ds(0, half)
        copies += [(near, other.at[rows, low]), (far, other.at[rows, high])]
        copies += [(apart.at[0], stage.at[rows, low]), (apart.at[1], stage.at[rows, high])]
    load_all(copies, sems)

    @pl.loop(0, half // tile)
    def _(i):
        rows = part_of(0, i, tile)
        here_i, there_i = part_of(here, i, tile), part_of(there, i, tile)
        for j in range(half // tile):
            here_j, there_j = part_of(here, j, tile), part_of(there, j, tile)
            real = stage[rows, pl.ds(j * tile, tile)].astype(F32)
            imag = stage[rows, pl.ds(half + j * tile, tile)].astype(F32)
            total, less = (real + imag).astype(BF16), (real - imag).astype(BF16)
            c_ref[there_i, here_j] = total
            d_ref[there_i, here_j] = less
            c_ref[here_j, there_i] = less.T
            d_ref[here_j, there_i] = total.T
            block = other[rows, pl.ds(j * tile, tile)]
            c_ref[here_i, here_j] = block
            d_ref[here_j, here_i] = block.T
            block = other[rows, pl.ds(half + j * tile, tile)]
            c_ref[there_i, there_j] = block
            d_ref[there_j, there_i] = block.T


def whole_step(step, c_ref, d_ref, r_ref, x_ref, c_new, d_new, tile):
    n = c_ref.shape[0]
    count = tile // step.size
    products = (
        (r_ref, lambda c, cols: step.ham(step.minus, c, c_ref, d_ref, cols)),
        (x_ref, lambda c, cols: step.pull(c, d_ref, cols)),
    )

    @pl.loop(0, n // tile)
    def _(g):
        @pl.loop(0, n // tile, unroll=2)
        def _(s):
            cols = part_of(0, s, tile)
            for target, product in products:
                rows = [product(g * count + u, cols).astype(BF16) for u in range(count)]
                target[cols, part_of(0, g, tile)] = jnp.concatenate(rows, axis=0).T

    @pl.loop(0, n // tile)
    def _(g):
        @pl.loop(0, n // tile, unroll=2)
        def _(s):
            cols = part_of(0, s, tile)
            made = []
            for u in range(count):
                c = g * count + u
                own = pl.ds(pl.multiple_of(c * step.size, step.size), step.size)
                change = step.ham(step.plus, c, d_ref, c_ref, cols) + step.pull(c, x_ref, cols)
                change = change + r_ref[own, cols].astype(F32)
                made.append((c_ref[own, cols].astype(F32) + time_step * change).astype(BF16))
                c_new[own, cols] = made[u]
            d_new[cols, part_of(0, g, tile)] = jnp.concatenate(made, axis=0).T


def own_step(step, start, width, c_ref, d_ref, turned, tile, base, out):
    n = c_ref.shape[0]
    part = min(tile, width)
    products = (
        lambda c, cols: step.ham(step.minus, c, c_ref, d_ref, cols),
        lambda c, cols: step.ham(step.plus, c, d_ref, c_ref, cols),
        lambda c, cols: step.pull(c, d_ref, cols),
        lambda c, cols: step.pull(c, c_ref, cols),
    )

    @pl.loop(0, width // part)
    def _(g):
        first = start // step.size + g * (part // step.size)

        @pl.loop(0, n // tile)
        def _(s):
            cols = part_of(0, s, tile)
            for k, product in enumerate(products):
                rows = [product(first + u, cols).astype(BF16) for u in range(part // step.size)]
                turned[cols, part_of(k * width, g, part)] = jnp.concatenate(rows, axis=0).T

    @pl.loop(0, n // step.size, unroll=4)
    def _(c):
        own = pl.ds(pl.multiple_of(c * step.size, step.size), step.size)
        for s in range(width // part):
            cols = pl.ds(pl.multiple_of(start + s * part, part), part)
            to = pl.ds(s * part, part)
            of = [pl.ds(k * width + s * part, part) for k in range(4)]
            change = step.ham(step.plus, c, d_ref, c_ref, cols) + step.pull(c, turned, of[2])
            second = step.ham(step.minus, c, c_ref, d_ref, cols) + step.pull(c, turned, of[3])
            change = change + turned[own, of[0]].astype(F32)
            second = second + turned[own, of[1]].astype(F32)
            real, imag = base(own, cols, to)
            out[0, 0, own, to] = (real + 0.5 * time_step * (change + second)).astype(BF16)
            out[0, 1, own, to] = (imag + 0.5 * time_step * (change - second)).astype(BF16)


def fill_whole(piece, c_ref, d_ref, sems, tile):
    load_all([(piece, c_ref)], sems)
    turn_whole(c_ref, d_ref, tile)


def inner_kernel(counts, tile, number, rows, place, terminal, plus, minus, jump, *refs):
    pieces, refs = refs[:number], refs[number:]
    out, c_ref, d_ref, stage, turned, sems = refs
    if number == 1:
        fill_whole(pieces[0], c_ref, d_ref, sems, tile)
    else:
        assemble_first(place, *pieces, c_ref, d_ref, stage, turned, sems, tile)
    step = Step(rows, counts, plus.shape[1], plus, minus, jump)

    def base(own, _, cols):
        return terminal[0, 0, own, cols].astype(F32), terminal[0, 1, own, cols].astype(F32)

    own_step(step, place[0], out.shape[3], c_ref, d_ref, turned, tile, base, out)


def start_kernel(counts, tile, number, rows, place, terminal, plus, minus, jump, plus_two, minus_two, *refs):
    pieces, refs = refs[:number], refs[number:]
    out, c_ref, d_ref, r_ref, x_ref, c_new, d_new, sems = refs
    size = plus.shape[1]

    @pl.when(place[1] == 1)
    def _():
        load_all([(terminal, out)], sems)

    @pl.when(place[1] == 0)
    def _():
        if number == 1:
            fill_whole(pieces[0], c_ref, d_ref, sems, tile)
        else:
            assemble_next(place, pieces, c_ref, d_ref, r_ref, x_ref, sems, tile)
        whole_step(Step(rows, counts, size, plus, minus, jump), c_ref, d_ref, r_ref, x_ref, c_new, d_new, tile)

        def base(own, cols, _):
            first, second = c_new[own, cols].astype(F32), d_new[own, cols].astype(F32)
            return 0.5 * (first + second), 0.5 * (first - second)

        step = Step(rows, counts, size, plus_two, minus_two, jump)
        own_step(step, place[0], out.shape[3], c_new, d_new, r_ref, tile, base, out)


def swapped(block, bit):
    return lax.ppermute(block, "row", [(i, i ^ bit) for i in range(lax.axis_size("row"))])


def on_device(terminal, controls, ham_blocks, ham_cols, jump_blocks, jump_cols):
    n, width = terminal.shape[2], terminal.shape[3]
    tile = 256
    row = lax.axis_index("row")
    here = row // 2 * 2 * width
    controls_next = shifted_down(controls, "tm")
    is_last = lax.axis_index("tm") == lax.axis_size("tm") - 1
    place = jnp.stack([row * width, is_last.astype(jnp.int32), here, row % 2 * width]).astype(jnp.int32)
    operators = (ham_blocks, ham_cols, jump_blocks, jump_cols)
    which = ((0, 1), (1, 1), (1, 0))
    counts, rows, jump_row, plus, minus = operator_tables(which, *operators, controls, controls_next)

    smem = pl.BlockSpec(memory_space=pltpu.SMEM)
    vmem = pl.BlockSpec(memory_space=pltpu.VMEM)
    anywhere = pl.BlockSpec(memory_space=pl.ANY)
    square = pltpu.VMEM((n, n), BF16)

    def step_call(kernel, name, state_spec, squares, tables, pieces):
        return pl.pallas_call(
            functools.partial(kernel, counts, tile, len(pieces)),
            out_shape=jax.ShapeDtypeStruct(terminal.shape, BF16),
            in_specs=[smem, smem, state_spec] + [vmem] * len(tables) + [anywhere] * len(pieces),
            out_specs=vmem,
            scratch_shapes=[square] * squares + [pltpu.SemaphoreType.DMA((8,))],
            compiler_params=pltpu.CompilerParams(vmem_limit_bytes=60 * 2**20),
            cost_estimate=pl.CostEstimate(flops=1, bytes_accessed=1, transcendentals=0),
            name=name,
        )(rows, place, terminal, *tables, *pieces)

    first = [plus[0], minus[0], jump_row]
    second = [plus[1], minus[1], jump_row, plus[2], minus[2]]
    if lax.axis_size("row") == 4:
        near_pair = swapped(terminal, 1)
        size = (1, 1, 2 * width, width)
        mine = [lax.dynamic_slice(terminal, (0, k, here, 0), size)[0, 0].astype(F32) for k in range(2)]
        mixed = (mine[0] + mine[1]).astype(BF16)
        apart = lax.dynamic_slice(terminal, (0, 0, 2 * width - here, 0), (1, 2, 2 * width, width))[0]
        far = swapped(mixed, 2)
        mixed, apart, _ = lax.optimization_barrier((mixed, apart, controls_next))
        mixed, apart = shifted_down(mixed, "tm"), shifted_down(apart, "tm")
        far, rows, mixed = lax.optimization_barrier((far, rows, mixed))
        far_next = swapped(mixed, 2)
        new_fpoint = step_call(inner_kernel, "inner_point", vmem, 4, first, [terminal, near_pair, far, swapped(far, 1)])
        mixed_pair = swapped(mixed, 1)
        apart, far_next, new_fpoint = lax.optimization_barrier((apart, far_next, new_fpoint))
        pieces = [mixed, apart, far_next, mixed_pair, swapped(apart, 1), swapped(far_next, 1)]
    else:
        mixed = (terminal[0, 0].astype(F32) + terminal[0, 1].astype(F32)).astype(BF16)

        def gathered(piece):
            return [lax.all_gather(piece, "row", axis=1, tiled=True)]

        new_fpoint = step_call(inner_kernel, "inner_point", vmem, 4, first, gathered(mixed))
        pieces = gathered(shifted_down(mixed, "tm"))
    new_cpoint = step_call(start_kernel, "left_end", anywhere, 6, second, pieces)
    return (new_cpoint, new_fpoint)


def solution(mesh):
    in_specs = (P(("grp", "tm"), None, None, "row"), P(("grp", "tm"), None), P(), P(), P(), P())
    out_specs = (P(("grp", "tm"), None, None, "row"), P(("grp", "tm"), None, None, "row"))
    return jax.shard_map(
        on_device, mesh=mesh, in_specs=in_specs, out_specs=out_specs, check_vma=False
    )
```

```python
import functools

import jax
import jax.numpy as jnp
from jax import lax
from jax.experimental import pallas as pl
from jax.experimental.pallas import tpu as pltpu
from jax.sharding import PartitionSpec as P

time_step = 0.2
F32 = jnp.float32
BF16 = jnp.bfloat16


def shifted_down(block, axis):
    route = [(i, i - 1) for i in range(1, lax.axis_size(axis))]
    return lax.ppermute(block, axis, route)


def group_of(layers_j, size):
    return max(256 // (layers_j * size), 1)


def table_kernel(which, ham_cols, jump_cols, controls, controls_next, ham, jump, rows, jump_row, *tables):
    layers_h, count = ham_cols.shape
    layers_j = jump_cols.shape[0]
    size = ham.shape[-1]
    crossed = [(k, other) for k in range(layers_j) for other in range(layers_j) if k != other]
    group = jump_row.shape[1] // size
    first_k = 2 * layers_h
    first_j = first_k + 1 + len(crossed)

    @pl.loop(0, count)
    def _(b):
        for k in range(layers_h):
            rows[k, b] = ham_cols[k, b] * size
            rows[layers_h + k, ham_cols[k, b]] = b * size
        for k in range(layers_j):
            rows[first_j + k, jump_cols[k, b]] = b * size

    @pl.loop(0, count, unroll=8)
    def _(c):
        came_h = [rows[layers_h + k, c] // size for k in range(layers_h)]
        came_j = [rows[first_j + k, c] // size for k in range(layers_j)]
        rows[first_k, c] = c * size
        for at, (k, other) in enumerate(crossed):
            rows[first_k + 1 + at, c] = jump_cols[other, came_j[k]] * size

        def ham_row(term):
            parts = [ham[term, c, k].astype(F32) for k in range(layers_h)]
            parts += [ham[term, came_h[k], k].astype(F32).T for k in range(layers_h)]
            return jnp.concatenate(parts, axis=1)

        turned = [jump[came_j[k], k].astype(F32).T.astype(BF16) for k in range(layers_j)]
        jump_row[c // group, pl.ds(c % group * size, size), :] = jnp.concatenate(
            [jnp.where(c % group == v, piece, jnp.zeros_like(piece)) for v in range(group) for piece in turned], axis=1
        )
        square = sum(
            jnp.dot(turned[k], jump[came_j[k], k], preferred_element_type=F32) for k in range(layers_j)
        )
        blocks = [square] + [
            jnp.dot(turned[k], jump[came_j[k], other], preferred_element_type=F32) for k, other in crossed
        ]
        decay = -0.5 * jnp.concatenate(blocks, axis=1)
        drift, steer = ham_row(0), ham_row(1)
        for at, (later, fine) in enumerate(which):
            amplitude = (controls, controls_next)[later][0, fine]
            coeffs = drift + amplitude * steer
            tables[2 * at][c] = jnp.concatenate([coeffs, decay], axis=1).astype(BF16)
            tables[2 * at + 1][c] = jnp.concatenate([-coeffs, decay], axis=1).astype(BF16)


def operator_tables(which, ham_blocks, ham_cols, jump_blocks, jump_cols, controls, controls_next):
    layers_h, count = ham_cols.shape
    layers_j = jump_cols.shape[0]
    size = ham_blocks.shape[-1]
    layers_k = 1 + layers_j * (layers_j - 1)
    smem = pl.BlockSpec(memory_space=pltpu.SMEM)
    vmem = pl.BlockSpec(memory_space=pltpu.VMEM)
    table = jax.ShapeDtypeStruct((count, size, (2 * layers_h + layers_k) * size), BF16)
    number = len(which)
    group = group_of(layers_j, size)
    rows, jump_row, *tables = pl.pallas_call(
        functools.partial(table_kernel, which),
        out_shape=[
            jax.ShapeDtypeStruct((2 * layers_h + layers_k + layers_j, count), jnp.int32),
            jax.ShapeDtypeStruct((count // group, group * size, group * layers_j * size), BF16),
        ] + [table] * (2 * number),
        in_specs=[smem, smem, smem, smem, vmem, vmem],
        out_specs=[smem, vmem] + [vmem] * (2 * number),
        compiler_params=pltpu.CompilerParams(vmem_limit_bytes=60 * 2**20),
        cost_estimate=pl.CostEstimate(flops=1, bytes_accessed=1, transcendentals=0),
        name="operator_tables",
    )(ham_cols, jump_cols, controls, controls_next, ham_blocks, jump_blocks)
    return (2 * layers_h, layers_k, layers_j), rows, jump_row, tables[0::2], tables[1::2]


class Step:
    def __init__(self, rows, counts, size, plus, minus, jump):
        self.rows, self.counts, self.size = rows, counts, size
        self.plus, self.minus, self.jump = plus, minus, jump
        self.group = jump.shape[1] // size

    def take(self, ref, kind, c, cols):
        first = sum(self.counts[:kind])
        return [
            ref[pl.ds(pl.multiple_of(self.rows[first + k, c], self.size), self.size), cols]
            for k in range(self.counts[kind])
        ]

    def ham(self, table, c, ham_ref, decay_ref, cols):
        met = jnp.concatenate(self.take(ham_ref, 0, c, cols) + self.take(decay_ref, 1, c, cols), axis=0)
        return jnp.dot(table[c], met, preferred_element_type=F32)

    def pull(self, q, ref, cols):
        met = jnp.concatenate(sum((self.take(ref, 2, q * self.group + v, cols) for v in range(self.group)), []), axis=0)
        return jnp.dot(self.jump[q], met, preferred_element_type=F32)

    def flat(self, kind, table, q, cols, *refs):
        if kind == "pull":
            return [self.pull(q, *refs, cols)]
        return [self.ham(table, q * self.group + v, *refs, cols) for v in range(self.group)]


def turn_whole(source, target, tile):
    n = source.shape[0] // tile

    @pl.loop(0, n)
    def _(i):
        near = pl.ds(pl.multiple_of(i * tile, tile), tile)
        for j in range(n):
            far = pl.ds(j * tile, tile)
            target[far, near] = source[near, far].T


def load_all(copies, sems):
    copies = [pltpu.make_async_copy(source, target, sems.at[k]) for k, (source, target) in enumerate(copies)]
    for copy in copies:
        copy.start()
    for copy in copies:
        copy.wait()


def part_of(first, k, tile):
    return pl.ds(pl.multiple_of(first + k * tile, tile), tile)


def assemble_first(place, near, near_pair, far, far_pair, c_ref, d_ref, stage, other, sems, tile):
    half, width = far.shape
    here, there = place[2], half - place[2]
    own, pair = place[3], width - place[3]

    def cols(first):
        return pl.ds(pl.multiple_of(first, width), width)

    copies = [
        (far, other.at[pl.ds(0, half), cols(own)]),
        (far_pair, other.at[pl.ds(0, half), cols(pair)]),
    ]
    for k in range(2):
        copies.append((near.at[0, k], stage.at[:, cols(k * half + own)]))
        copies.append((near_pair.at[0, k], stage.at[:, cols(k * half + pair)]))
    load_all(copies, sems)

    def mixed(rows, j):
        real = stage[rows, pl.ds(j * tile, tile)].astype(F32)
        imag = stage[rows, pl.ds(half + j * tile, tile)].astype(F32)
        return (real + imag).astype(BF16), (real - imag).astype(BF16)

    @pl.loop(0, half // tile)
    def _(i):
        here_i, there_i = part_of(here, i, tile), part_of(there, i, tile)
        for j in range(half // tile):
            here_j, there_j = part_of(here, j, tile), part_of(there, j, tile)
            total, less = mixed(there_i, j)
            c_ref[there_i, here_j] = total
            d_ref[there_i, here_j] = less
            c_ref[here_j, there_i] = less.T
            d_ref[here_j, there_i] = total.T
            block = other[part_of(0, i, tile), pl.ds(j * tile, tile)]
            c_ref[there_i, there_j] = block
            d_ref[there_j, there_i] = block.T
            total, less = mixed(here_i, j)
            c_ref[here_i, here_j] = total
            d_ref[here_i, here_j] = less


def assemble_next(place, pieces, c_ref, d_ref, stage, other, sems, tile):
    half, width = pieces[0].shape
    here, there = place[2], half - place[2]
    copies = []
    for (near, apart, far), core in ((pieces[:3], place[3]), (pieces[3:], width - place[3])):
        low = pl.ds(pl.multiple_of(core, width), width)
        high = pl.ds(pl.multiple_of(half + core, width), width)
        rows = pl.ds(0, half)
        copies += [(near, other.at[rows, low]), (far, other.at[rows, high])]
        copies += [(apart.at[0], stage.at[rows, low]), (apart.at[1], stage.at[rows, high])]
    load_all(copies, sems)

    @pl.loop(0, half // tile)
    def _(i):
        rows = part_of(0, i, tile)
        here_i, there_i = part_of(here, i, tile), part_of(there, i, tile)
        for j in range(half // tile):
            here_j, there_j = part_of(here, j, tile), part_of(there, j, tile)
            real = stage[rows, pl.ds(j * tile, tile)].astype(F32)
            imag = stage[rows, pl.ds(half + j * tile, tile)].astype(F32)
            total, less = (real + imag).astype(BF16), (real - imag).astype(BF16)
            c_ref[there_i, here_j] = total
            d_ref[there_i, here_j] = less
            c_ref[here_j, there_i] = less.T
            d_ref[here_j, there_i] = total.T
            block = other[rows, pl.ds(j * tile, tile)]
            c_ref[here_i, here_j] = block
            d_ref[here_j, here_i] = block.T
            block = other[rows, pl.ds(half + j * tile, tile)]
            c_ref[there_i, there_j] = block
            d_ref[there_j, there_i] = block.T


def put_turned(step, target, cols, to, first, count, kind, table, *refs):
    rows = sum((step.flat(kind, table, first + v, cols, *refs) for v in range(count)), [])
    target[cols, to] = jnp.concatenate([piece.astype(BF16) for piece in rows], axis=0).T


def whole_step(step, c_ref, d_ref, r_ref, x_ref, c_new, d_new, tile):
    n = c_ref.shape[0]
    size = step.size
    count = tile // (step.group * size)

    @pl.loop(0, n // tile)
    def _(g):
        to = part_of(0, g, tile)

        @pl.loop(0, n // tile, unroll=2)
        def _(s):
            cols = part_of(0, s, tile)
            put_turned(step, r_ref, cols, to, g * count, count, "ham", step.minus, c_ref, d_ref)
            put_turned(step, x_ref, cols, to, g * count, count, "pull", None, d_ref)

    @pl.loop(0, n // tile)
    def _(g):
        @pl.loop(0, n // tile, unroll=2)
        def _(s):
            cols = part_of(0, s, tile)
            made = []
            for q in range(count):
                pulled = step.pull(g * count + q, x_ref, cols)
                for v in range(step.group):
                    c = (g * count + q) * step.group + v
                    own = pl.ds(pl.multiple_of(c * size, size), size)
                    change = step.ham(step.plus, c, d_ref, c_ref, cols) + pulled[v * size : (v + 1) * size]
                    change = change + r_ref[own, cols].astype(F32)
                    made.append((c_ref[own, cols].astype(F32) + time_step * change).astype(BF16))
                    c_new[own, cols] = made[-1]
            d_new[cols, part_of(0, g, tile)] = jnp.concatenate(made, axis=0).T


def own_step(step, start, width, c_ref, d_ref, turned, tile, base, out):
    n = c_ref.shape[0]
    part = min(tile, width)
    size = step.size
    deep = step.group * size
    count = part // deep
    kinds = (
        ("ham", step.minus, c_ref, d_ref),
        ("ham", step.plus, d_ref, c_ref),
        ("pull", None, d_ref),
        ("pull", None, c_ref),
    )

    @pl.loop(0, width // part)
    def _(g):
        @pl.loop(0, n // tile)
        def _(s):
            for k, kind in enumerate(kinds):
                to = part_of(k * width, g, part)
                put_turned(step, turned, part_of(0, s, tile), to, start // deep + g * count, count, *kind)

    @pl.loop(0, n // deep)
    def _(q):
        for s in range(width // part):
            cols = pl.ds(pl.multiple_of(start + s * part, part), part)
            to = pl.ds(s * part, part)
            of = [pl.ds(k * width + s * part, part) for k in range(4)]
            pulled = [step.pull(q, turned, of[k]) for k in (2, 3)]
            for v in range(step.group):
                c = q * step.group + v
                own = pl.ds(pl.multiple_of(c * size, size), size)
                here = slice(v * size, (v + 1) * size)
                change = step.ham(step.plus, c, d_ref, c_ref, cols) + pulled[0][here]
                second = step.ham(step.minus, c, c_ref, d_ref, cols) + pulled[1][here]
                change = change + turned[own, of[0]].astype(F32)
                second = second + turned[own, of[1]].astype(F32)
                real, imag = base(own, cols, to)
                out[0, 0, own, to] = (real + 0.5 * time_step * (change + second)).astype(BF16)
                out[0, 1, own, to] = (imag + 0.5 * time_step * (change - second)).astype(BF16)


def fill_whole(piece, c_ref, d_ref, sems, tile):
    load_all([(piece, c_ref)], sems)
    turn_whole(c_ref, d_ref, tile)


def inner_kernel(counts, tile, number, rows, place, terminal, plus, minus, jump, *refs):
    pieces, refs = refs[:number], refs[number:]
    out, c_ref, d_ref, stage, turned, sems = refs
    if number == 1:
        fill_whole(pieces[0], c_ref, d_ref, sems, tile)
    else:
        assemble_first(place, *pieces, c_ref, d_ref, stage, turned, sems, tile)
    step = Step(rows, counts, plus.shape[1], plus, minus, jump)

    def base(own, _, cols):
        return terminal[0, 0, own, cols].astype(F32), terminal[0, 1, own, cols].astype(F32)

    own_step(step, place[0], out.shape[3], c_ref, d_ref, turned, tile, base, out)


def start_kernel(counts, tile, number, rows, place, terminal, plus, minus, jump, plus_two, minus_two, *refs):
    pieces, refs = refs[:number], refs[number:]
    out, c_ref, d_ref, r_ref, x_ref, c_new, d_new, sems = refs
    size = plus.shape[1]

    @pl.when(place[1] == 1)
    def _():
        load_all([(terminal, out)], sems)

    @pl.when(place[1] == 0)
    def _():
        if number == 1:
            fill_whole(pieces[0], c_ref, d_ref, sems, tile)
        else:
            assemble_next(place, pieces, c_ref, d_ref, r_ref, x_ref, sems, tile)
        whole_step(Step(rows, counts, size, plus, minus, jump), c_ref, d_ref, r_ref, x_ref, c_new, d_new, tile)

        def base(own, cols, _):
            first, second = c_new[own, cols].astype(F32), d_new[own, cols].astype(F32)
            return 0.5 * (first + second), 0.5 * (first - second)

        step = Step(rows, counts, size, plus_two, minus_two, jump)
        own_step(step, place[0], out.shape[3], c_new, d_new, r_ref, tile, base, out)


def swapped(block, bit):
    return lax.ppermute(block, "row", [(i, i ^ bit) for i in range(lax.axis_size("row"))])


def on_device(terminal, controls, ham_blocks, ham_cols, jump_blocks, jump_cols):
    n, width = terminal.shape[2], terminal.shape[3]
    tile = 256
    row = lax.axis_index("row")
    here = row // 2 * 2 * width
    controls_next = shifted_down(controls, "tm")
    is_last = lax.axis_index("tm") == lax.axis_size("tm") - 1
    place = jnp.stack([row * width, is_last.astype(jnp.int32), here, row % 2 * width]).astype(jnp.int32)
    operators = (ham_blocks, ham_cols, jump_blocks, jump_cols)
    which = ((0, 1), (1, 1), (1, 0))
    counts, rows, jump_row, plus, minus = operator_tables(which, *operators, controls, controls_next)

    smem = pl.BlockSpec(memory_space=pltpu.SMEM)
    vmem = pl.BlockSpec(memory_space=pltpu.VMEM)
    anywhere = pl.BlockSpec(memory_space=pl.ANY)
    square = pltpu.VMEM((n, n), BF16)

    def step_call(kernel, name, state_spec, squares, tables, pieces):
        return pl.pallas_call(
            functools.partial(kernel, counts, tile, len(pieces)),
            out_shape=jax.ShapeDtypeStruct(terminal.shape, BF16),
            in_specs=[smem, smem, state_spec] + [vmem] * len(tables) + [anywhere] * len(pieces),
            out_specs=vmem,
            scratch_shapes=[square] * squares + [pltpu.SemaphoreType.DMA((8,))],
            compiler_params=pltpu.CompilerParams(vmem_limit_bytes=60 * 2**20),
            cost_estimate=pl.CostEstimate(flops=1, bytes_accessed=1, transcendentals=0),
            name=name,
        )(rows, place, terminal, *tables, *pieces)

    first = [plus[0], minus[0], jump_row]
    second = [plus[1], minus[1], jump_row, plus[2], minus[2]]
    if lax.axis_size("row") == 4:
        near_pair = swapped(terminal, 1)
        size = (1, 1, 2 * width, width)
        mine = [lax.dynamic_slice(terminal, (0, k, here, 0), size)[0, 0].astype(F32) for k in range(2)]
        mixed = (mine[0] + mine[1]).astype(BF16)
        far = swapped(mixed, 2)
        mixed, _ = lax.optimization_barrier((mixed, controls_next))
        mixed = shifted_down(mixed, "tm")
        apart = lax.dynamic_slice(terminal, (0, 0, 2 * width - here, 0), (1, 2, 2 * width, width))[0]
        apart = shifted_down(apart, "tm")
        far, rows = lax.optimization_barrier((far, rows))
        far_pair = swapped(far, 1)
        rows, mixed = lax.optimization_barrier((rows, mixed))
        far_next = swapped(mixed, 2)
        new_fpoint = step_call(inner_kernel, "inner_point", vmem, 4, first, [terminal, near_pair, far, far_pair])
        mixed_pair = swapped(mixed, 1)
        apart, far_next, mixed_pair, new_fpoint = lax.optimization_barrier((apart, far_next, mixed_pair, new_fpoint))
        pieces = [mixed, apart, far_next, mixed_pair, swapped(apart, 1), swapped(far_next, 1)]
    else:
        mixed = (terminal[0, 0].astype(F32) + terminal[0, 1].astype(F32)).astype(BF16)

        def gathered(piece):
            return [lax.all_gather(piece, "row", axis=1, tiled=True)]

        new_fpoint = step_call(inner_kernel, "inner_point", vmem, 4, first, gathered(mixed))
        pieces = gathered(shifted_down(mixed, "tm"))
    new_cpoint = step_call(start_kernel, "left_end", anywhere, 6, second, pieces)
    return (new_cpoint, new_fpoint)


def solution(mesh):
    in_specs = (P(("grp", "tm"), None, None, "row"), P(("grp", "tm"), None), P(), P(), P(), P())
    out_specs = (P(("grp", "tm"), None, None, "row"), P(("grp", "tm"), None, None, "row"))
    return jax.shard_map(
        on_device, mesh=mesh, in_specs=in_specs, out_specs=out_specs, check_vma=False
    )
```

```python
import functools

import jax
import jax.numpy as jnp
from jax import lax
from jax.experimental import pallas as pl
from jax.experimental.pallas import tpu as pltpu
from jax.sharding import PartitionSpec as P

time_step = 0.2
F32 = jnp.float32
BF16 = jnp.bfloat16


def shifted_down(block, axis):
    route = [(i, i - 1) for i in range(1, lax.axis_size(axis))]
    return lax.ppermute(block, axis, route)


def group_of(layers_j, size):
    return max(256 // (layers_j * size), 1)


def table_kernel(which, ham_cols, jump_cols, controls, controls_next, ham, jump, rows, jump_row, *tables):
    layers_h, count = ham_cols.shape
    layers_j = jump_cols.shape[0]
    size = ham.shape[-1]
    crossed = [(k, other) for k in range(layers_j) for other in range(layers_j) if k != other]
    group = jump_row.shape[1] // size
    first_k = 2 * layers_h
    first_j = first_k + 1 + len(crossed)

    @pl.loop(0, count)
    def _(b):
        for k in range(layers_h):
            rows[k, b] = ham_cols[k, b] * size
            rows[layers_h + k, ham_cols[k, b]] = b * size
        for k in range(layers_j):
            rows[first_j + k, jump_cols[k, b]] = b * size

    @pl.loop(0, count, unroll=8)
    def _(c):
        came_h = [rows[layers_h + k, c] // size for k in range(layers_h)]
        came_j = [rows[first_j + k, c] // size for k in range(layers_j)]
        rows[first_k, c] = c * size
        for at, (k, other) in enumerate(crossed):
            rows[first_k + 1 + at, c] = jump_cols[other, came_j[k]] * size

        def ham_row(term):
            parts = [ham[term, c, k].astype(F32) for k in range(layers_h)]
            parts += [ham[term, came_h[k], k].astype(F32).T for k in range(layers_h)]
            return jnp.concatenate(parts, axis=1)

        turned = [jump[came_j[k], k].astype(F32).T.astype(BF16) for k in range(layers_j)]
        jump_row[c // group, pl.ds(c % group * size, size), :] = jnp.concatenate(
            [jnp.where(c % group == v, piece, jnp.zeros_like(piece)) for v in range(group) for piece in turned], axis=1
        )
        square = sum(
            jnp.dot(turned[k], jump[came_j[k], k], preferred_element_type=F32) for k in range(layers_j)
        )
        blocks = [square] + [
            jnp.dot(turned[k], jump[came_j[k], other], preferred_element_type=F32) for k, other in crossed
        ]
        decay = -0.5 * jnp.concatenate(blocks, axis=1)
        drift, steer = ham_row(0), ham_row(1)
        for at, (later, fine) in enumerate(which):
            amplitude = (controls, controls_next)[later][0, fine]
            coeffs = drift + amplitude * steer
            tables[2 * at][c] = jnp.concatenate([coeffs, decay], axis=1).astype(BF16)
            tables[2 * at + 1][c] = jnp.concatenate([-coeffs, decay], axis=1).astype(BF16)


def operator_tables(which, ham_blocks, ham_cols, jump_blocks, jump_cols, controls, controls_next):
    layers_h, count = ham_cols.shape
    layers_j = jump_cols.shape[0]
    size = ham_blocks.shape[-1]
    layers_k = 1 + layers_j * (layers_j - 1)
    smem = pl.BlockSpec(memory_space=pltpu.SMEM)
    vmem = pl.BlockSpec(memory_space=pltpu.VMEM)
    table = jax.ShapeDtypeStruct((count, size, (2 * layers_h + layers_k) * size), BF16)
    number = len(which)
    group = group_of(layers_j, size)
    rows, jump_row, *tables = pl.pallas_call(
        functools.partial(table_kernel, which),
        out_shape=[
            jax.ShapeDtypeStruct((2 * layers_h + layers_k + layers_j, count), jnp.int32),
            jax.ShapeDtypeStruct((count // group, group * size, group * layers_j * size), BF16),
        ] + [table] * (2 * number),
        in_specs=[smem, smem, smem, smem, vmem, vmem],
        out_specs=[smem, vmem] + [vmem] * (2 * number),
        compiler_params=pltpu.CompilerParams(vmem_limit_bytes=60 * 2**20),
        cost_estimate=pl.CostEstimate(flops=1, bytes_accessed=1, transcendentals=0),
        name="operator_tables",
    )(ham_cols, jump_cols, controls, controls_next, ham_blocks, jump_blocks)
    return (2 * layers_h, layers_k, layers_j), rows, jump_row, *tables


class Step:
    def __init__(self, rows, counts, size, plus, minus, jump):
        self.rows, self.counts, self.size = rows, counts, size
        self.plus, self.minus, self.jump = plus, minus, jump
        self.group = jump.shape[1] // size

    def take(self, ref, kind, c, cols):
        first = sum(self.counts[:kind])
        return [
            ref[pl.ds(pl.multiple_of(self.rows[first + k, c], self.size), self.size), cols]
            for k in range(self.counts[kind])
        ]

    def ham(self, table, c, ham_ref, decay_ref, cols):
        met = jnp.concatenate(self.take(ham_ref, 0, c, cols) + self.take(decay_ref, 1, c, cols), axis=0)
        return jnp.dot(table[c], met, preferred_element_type=F32)

    def pull(self, q, ref, cols):
        met = jnp.concatenate(sum((self.take(ref, 2, q * self.group + v, cols) for v in range(self.group)), []), axis=0)
        return jnp.dot(self.jump[q], met, preferred_element_type=F32)

    def flat(self, kind, table, q, cols, *refs):
        if kind == "pull":
            return [self.pull(q, *refs, cols)]
        return [self.ham(table, q * self.group + v, *refs, cols) for v in range(self.group)]


def turn_whole(source, target, tile):
    n = source.shape[0] // tile

    @pl.loop(0, n)
    def _(i):
        near = pl.ds(pl.multiple_of(i * tile, tile), tile)
        for j in range(n):
            far = pl.ds(j * tile, tile)
            target[far, near] = source[near, far].T


def load_all(copies, sems):
    copies = [pltpu.make_async_copy(source, target, sems.at[k]) for k, (source, target) in enumerate(copies)]
    for copy in copies:
        copy.start()
    for copy in copies:
        copy.wait()


def part_of(first, k, tile):
    return pl.ds(pl.multiple_of(first + k * tile, tile), tile)


def assemble_first(place, near, near_pair, far, far_pair, c_ref, d_ref, stage, other, sems, tile):
    half, width = far.shape
    here, there = place[2], half - place[2]
    own, pair = place[3], width - place[3]

    def cols(first):
        return pl.ds(pl.multiple_of(first, width), width)

    copies = [
        (far, other.at[pl.ds(0, half), cols(own)]),
        (far_pair, other.at[pl.ds(0, half), cols(pair)]),
    ]
    for k in range(2):
        copies.append((near.at[0, k], stage.at[:, cols(k * half + own)]))
        copies.append((near_pair.at[0, k], stage.at[:, cols(k * half + pair)]))
    load_all(copies, sems)

    def mixed(rows, j):
        real = stage[rows, pl.ds(j * tile, tile)].astype(F32)
        imag = stage[rows, pl.ds(half + j * tile, tile)].astype(F32)
        return (real + imag).astype(BF16), (real - imag).astype(BF16)

    @pl.loop(0, half // tile)
    def _(i):
        here_i, there_i = part_of(here, i, tile), part_of(there, i, tile)
        for j in range(half // tile):
            here_j, there_j = part_of(here, j, tile), part_of(there, j, tile)
            total, less = mixed(there_i, j)
            c_ref[there_i, here_j] = total
            d_ref[there_i, here_j] = less
            c_ref[here_j, there_i] = less.T
            d_ref[here_j, there_i] = total.T
            block = other[part_of(0, i, tile), pl.ds(j * tile, tile)]
            c_ref[there_i, there_j] = block
            d_ref[there_j, there_i] = block.T
            total, less = mixed(here_i, j)
            c_ref[here_i, here_j] = total
            d_ref[here_i, here_j] = less


def assemble_next(place, pieces, c_ref, d_ref, stage, other, sems, tile):
    half, width = pieces[0].shape
    here, there = place[2], half - place[2]
    copies = []
    for (near, apart, far), core in ((pieces[:3], place[3]), (pieces[3:], width - place[3])):
        low = pl.ds(pl.multiple_of(core, width), width)
        high = pl.ds(pl.multiple_of(half + core, width), width)
        rows = pl.ds(0, half)
        copies += [(near, other.at[rows, low]), (far, other.at[rows, high])]
        copies += [(apart.at[0], stage.at[rows, low]), (apart.at[1], stage.at[rows, high])]
    load_all(copies, sems)

    @pl.loop(0, half // tile)
    def _(i):
        rows = part_of(0, i, tile)
        here_i, there_i = part_of(here, i, tile), part_of(there, i, tile)
        for j in range(half // tile):
            here_j, there_j = part_of(here, j, tile), part_of(there, j, tile)
            real = stage[rows, pl.ds(j * tile, tile)].astype(F32)
            imag = stage[rows, pl.ds(half + j * tile, tile)].astype(F32)
            total, less = (real + imag).astype(BF16), (real - imag).astype(BF16)
            c_ref[there_i, here_j] = total
            d_ref[there_i, here_j] = less
            c_ref[here_j, there_i] = less.T
            d_ref[here_j, there_i] = total.T
            block = other[rows, pl.ds(j * tile, tile)]
            c_ref[here_i, here_j] = block
            d_ref[here_j, here_i] = block.T
            block = other[rows, pl.ds(half + j * tile, tile)]
            c_ref[there_i, there_j] = block
            d_ref[there_j, there_i] = block.T


def put_turned(step, target, cols, to, first, count, kind, table, *refs):
    rows = sum((step.flat(kind, table, first + v, cols, *refs) for v in range(count)), [])
    target[cols, to] = jnp.concatenate([piece.astype(BF16) for piece in rows], axis=0).T


def whole_step(step, c_ref, d_ref, r_ref, x_ref, c_new, d_new, tile):
    n = c_ref.shape[0]
    size = step.size
    count = tile // (step.group * size)

    @pl.loop(0, n // tile)
    def _(g):
        to = part_of(0, g, tile)

        @pl.loop(0, n // tile, unroll=2)
        def _(s):
            cols = part_of(0, s, tile)
            put_turned(step, r_ref, cols, to, g * count, count, "ham", step.minus, c_ref, d_ref)
            put_turned(step, x_ref, cols, to, g * count, count, "pull", None, d_ref)

    @pl.loop(0, n // tile)
    def _(g):
        @pl.loop(0, n // tile, unroll=2)
        def _(s):
            cols = part_of(0, s, tile)
            made = []
            for q in range(count):
                pulled = step.pull(g * count + q, x_ref, cols)
                for v in range(step.group):
                    c = (g * count + q) * step.group + v
                    own = pl.ds(pl.multiple_of(c * size, size), size)
                    change = step.ham(step.plus, c, d_ref, c_ref, cols) + pulled[v * size : (v + 1) * size]
                    change = change + r_ref[own, cols].astype(F32)
                    made.append((c_ref[own, cols].astype(F32) + time_step * change).astype(BF16))
                    c_new[own, cols] = made[-1]
            d_new[cols, part_of(0, g, tile)] = jnp.concatenate(made, axis=0).T


def own_step(step, start, width, c_ref, d_ref, turned, tile, base, out):
    n = c_ref.shape[0]
    part = min(tile, width)
    size = step.size
    deep = step.group * size
    count = part // deep
    kinds = (
        ("ham", step.minus, c_ref, d_ref),
        ("ham", step.plus, d_ref, c_ref),
        ("pull", None, d_ref),
        ("pull", None, c_ref),
    )

    @pl.loop(0, width // part)
    def _(g):
        @pl.loop(0, n // tile)
        def _(s):
            for k, kind in enumerate(kinds):
                to = part_of(k * width, g, part)
                put_turned(step, turned, part_of(0, s, tile), to, start // deep + g * count, count, *kind)

    @pl.loop(0, n // deep)
    def _(q):
        for s in range(width // part):
            cols = pl.ds(pl.multiple_of(start + s * part, part), part)
            to = pl.ds(s * part, part)
            of = [pl.ds(k * width + s * part, part) for k in range(4)]
            pulled = [step.pull(q, turned, of[k]) for k in (2, 3)]
            for v in range(step.group):
                c = q * step.group + v
                own = pl.ds(pl.multiple_of(c * size, size), size)
                here = slice(v * size, (v + 1) * size)
                change = step.ham(step.plus, c, d_ref, c_ref, cols) + pulled[0][here]
                second = step.ham(step.minus, c, c_ref, d_ref, cols) + pulled[1][here]
                change = change + turned[own, of[0]].astype(F32)
                second = second + turned[own, of[1]].astype(F32)
                real, imag = base(own, cols, to)
                out[0, 0, own, to] = (real + 0.5 * time_step * (change + second)).astype(BF16)
                out[0, 1, own, to] = (imag + 0.5 * time_step * (change - second)).astype(BF16)


def fill_whole(piece, c_ref, d_ref, sems, tile):
    load_all([(piece, c_ref)], sems)
    turn_whole(c_ref, d_ref, tile)


def inner_kernel(counts, tile, number, rows, place, terminal, jump, plus, minus, *refs):
    pieces, refs = refs[:number], refs[number:]
    out, c_ref, d_ref, stage, turned, sems = refs
    n, width = out.shape[2], out.shape[3]
    if number == 1:
        fill_whole(pieces[0], c_ref, d_ref, sems, tile)
        load_all([(terminal.at[0, k], stage.at[:, pl.ds(k * width, width)]) for k in range(2)], sems)
        starts = (0, width)
    else:
        assemble_first(place, terminal, *pieces, c_ref, d_ref, stage, turned, sems, tile)
        starts = (place[3], place[3] + 2 * width)
    step = Step(rows, counts, plus.shape[1], plus, minus, jump)

    def base(own, _, cols):
        part = cols.size
        return [
            stage[own, pl.ds(pl.multiple_of(first + cols.start, part), part)].astype(F32) for first in starts
        ]

    own_step(step, place[0], width, c_ref, d_ref, turned, tile, base, out)


def start_kernel(counts, tile, number, rows, place, terminal, jump, plus, minus, plus_two, minus_two, *refs):
    pieces, refs = refs[:number], refs[number:]
    out, c_ref, d_ref, r_ref, x_ref, c_new, d_new, sems = refs
    size = plus.shape[1]

    @pl.when(place[1] == 1)
    def _():
        load_all([(terminal, out)], sems)

    @pl.when(place[1] == 0)
    def _():
        if number == 1:
            fill_whole(pieces[0], c_ref, d_ref, sems, tile)
        else:
            assemble_next(place, pieces, c_ref, d_ref, r_ref, x_ref, sems, tile)
        whole_step(Step(rows, counts, size, plus, minus, jump), c_ref, d_ref, r_ref, x_ref, c_new, d_new, tile)

        def base(own, cols, _):
            first, second = c_new[own, cols].astype(F32), d_new[own, cols].astype(F32)
            return 0.5 * (first + second), 0.5 * (first - second)

        step = Step(rows, counts, size, plus_two, minus_two, jump)
        own_step(step, place[0], out.shape[3], c_new, d_new, r_ref, tile, base, out)


def swapped(block, bit):
    return lax.ppermute(block, "row", [(i, i ^ bit) for i in range(lax.axis_size("row"))])


def on_device(terminal, controls, ham_blocks, ham_cols, jump_blocks, jump_cols):
    n, width = terminal.shape[2], terminal.shape[3]
    tile = 256
    row = lax.axis_index("row")
    here = row // 2 * 2 * width
    controls_next = shifted_down(controls, "tm")
    is_last = lax.axis_index("tm") == lax.axis_size("tm") - 1
    place = jnp.stack([row * width, is_last.astype(jnp.int32), here, row % 2 * width]).astype(jnp.int32)
    operators = (ham_blocks, ham_cols, jump_blocks, jump_cols)
    counts, rows, *first = operator_tables(((0, 1),), *operators, controls, controls)

    smem = pl.BlockSpec(memory_space=pltpu.SMEM)
    vmem = pl.BlockSpec(memory_space=pltpu.VMEM)
    anywhere = pl.BlockSpec(memory_space=pl.ANY)
    square = pltpu.VMEM((n, n), BF16)

    def step_call(kernel, name, squares, rows, tables, pieces):
        return pl.pallas_call(
            functools.partial(kernel, counts, tile, len(pieces)),
            out_shape=jax.ShapeDtypeStruct(terminal.shape, BF16),
            in_specs=[smem, smem, anywhere] + [vmem] * len(tables) + [anywhere] * len(pieces),
            out_specs=vmem,
            scratch_shapes=[square] * squares + [pltpu.SemaphoreType.DMA((8,))],
            compiler_params=pltpu.CompilerParams(vmem_limit_bytes=60 * 2**20),
            cost_estimate=pl.CostEstimate(flops=1, bytes_accessed=1, transcendentals=0),
            name=name,
        )(rows, place, terminal, *tables, *pieces)


    def second_tables(controls_next, after):
        later, _ = lax.optimization_barrier((controls_next, after))
        return operator_tables(((1, 1), (1, 0)), *operators, controls, later)[1:]

    if lax.axis_size("row") == 4:
        near_pair = swapped(terminal, 1)
        size = (1, 1, 2 * width, width)
        mine = [lax.dynamic_slice(terminal, (0, k, here, 0), size)[0, 0].astype(F32) for k in range(2)]
        mixed = (mine[0] + mine[1]).astype(BF16)
        mixed, controls_next = lax.optimization_barrier((mixed, controls_next))
        far = swapped(mixed, 2)
        mixed = shifted_down(mixed, "tm")
        apart = lax.dynamic_slice(terminal, (0, 0, 2 * width - here, 0), (1, 2, 2 * width, width))[0]
        apart = shifted_down(apart, "tm")
        far, rows = lax.optimization_barrier((far, rows))
        far_pair = swapped(far, 1)
        rows, mixed = lax.optimization_barrier((rows, mixed))
        far_next = swapped(mixed, 2)
        new_fpoint = step_call(inner_kernel, "inner_point", 4, rows, first, [near_pair, far, far_pair])
        mixed_pair = swapped(mixed, 1)
        apart, far_next, mixed_pair, new_fpoint = lax.optimization_barrier((apart, far_next, mixed_pair, new_fpoint))
        pieces = [mixed, apart, far_next, mixed_pair, swapped(apart, 1), swapped(far_next, 1)]
    else:
        mixed = (terminal[0, 0].astype(F32) + terminal[0, 1].astype(F32)).astype(BF16)

        def gathered(piece):
            return [lax.all_gather(piece, "row", axis=1, tiled=True)]

        new_fpoint = step_call(inner_kernel, "inner_point", 4, rows, first, gathered(mixed))
        pieces = gathered(shifted_down(mixed, "tm"))
    rows, *second = second_tables(controls_next, new_fpoint)
    new_cpoint = step_call(start_kernel, "left_end", 6, rows, second, pieces)
    return (new_cpoint, new_fpoint)


def solution(mesh):
    in_specs = (P(("grp", "tm"), None, None, "row"), P(("grp", "tm"), None), P(), P(), P(), P())
    out_specs = (P(("grp", "tm"), None, None, "row"), P(("grp", "tm"), None, None, "row"))
    return jax.shard_map(
        on_device, mesh=mesh, in_specs=in_specs, out_specs=out_specs, check_vma=False
    )
```

```python
import functools

import jax
import jax.numpy as jnp
from jax import lax
from jax.experimental import pallas as pl
from jax.experimental.pallas import tpu as pltpu
from jax.sharding import PartitionSpec as P

time_step = 0.2
F32 = jnp.float32
BF16 = jnp.bfloat16


def shifted_down(block, axis):
    route = [(i, i - 1) for i in range(1, lax.axis_size(axis))]
    return lax.ppermute(block, axis, route)


def group_of(layers_j, size):
    return max(256 // (layers_j * size), 1)


def table_kernel(which, ham_cols, jump_cols, controls, controls_next, ham, jump, rows, jump_row, *tables):
    layers_h, count = ham_cols.shape
    layers_j = jump_cols.shape[0]
    size = ham.shape[-1]
    crossed = [(k, other) for k in range(layers_j) for other in range(layers_j) if k != other]
    group = jump_row.shape[1] // size
    first_k = 2 * layers_h
    first_j = first_k + 1 + len(crossed)

    @pl.loop(0, count)
    def _(b):
        for k in range(layers_h):
            rows[k, b] = ham_cols[k, b] * size
            rows[layers_h + k, ham_cols[k, b]] = b * size
        for k in range(layers_j):
            rows[first_j + k, jump_cols[k, b]] = b * size

    @pl.loop(0, count, unroll=8)
    def _(c):
        came_h = [rows[layers_h + k, c] // size for k in range(layers_h)]
        came_j = [rows[first_j + k, c] // size for k in range(layers_j)]
        rows[first_k, c] = c * size
        for at, (k, other) in enumerate(crossed):
            rows[first_k + 1 + at, c] = jump_cols[other, came_j[k]] * size

        def ham_row(term):
            parts = [ham[term, c, k].astype(F32) for k in range(layers_h)]
            parts += [ham[term, came_h[k], k].astype(F32).T for k in range(layers_h)]
            return jnp.concatenate(parts, axis=1)

        turned = [jump[came_j[k], k].astype(F32).T.astype(BF16) for k in range(layers_j)]
        jump_row[c // group, pl.ds(c % group * size, size), :] = jnp.concatenate(
            [jnp.where(c % group == v, piece, jnp.zeros_like(piece)) for v in range(group) for piece in turned], axis=1
        )
        square = sum(
            jnp.dot(turned[k], jump[came_j[k], k], preferred_element_type=F32) for k in range(layers_j)
        )
        blocks = [square] + [
            jnp.dot(turned[k], jump[came_j[k], other], preferred_element_type=F32) for k, other in crossed
        ]
        decay = -0.5 * jnp.concatenate(blocks, axis=1)
        drift, steer = ham_row(0), ham_row(1)
        for at, (later, fine) in enumerate(which):
            amplitude = (controls, controls_next)[later][0, fine]
            coeffs = drift + amplitude * steer
            tables[2 * at][c] = jnp.concatenate([coeffs, decay], axis=1).astype(BF16)
            tables[2 * at + 1][c] = jnp.concatenate([-coeffs, decay], axis=1).astype(BF16)


def operator_tables(which, ham_blocks, ham_cols, jump_blocks, jump_cols, controls, controls_next):
    layers_h, count = ham_cols.shape
    layers_j = jump_cols.shape[0]
    size = ham_blocks.shape[-1]
    layers_k = 1 + layers_j * (layers_j - 1)
    smem = pl.BlockSpec(memory_space=pltpu.SMEM)
    vmem = pl.BlockSpec(memory_space=pltpu.VMEM)
    table = jax.ShapeDtypeStruct((count, size, (2 * layers_h + layers_k) * size), BF16)
    number = len(which)
    group = group_of(layers_j, size)
    rows, jump_row, *tables = pl.pallas_call(
        functools.partial(table_kernel, which),
        out_shape=[
            jax.ShapeDtypeStruct((2 * layers_h + layers_k + layers_j, count), jnp.int32),
            jax.ShapeDtypeStruct((count // group, group * size, group * layers_j * size), BF16),
        ] + [table] * (2 * number),
        in_specs=[smem, smem, smem, smem, vmem, vmem],
        out_specs=[smem, vmem] + [vmem] * (2 * number),
        compiler_params=pltpu.CompilerParams(vmem_limit_bytes=60 * 2**20),
        cost_estimate=pl.CostEstimate(flops=1, bytes_accessed=1, transcendentals=0),
        name="operator_tables",
    )(ham_cols, jump_cols, controls, controls_next, ham_blocks, jump_blocks)
    return (2 * layers_h, layers_k, layers_j), rows, jump_row, *tables


class Step:
    def __init__(self, rows, counts, size, plus, minus, jump):
        self.rows, self.counts, self.size = rows, counts, size
        self.plus, self.minus, self.jump = plus, minus, jump
        self.group = jump.shape[1] // size

    def take(self, ref, kind, c, cols):
        first = sum(self.counts[:kind])
        return [
            ref[pl.ds(pl.multiple_of(self.rows[first + k, c], self.size), self.size), cols]
            for k in range(self.counts[kind])
        ]

    def ham(self, table, c, ham_ref, decay_ref, cols):
        met = jnp.concatenate(self.take(ham_ref, 0, c, cols) + self.take(decay_ref, 1, c, cols), axis=0)
        return jnp.dot(table[c], met, preferred_element_type=F32)

    def pull(self, q, ref, cols):
        met = jnp.concatenate(sum((self.take(ref, 2, q * self.group + v, cols) for v in range(self.group)), []), axis=0)
        return jnp.dot(self.jump[q], met, preferred_element_type=F32)

    def flat(self, kind, table, q, cols, *refs):
        if kind == "pull":
            return [self.pull(q, *refs, cols)]
        return [self.ham(table, q * self.group + v, *refs, cols) for v in range(self.group)]


def turn_whole(source, target, tile):
    n = source.shape[0] // tile

    @pl.loop(0, n)
    def _(i):
        near = pl.ds(pl.multiple_of(i * tile, tile), tile)
        for j in range(n):
            far = pl.ds(j * tile, tile)
            target[far, near] = source[near, far].T


def load_all(copies, sems):
    copies = [pltpu.make_async_copy(source, target, sems.at[k]) for k, (source, target) in enumerate(copies)]
    for copy in copies:
        copy.start()
    for copy in copies:
        copy.wait()


def part_of(first, k, tile):
    return pl.ds(pl.multiple_of(first + k * tile, tile), tile)


def assemble_first(place, near, near_pair, far, far_pair, c_ref, d_ref, stage, other, sems, tile):
    half, width = far.shape
    here, there = place[2], half - place[2]
    own, pair = place[3], width - place[3]

    def cols(first):
        return pl.ds(pl.multiple_of(first, width), width)

    copies = [
        (far, other.at[pl.ds(0, half), cols(own)]),
        (far_pair, other.at[pl.ds(0, half), cols(pair)]),
    ]
    for k in range(2):
        copies.append((near.at[0, k], stage.at[:, cols(k * half + own)]))
        copies.append((near_pair.at[0, k], stage.at[:, cols(k * half + pair)]))
    load_all(copies, sems)

    def mixed(rows, j):
        real = stage[rows, pl.ds(j * tile, tile)].astype(F32)
        imag = stage[rows, pl.ds(half + j * tile, tile)].astype(F32)
        return (real + imag).astype(BF16), (real - imag).astype(BF16)

    @pl.loop(0, half // tile)
    def _(i):
        here_i, there_i = part_of(here, i, tile), part_of(there, i, tile)
        for j in range(half // tile):
            here_j, there_j = part_of(here, j, tile), part_of(there, j, tile)
            total, less = mixed(there_i, j)
            c_ref[there_i, here_j] = total
            d_ref[there_i, here_j] = less
            c_ref[here_j, there_i] = less.T
            d_ref[here_j, there_i] = total.T
            block = other[part_of(0, i, tile), pl.ds(j * tile, tile)]
            c_ref[there_i, there_j] = block
            d_ref[there_j, there_i] = block.T
            total, less = mixed(here_i, j)
            c_ref[here_i, here_j] = total
            d_ref[here_i, here_j] = less


def assemble_next(place, pieces, c_ref, d_ref, stage, other, sems, tile):
    half, width = pieces[0].shape
    here, there = place[2], half - place[2]
    copies = []
    for (near, upper, lower, far), core in ((pieces[:4], place[3]), (pieces[4:], width - place[3])):
        low = pl.ds(pl.multiple_of(core, width), width)
        high = pl.ds(pl.multiple_of(half + core, width), width)
        rows = pl.ds(0, half)
        copies += [(near, other.at[rows, low]), (far, other.at[rows, high])]
        top = upper.shape[1]
        for k, to in enumerate((low, high)):
            copies.append((upper.at[k], stage.at[pl.ds(0, top), to]))
            copies.append((lower.at[k], stage.at[pl.ds(top, half - top), to]))
    load_all(copies, sems)

    @pl.loop(0, half // tile)
    def _(i):
        rows = part_of(0, i, tile)
        here_i, there_i = part_of(here, i, tile), part_of(there, i, tile)
        for j in range(half // tile):
            here_j, there_j = part_of(here, j, tile), part_of(there, j, tile)
            real = stage[rows, pl.ds(j * tile, tile)].astype(F32)
            imag = stage[rows, pl.ds(half + j * tile, tile)].astype(F32)
            total, less = (real + imag).astype(BF16), (real - imag).astype(BF16)
            c_ref[there_i, here_j] = total
            d_ref[there_i, here_j] = less
            c_ref[here_j, there_i] = less.T
            d_ref[here_j, there_i] = total.T
            block = other[rows, pl.ds(j * tile, tile)]
            c_ref[here_i, here_j] = block
            d_ref[here_j, here_i] = block.T
            block = other[rows, pl.ds(half + j * tile, tile)]
            c_ref[there_i, there_j] = block
            d_ref[there_j, there_i] = block.T


def put_turned(step, target, cols, to, first, count, kind, table, *refs):
    rows = sum((step.flat(kind, table, first + v, cols, *refs) for v in range(count)), [])
    target[cols, to] = jnp.concatenate([piece.astype(BF16) for piece in rows], axis=0).T


def whole_step(step, c_ref, d_ref, r_ref, x_ref, c_new, d_new, tile):
    n = c_ref.shape[0]
    size = step.size
    count = tile // (step.group * size)

    @pl.loop(0, n // tile)
    def _(g):
        to = part_of(0, g, tile)

        @pl.loop(0, n // tile, unroll=2)
        def _(s):
            cols = part_of(0, s, tile)
            put_turned(step, r_ref, cols, to, g * count, count, "ham", step.minus, c_ref, d_ref)
            put_turned(step, x_ref, cols, to, g * count, count, "pull", None, d_ref)

    @pl.loop(0, n // tile)
    def _(g):
        @pl.loop(0, n // tile, unroll=2)
        def _(s):
            cols = part_of(0, s, tile)
            made = []
            for q in range(count):
                pulled = step.pull(g * count + q, x_ref, cols)
                for v in range(step.group):
                    c = (g * count + q) * step.group + v
                    own = pl.ds(pl.multiple_of(c * size, size), size)
                    change = step.ham(step.plus, c, d_ref, c_ref, cols) + pulled[v * size : (v + 1) * size]
                    change = change + r_ref[own, cols].astype(F32)
                    made.append((c_ref[own, cols].astype(F32) + time_step * change).astype(BF16))
                    c_new[own, cols] = made[-1]
            d_new[cols, part_of(0, g, tile)] = jnp.concatenate(made, axis=0).T


def own_step(step, start, width, c_ref, d_ref, turned, tile, base, out):
    n = c_ref.shape[0]
    part = min(tile, width)
    size = step.size
    deep = step.group * size
    count = part // deep
    kinds = (
        ("ham", step.minus, c_ref, d_ref),
        ("ham", step.plus, d_ref, c_ref),
        ("pull", None, d_ref),
        ("pull", None, c_ref),
    )

    @pl.loop(0, width // part)
    def _(g):
        @pl.loop(0, n // tile)
        def _(s):
            for k, kind in enumerate(kinds):
                to = part_of(k * width, g, part)
                put_turned(step, turned, part_of(0, s, tile), to, start // deep + g * count, count, *kind)

    @pl.loop(0, n // deep)
    def _(q):
        for s in range(width // part):
            cols = pl.ds(pl.multiple_of(start + s * part, part), part)
            to = pl.ds(s * part, part)
            of = [pl.ds(k * width + s * part, part) for k in range(4)]
            pulled = [step.pull(q, turned, of[k]) for k in (2, 3)]
            for v in range(step.group):
                c = q * step.group + v
                own = pl.ds(pl.multiple_of(c * size, size), size)
                here = slice(v * size, (v + 1) * size)
                change = step.ham(step.plus, c, d_ref, c_ref, cols) + pulled[0][here]
                second = step.ham(step.minus, c, c_ref, d_ref, cols) + pulled[1][here]
                change = change + turned[own, of[0]].astype(F32)
                second = second + turned[own, of[1]].astype(F32)
                real, imag = base(own, cols, to)
                out[0, 0, own, to] = (real + 0.5 * time_step * (change + second)).astype(BF16)
                out[0, 1, own, to] = (imag + 0.5 * time_step * (change - second)).astype(BF16)


def fill_whole(piece, c_ref, d_ref, sems, tile):
    load_all([(piece, c_ref)], sems)
    turn_whole(c_ref, d_ref, tile)


def inner_kernel(counts, tile, number, rows, place, terminal, jump, plus, minus, *refs):
    pieces, refs = refs[:number], refs[number:]
    out, c_ref, d_ref, stage, turned, sems = refs
    n, width = out.shape[2], out.shape[3]
    if number == 1:
        fill_whole(pieces[0], c_ref, d_ref, sems, tile)
        load_all([(terminal.at[0, k], stage.at[:, pl.ds(k * width, width)]) for k in range(2)], sems)
        starts = (0, width)
    else:
        assemble_first(place, terminal, *pieces, c_ref, d_ref, stage, turned, sems, tile)
        starts = (place[3], place[3] + 2 * width)
    step = Step(rows, counts, plus.shape[1], plus, minus, jump)

    def base(own, _, cols):
        part = cols.size
        return [
            stage[own, pl.ds(pl.multiple_of(first + cols.start, part), part)].astype(F32) for first in starts
        ]

    own_step(step, place[0], width, c_ref, d_ref, turned, tile, base, out)


def start_kernel(counts, tile, number, rows, place, terminal, jump, plus, minus, plus_two, minus_two, *refs):
    pieces, refs = refs[:number], refs[number:]
    out, c_ref, d_ref, r_ref, x_ref, c_new, d_new, sems = refs
    size = plus.shape[1]

    @pl.when(place[1] == 1)
    def _():
        load_all([(terminal, out)], sems)

    @pl.when(place[1] == 0)
    def _():
        if number == 1:
            fill_whole(pieces[0], c_ref, d_ref, sems, tile)
        else:
            assemble_next(place, pieces, c_ref, d_ref, r_ref, x_ref, sems, tile)
        whole_step(Step(rows, counts, size, plus, minus, jump), c_ref, d_ref, r_ref, x_ref, c_new, d_new, tile)

        def base(own, cols, _):
            first, second = c_new[own, cols].astype(F32), d_new[own, cols].astype(F32)
            return 0.5 * (first + second), 0.5 * (first - second)

        step = Step(rows, counts, size, plus_two, minus_two, jump)
        own_step(step, place[0], out.shape[3], c_new, d_new, r_ref, tile, base, out)


def swapped(block, bit):
    return lax.ppermute(block, "row", [(i, i ^ bit) for i in range(lax.axis_size("row"))])


def on_device(terminal, controls, ham_blocks, ham_cols, jump_blocks, jump_cols):
    n, width = terminal.shape[2], terminal.shape[3]
    tile = 256
    row = lax.axis_index("row")
    here = row // 2 * 2 * width
    controls_next = shifted_down(controls, "tm")
    is_last = lax.axis_index("tm") == lax.axis_size("tm") - 1
    place = jnp.stack([row * width, is_last.astype(jnp.int32), here, row % 2 * width]).astype(jnp.int32)
    operators = (ham_blocks, ham_cols, jump_blocks, jump_cols)

    smem = pl.BlockSpec(memory_space=pltpu.SMEM)
    vmem = pl.BlockSpec(memory_space=pltpu.VMEM)
    anywhere = pl.BlockSpec(memory_space=pl.ANY)
    square = pltpu.VMEM((n, n), BF16)

    def step_call(kernel, name, squares, rows, tables, pieces):
        return pl.pallas_call(
            functools.partial(kernel, counts, tile, len(pieces)),
            out_shape=jax.ShapeDtypeStruct(terminal.shape, BF16),
            in_specs=[smem, smem, anywhere] + [vmem] * len(tables) + [anywhere] * len(pieces),
            out_specs=vmem,
            scratch_shapes=[square] * squares + [pltpu.SemaphoreType.DMA((12,))],
            compiler_params=pltpu.CompilerParams(vmem_limit_bytes=60 * 2**20),
            cost_estimate=pl.CostEstimate(flops=1, bytes_accessed=1, transcendentals=0),
            name=name,
        )(rows, place, terminal, *tables, *pieces)

    counts, rows, *tables = operator_tables(((0, 1), (1, 1), (1, 0)), *operators, controls, controls_next)
    first, second = tables[:3], tables[:1] + tables[3:]
    if lax.axis_size("row") == 4:
        near_pair = swapped(terminal, 1)
        size = (1, 1, 2 * width, width)
        mine = [lax.dynamic_slice(terminal, (0, k, here, 0), size)[0, 0].astype(F32) for k in range(2)]
        mixed = (mine[0] + mine[1]).astype(BF16)
        mixed, controls_next = lax.optimization_barrier((mixed, controls_next))
        far = swapped(mixed, 2)
        mixed = shifted_down(mixed, "tm")
        there = 2 * width - here
        top = 5 * width // 4
        upper = lax.dynamic_slice(terminal, (0, 0, there, 0), (1, 2, top, width))[0]
        lower = lax.dynamic_slice(terminal, (0, 0, there + top, 0), (1, 2, 2 * width - top, width))[0]
        upper, lower = shifted_down(upper, "tm"), shifted_down(lower, "tm")
        far, rows = lax.optimization_barrier((far, rows))
        far_pair = swapped(far, 1)
        rows, mixed = lax.optimization_barrier((rows, mixed))
        far_next = swapped(mixed, 2)
        new_fpoint = step_call(inner_kernel, "inner_point", 4, rows, first, [near_pair, far, far_pair])
        mixed_pair = swapped(mixed, 1)
        upper, far_next, mixed_pair, new_fpoint = lax.optimization_barrier((upper, far_next, mixed_pair, new_fpoint))
        pieces = [mixed, upper, lower, far_next]
        pieces += [mixed_pair] + [swapped(piece, 1) for piece in pieces[1:]]
    else:
        mixed = (terminal[0, 0].astype(F32) + terminal[0, 1].astype(F32)).astype(BF16)

        def gathered(piece):
            return [lax.all_gather(piece, "row", axis=1, tiled=True)]

        new_fpoint = step_call(inner_kernel, "inner_point", 4, rows, first, gathered(mixed))
        pieces = gathered(shifted_down(mixed, "tm"))
    new_cpoint = step_call(start_kernel, "left_end", 6, rows, second, pieces)
    return (new_cpoint, new_fpoint)


def solution(mesh):
    in_specs = (P(("grp", "tm"), None, None, "row"), P(("grp", "tm"), None), P(), P(), P(), P())
    out_specs = (P(("grp", "tm"), None, None, "row"), P(("grp", "tm"), None, None, "row"))
    return jax.shard_map(
        on_device, mesh=mesh, in_specs=in_specs, out_specs=out_specs, check_vma=False
    )
```

```python
import functools

import jax
import jax.numpy as jnp
from jax import lax
from jax.experimental import pallas as pl
from jax.experimental.pallas import tpu as pltpu
from jax.sharding import PartitionSpec as P

time_step = 0.2
F32 = jnp.float32
BF16 = jnp.bfloat16


def shifted_down(block, axis):
    route = [(i, i - 1) for i in range(1, lax.axis_size(axis))]
    return lax.ppermute(block, axis, route)


def group_of(layers_j, size):
    return max(256 // (layers_j * size), 1)


def table_kernel(which, ham_cols, jump_cols, controls, controls_next, ham, jump, rows, jump_row, *refs):
    layers_h, count = ham_cols.shape
    layers_j = jump_cols.shape[0]
    size = ham.shape[-1]
    crossed = [(k, other) for k in range(layers_j) for other in range(layers_j) if k != other]
    *tables, came = refs
    group = jump_row.shape[1] // size
    first_k = 2 * layers_h
    first_j = first_k + 1 + len(crossed)

    @pl.loop(0, count, unroll=4)
    def _(b):
        for k in range(layers_h):
            rows[k, b] = ham_cols[k, b] * size
            rows[layers_h + k, ham_cols[k, b]] = b * size
            came[k, ham_cols[k, b]] = b
        for k in range(layers_j):
            rows[first_j + k, jump_cols[k, b]] = b * size
            came[layers_h + k, jump_cols[k, b]] = b

    def block_row(q, v):
        c = q * group + v
        came_h = [came[k, c] for k in range(layers_h)]
        came_j = [came[layers_h + k, c] for k in range(layers_j)]
        rows[first_k, c] = c * size
        for at, (k, other) in enumerate(crossed):
            rows[first_k + 1 + at, c] = jump_cols[other, came_j[k]] * size

        def ham_row(term):
            parts = [ham[term, c, k].astype(F32) for k in range(layers_h)]
            parts += [ham[term, came_h[k], k].astype(F32).T for k in range(layers_h)]
            return jnp.concatenate(parts, axis=1)

        stored = [[jump[came_j[k], other] for other in range(layers_j)] for k in range(layers_j)]
        turned = [stored[k][k].astype(F32).T.astype(BF16) for k in range(layers_j)]
        empty = [jnp.zeros_like(piece) for piece in turned]
        jump_row[q, v * size : (v + 1) * size, :] = jnp.concatenate(empty * v + turned + empty * (group - 1 - v), axis=1)
        square = sum(jnp.dot(turned[k], stored[k][k], preferred_element_type=F32) for k in range(layers_j))
        blocks = [square] + [jnp.dot(turned[k], stored[k][other], preferred_element_type=F32) for k, other in crossed]
        decay = -0.5 * jnp.concatenate(blocks, axis=1)
        drift, steer = ham_row(0), ham_row(1)
        for at, (later, fine) in enumerate(which):
            amplitude = (controls, controls_next)[later][0, fine]
            coeffs = drift + amplitude * steer
            tables[2 * at][c] = jnp.concatenate([coeffs, decay], axis=1).astype(BF16)
            tables[2 * at + 1][c] = jnp.concatenate([-coeffs, decay], axis=1).astype(BF16)

    @pl.loop(0, count // group, unroll=2)
    def _(q):
        for v in range(group):
            block_row(q, v)


def operator_tables(which, ham_blocks, ham_cols, jump_blocks, jump_cols, controls, controls_next):
    layers_h, count = ham_cols.shape
    layers_j = jump_cols.shape[0]
    size = ham_blocks.shape[-1]
    layers_k = 1 + layers_j * (layers_j - 1)
    smem = pl.BlockSpec(memory_space=pltpu.SMEM)
    vmem = pl.BlockSpec(memory_space=pltpu.VMEM)
    table = jax.ShapeDtypeStruct((count, size, (2 * layers_h + layers_k) * size), BF16)
    number = len(which)
    group = group_of(layers_j, size)
    rows, jump_row, *tables = pl.pallas_call(
        functools.partial(table_kernel, which),
        out_shape=[
            jax.ShapeDtypeStruct((2 * layers_h + layers_k + layers_j, count), jnp.int32),
            jax.ShapeDtypeStruct((count // group, group * size, group * layers_j * size), BF16),
        ] + [table] * (2 * number),
        in_specs=[smem, smem, smem, smem, vmem, vmem],
        out_specs=[smem, vmem] + [vmem] * (2 * number),
        scratch_shapes=[pltpu.SMEM((layers_h + layers_j, count), jnp.int32)],
        compiler_params=pltpu.CompilerParams(vmem_limit_bytes=60 * 2**20),
        cost_estimate=pl.CostEstimate(flops=1, bytes_accessed=1, transcendentals=0),
        name="operator_tables",
    )(ham_cols, jump_cols, controls, controls_next, ham_blocks, jump_blocks)
    return (2 * layers_h, layers_k, layers_j), rows, jump_row, *tables


class Step:
    def __init__(self, rows, counts, size, plus, minus, jump):
        self.rows, self.counts, self.size = rows, counts, size
        self.plus, self.minus, self.jump = plus, minus, jump
        self.group = jump.shape[1] // size

    def take(self, ref, kind, c, cols):
        first = sum(self.counts[:kind])
        return [
            ref[pl.ds(pl.multiple_of(self.rows[first + k, c], self.size), self.size), cols]
            for k in range(self.counts[kind])
        ]

    def ham(self, table, c, ham_ref, decay_ref, cols):
        met = jnp.concatenate(self.take(ham_ref, 0, c, cols) + self.take(decay_ref, 1, c, cols), axis=0)
        return jnp.dot(table[c], met, preferred_element_type=F32)

    def pull(self, q, ref, cols):
        met = jnp.concatenate(sum((self.take(ref, 2, q * self.group + v, cols) for v in range(self.group)), []), axis=0)
        return jnp.dot(self.jump[q], met, preferred_element_type=F32)

    def flat(self, kind, table, q, cols, *refs):
        if kind == "pull":
            return [self.pull(q, *refs, cols)]
        return [self.ham(table, q * self.group + v, *refs, cols) for v in range(self.group)]


def turn_whole(source, target, tile):
    n = source.shape[0] // tile

    @pl.loop(0, n)
    def _(i):
        near = pl.ds(pl.multiple_of(i * tile, tile), tile)
        for j in range(n):
            far = pl.ds(j * tile, tile)
            target[far, near] = source[near, far].T


def load_all(copies, sems):
    copies = [pltpu.make_async_copy(source, target, sems.at[k]) for k, (source, target) in enumerate(copies)]
    for copy in copies:
        copy.start()
    for copy in copies:
        copy.wait()


def part_of(first, k, tile):
    return pl.ds(pl.multiple_of(first + k * tile, tile), tile)


def assemble_first(place, near, near_pair, far, far_pair, c_ref, d_ref, stage, other, sems, tile):
    half, width = far.shape
    here, there = place[2], half - place[2]
    own, pair = place[3], width - place[3]

    def cols(first):
        return pl.ds(pl.multiple_of(first, width), width)

    copies = [
        (far, other.at[pl.ds(0, half), cols(own)]),
        (far_pair, other.at[pl.ds(0, half), cols(pair)]),
    ]
    for k in range(2):
        copies.append((near.at[0, k], stage.at[:, cols(k * half + own)]))
        copies.append((near_pair.at[0, k], stage.at[:, cols(k * half + pair)]))
    load_all(copies, sems)

    def mixed(rows, j):
        real = stage[rows, pl.ds(j * tile, tile)].astype(F32)
        imag = stage[rows, pl.ds(half + j * tile, tile)].astype(F32)
        return (real + imag).astype(BF16), (real - imag).astype(BF16)

    @pl.loop(0, half // tile)
    def _(i):
        here_i, there_i = part_of(here, i, tile), part_of(there, i, tile)
        for j in range(half // tile):
            here_j, there_j = part_of(here, j, tile), part_of(there, j, tile)
            total, less = mixed(there_i, j)
            c_ref[there_i, here_j] = total
            d_ref[there_i, here_j] = less
            c_ref[here_j, there_i] = less.T
            d_ref[here_j, there_i] = total.T
            block = other[part_of(0, i, tile), pl.ds(j * tile, tile)]
            c_ref[there_i, there_j] = block
            d_ref[there_j, there_i] = block.T
            total, less = mixed(here_i, j)
            c_ref[here_i, here_j] = total
            d_ref[here_i, here_j] = less


def assemble_next(place, pieces, c_ref, d_ref, stage, other, sems, tile):
    half, width = pieces[0].shape
    here, there = place[2], half - place[2]
    copies = []
    for (near, upper, lower, far), core in ((pieces[:4], place[3]), (pieces[4:], width - place[3])):
        low = pl.ds(pl.multiple_of(core, width), width)
        high = pl.ds(pl.multiple_of(half + core, width), width)
        rows = pl.ds(0, half)
        copies += [(near, other.at[rows, low]), (far, other.at[rows, high])]
        top = upper.shape[1]
        for k, to in enumerate((low, high)):
            copies.append((upper.at[k], stage.at[pl.ds(0, top), to]))
            copies.append((lower.at[k], stage.at[pl.ds(top, half - top), to]))
    load_all(copies, sems)

    @pl.loop(0, half // tile)
    def _(i):
        rows = part_of(0, i, tile)
        here_i, there_i = part_of(here, i, tile), part_of(there, i, tile)
        for j in range(half // tile):
            here_j, there_j = part_of(here, j, tile), part_of(there, j, tile)
            real = stage[rows, pl.ds(j * tile, tile)].astype(F32)
            imag = stage[rows, pl.ds(half + j * tile, tile)].astype(F32)
            total, less = (real + imag).astype(BF16), (real - imag).astype(BF16)
            c_ref[there_i, here_j] = total
            d_ref[there_i, here_j] = less
            c_ref[here_j, there_i] = less.T
            d_ref[here_j, there_i] = total.T
            block = other[rows, pl.ds(j * tile, tile)]
            c_ref[here_i, here_j] = block
            d_ref[here_j, here_i] = block.T
            block = other[rows, pl.ds(half + j * tile, tile)]
            c_ref[there_i, there_j] = block
            d_ref[there_j, there_i] = block.T


def put_turned(step, target, cols, to, first, count, kind, table, *refs):
    rows = sum((step.flat(kind, table, first + v, cols, *refs) for v in range(count)), [])
    target[cols, to] = jnp.concatenate([piece.astype(BF16) for piece in rows], axis=0).T


def whole_step(step, c_ref, d_ref, r_ref, x_ref, c_new, d_new, tile):
    n = c_ref.shape[0]
    size = step.size
    count = tile // (step.group * size)

    @pl.loop(0, n // tile)
    def _(g):
        to = part_of(0, g, tile)

        @pl.loop(0, n // tile, unroll=4)
        def _(s):
            cols = part_of(0, s, tile)
            put_turned(step, r_ref, cols, to, g * count, count, "ham", step.minus, c_ref, d_ref)
            put_turned(step, x_ref, cols, to, g * count, count, "pull", None, d_ref)

    @pl.loop(0, n // tile)
    def _(g):
        @pl.loop(0, n // tile, unroll=4)
        def _(s):
            cols = part_of(0, s, tile)
            made = []
            for q in range(count):
                pulled = step.pull(g * count + q, x_ref, cols)
                for v in range(step.group):
                    c = (g * count + q) * step.group + v
                    own = pl.ds(pl.multiple_of(c * size, size), size)
                    change = step.ham(step.plus, c, d_ref, c_ref, cols) + pulled[v * size : (v + 1) * size]
                    change = change + r_ref[own, cols].astype(F32)
                    made.append((c_ref[own, cols].astype(F32) + time_step * change).astype(BF16))
                    c_new[own, cols] = made[-1]
            d_new[cols, part_of(0, g, tile)] = jnp.concatenate(made, axis=0).T


def own_step(step, start, width, c_ref, d_ref, turned, tile, base, out):
    n = c_ref.shape[0]
    part = min(tile, width)
    size = step.size
    deep = step.group * size
    count = part // deep
    kinds = (
        ("ham", step.minus, c_ref, d_ref),
        ("ham", step.plus, d_ref, c_ref),
        ("pull", None, d_ref),
        ("pull", None, c_ref),
    )

    @pl.loop(0, width // part)
    def _(g):
        @pl.loop(0, n // tile, unroll=2)
        def _(s):
            for k, kind in enumerate(kinds):
                to = part_of(k * width, g, part)
                put_turned(step, turned, part_of(0, s, tile), to, start // deep + g * count, count, *kind)

    @pl.loop(0, n // deep, unroll=2)
    def _(q):
        for s in range(width // part):
            cols = pl.ds(pl.multiple_of(start + s * part, part), part)
            to = pl.ds(s * part, part)
            of = [pl.ds(k * width + s * part, part) for k in range(4)]
            pulled = [step.pull(q, turned, of[k]) for k in (2, 3)]
            for v in range(step.group):
                c = q * step.group + v
                own = pl.ds(pl.multiple_of(c * size, size), size)
                here = slice(v * size, (v + 1) * size)
                change = step.ham(step.plus, c, d_ref, c_ref, cols) + pulled[0][here]
                second = step.ham(step.minus, c, c_ref, d_ref, cols) + pulled[1][here]
                change = change + turned[own, of[0]].astype(F32)
                second = second + turned[own, of[1]].astype(F32)
                real, imag = base(own, cols, to)
                out[0, 0, own, to] = (real + 0.5 * time_step * (change + second)).astype(BF16)
                out[0, 1, own, to] = (imag + 0.5 * time_step * (change - second)).astype(BF16)


def fill_whole(piece, c_ref, d_ref, sems, tile):
    load_all([(piece, c_ref)], sems)
    turn_whole(c_ref, d_ref, tile)


def inner_kernel(counts, tile, number, rows, place, terminal, jump, plus, minus, *refs):
    pieces, refs = refs[:number], refs[number:]
    out, c_ref, d_ref, stage, turned, sems = refs
    n, width = out.shape[2], out.shape[3]
    if number == 1:
        fill_whole(pieces[0], c_ref, d_ref, sems, tile)
        load_all([(terminal.at[0, k], stage.at[:, pl.ds(k * width, width)]) for k in range(2)], sems)
        starts = (0, width)
    else:
        assemble_first(place, terminal, *pieces, c_ref, d_ref, stage, turned, sems, tile)
        starts = (place[3], place[3] + 2 * width)
    step = Step(rows, counts, plus.shape[1], plus, minus, jump)

    def base(own, _, cols):
        part = cols.size
        return [
            stage[own, pl.ds(pl.multiple_of(first + cols.start, part), part)].astype(F32) for first in starts
        ]

    own_step(step, place[0], width, c_ref, d_ref, turned, tile, base, out)


def start_kernel(counts, tile, number, rows, place, terminal, jump, plus, minus, plus_two, minus_two, *refs):
    pieces, refs = refs[:number], refs[number:]
    out, c_ref, d_ref, r_ref, x_ref, c_new, d_new, sems = refs
    size = plus.shape[1]

    @pl.when(place[1] == 1)
    def _():
        load_all([(terminal, out)], sems)

    @pl.when(place[1] == 0)
    def _():
        if number == 1:
            fill_whole(pieces[0], c_ref, d_ref, sems, tile)
        else:
            assemble_next(place, pieces, c_ref, d_ref, r_ref, x_ref, sems, tile)
        whole_step(Step(rows, counts, size, plus, minus, jump), c_ref, d_ref, r_ref, x_ref, c_new, d_new, tile)

        def base(own, cols, _):
            first, second = c_new[own, cols].astype(F32), d_new[own, cols].astype(F32)
            return 0.5 * (first + second), 0.5 * (first - second)

        step = Step(rows, counts, size, plus_two, minus_two, jump)
        own_step(step, place[0], out.shape[3], c_new, d_new, r_ref, tile, base, out)


def swapped(block, bit):
    return lax.ppermute(block, "row", [(i, i ^ bit) for i in range(lax.axis_size("row"))])


def on_device(terminal, controls, ham_blocks, ham_cols, jump_blocks, jump_cols):
    n, width = terminal.shape[2], terminal.shape[3]
    tile = 256
    row = lax.axis_index("row")
    here = row // 2 * 2 * width
    controls_next = shifted_down(controls, "tm")
    is_last = lax.axis_index("tm") == lax.axis_size("tm") - 1
    place = jnp.stack([row * width, is_last.astype(jnp.int32), here, row % 2 * width]).astype(jnp.int32)
    operators = (ham_blocks, ham_cols, jump_blocks, jump_cols)

    smem = pl.BlockSpec(memory_space=pltpu.SMEM)
    vmem = pl.BlockSpec(memory_space=pltpu.VMEM)
    anywhere = pl.BlockSpec(memory_space=pl.ANY)
    square = pltpu.VMEM((n, n), BF16)

    def step_call(kernel, name, squares, rows, tables, pieces):
        return pl.pallas_call(
            functools.partial(kernel, counts, tile, len(pieces)),
            out_shape=jax.ShapeDtypeStruct(terminal.shape, BF16),
            in_specs=[smem, smem, anywhere] + [vmem] * len(tables) + [anywhere] * len(pieces),
            out_specs=vmem,
            scratch_shapes=[square] * squares + [pltpu.SemaphoreType.DMA((12,))],
            compiler_params=pltpu.CompilerParams(vmem_limit_bytes=60 * 2**20),
            cost_estimate=pl.CostEstimate(flops=1, bytes_accessed=1, transcendentals=0),
            name=name,
        )(rows, place, terminal, *tables, *pieces)

    counts, rows, *tables = operator_tables(((0, 1), (1, 1), (1, 0)), *operators, controls, controls_next)
    first, second = tables[:3], tables[:1] + tables[3:]
    if lax.axis_size("row") == 4:
        near_pair = swapped(terminal, 1)
        halves = terminal.reshape(2, 2, 2 * width, width)
        chip, top = row // 2, 5 * width // 4

        def cut(first, count, which, low, high):
            return lax.dynamic_slice(halves, (first, which, low, 0), (count, 1, high - low, width))[:, 0]

        mixed = (cut(0, 1, chip, 0, 2 * width)[0].astype(F32) + cut(1, 1, chip, 0, 2 * width)[0].astype(F32)).astype(BF16)
        mixed, controls_next = lax.optimization_barrier((mixed, controls_next))
        upper = shifted_down(cut(0, 2, 1 - chip, 0, top), "tm")
        lower = shifted_down(cut(0, 2, 1 - chip, top, 2 * width), "tm")
        near, far = shifted_down(mixed, "tm"), swapped(mixed, 2)
        far, rows = lax.optimization_barrier((far, rows))
        far_pair = swapped(far, 1)
        rows, mixed = lax.optimization_barrier((rows, near))
        far_next = swapped(mixed, 2)
        new_fpoint = step_call(inner_kernel, "inner_point", 4, rows, first, [near_pair, far, far_pair])
        mixed_pair = swapped(mixed, 1)
        upper, far_next, mixed_pair, new_fpoint = lax.optimization_barrier((upper, far_next, mixed_pair, new_fpoint))
        pieces = [mixed, upper, lower, far_next]
        pieces += [mixed_pair] + [swapped(piece, 1) for piece in pieces[1:]]
    else:
        mixed = (terminal[0, 0].astype(F32) + terminal[0, 1].astype(F32)).astype(BF16)

        def gathered(piece):
            return [lax.all_gather(piece, "row", axis=1, tiled=True)]

        new_fpoint = step_call(inner_kernel, "inner_point", 4, rows, first, gathered(mixed))
        pieces = gathered(shifted_down(mixed, "tm"))
    new_cpoint = step_call(start_kernel, "left_end", 6, rows, second, pieces)
    return (new_cpoint, new_fpoint)


def solution(mesh):
    in_specs = (P(("grp", "tm"), None, None, "row"), P(("grp", "tm"), None), P(), P(), P(), P())
    out_specs = (P(("grp", "tm"), None, None, "row"), P(("grp", "tm"), None, None, "row"))
    return jax.shard_map(
        on_device, mesh=mesh, in_specs=in_specs, out_specs=out_specs, check_vma=False
    )
```

```python
import functools

import jax
import jax.numpy as jnp
from jax import lax
from jax.experimental import pallas as pl
from jax.experimental.pallas import tpu as pltpu
from jax.sharding import PartitionSpec as P

time_step = 0.2
F32 = jnp.float32
BF16 = jnp.bfloat16


def shifted_down(block, axis):
    route = [(i, i - 1) for i in range(1, lax.axis_size(axis))]
    return lax.ppermute(block, axis, route)


def group_of(layers_j, size):
    return max(256 // (layers_j * size), 1)


def table_kernel(which, ham_cols, jump_cols, controls, controls_next, ham, jump, rows, jump_row, *refs):
    layers_h, count = ham_cols.shape
    layers_j = jump_cols.shape[0]
    size = ham.shape[-1]
    crossed = [(k, other) for k in range(layers_j) for other in range(layers_j) if k != other]
    *tables, came = refs
    group = jump_row.shape[1] // size
    first_k = 2 * layers_h
    first_j = first_k + 1 + len(crossed)

    @pl.loop(0, count, unroll=4)
    def _(b):
        for k in range(layers_h):
            rows[k, b] = ham_cols[k, b] * size
            rows[layers_h + k, ham_cols[k, b]] = b * size
            came[k, ham_cols[k, b]] = b
        for k in range(layers_j):
            rows[first_j + k, jump_cols[k, b]] = b * size
            came[layers_h + k, jump_cols[k, b]] = b

    def block_row(q, v):
        c = q * group + v
        came_h = [came[k, c] for k in range(layers_h)]
        came_j = [came[layers_h + k, c] for k in range(layers_j)]
        rows[first_k, c] = c * size
        for at, (k, other) in enumerate(crossed):
            rows[first_k + 1 + at, c] = jump_cols[other, came_j[k]] * size

        def ham_row(term):
            parts = [ham[term, c, k].astype(F32) for k in range(layers_h)]
            parts += [ham[term, came_h[k], k].astype(F32).T for k in range(layers_h)]
            return jnp.concatenate(parts, axis=1)

        stored = [[jump[came_j[k], other] for other in range(layers_j)] for k in range(layers_j)]
        turned = [stored[k][k].astype(F32).T.astype(BF16) for k in range(layers_j)]
        empty = [jnp.zeros_like(piece) for piece in turned]
        jump_row[q, v * size : (v + 1) * size, :] = jnp.concatenate(empty * v + turned + empty * (group - 1 - v), axis=1)
        square = sum(jnp.dot(turned[k], stored[k][k], preferred_element_type=F32) for k in range(layers_j))
        blocks = [square] + [jnp.dot(turned[k], stored[k][other], preferred_element_type=F32) for k, other in crossed]
        decay = -0.5 * jnp.concatenate(blocks, axis=1)
        drift, steer = ham_row(0), ham_row(1)
        for at, (later, fine) in enumerate(which):
            amplitude = (controls, controls_next)[later][0, fine]
            coeffs = drift + amplitude * steer
            tables[2 * at][c] = jnp.concatenate([coeffs, decay], axis=1).astype(BF16)
            tables[2 * at + 1][c] = jnp.concatenate([-coeffs, decay], axis=1).astype(BF16)

    @pl.loop(0, count // group, unroll=2)
    def _(q):
        for v in range(group):
            block_row(q, v)


def operator_tables(which, ham_blocks, ham_cols, jump_blocks, jump_cols, controls, controls_next):
    layers_h, count = ham_cols.shape
    layers_j = jump_cols.shape[0]
    size = ham_blocks.shape[-1]
    layers_k = 1 + layers_j * (layers_j - 1)
    smem = pl.BlockSpec(memory_space=pltpu.SMEM)
    vmem = pl.BlockSpec(memory_space=pltpu.VMEM)
    table = jax.ShapeDtypeStruct((count, size, (2 * layers_h + layers_k) * size), BF16)
    number = len(which)
    group = group_of(layers_j, size)
    rows, jump_row, *tables = pl.pallas_call(
        functools.partial(table_kernel, which),
        out_shape=[
            jax.ShapeDtypeStruct((2 * layers_h + layers_k + layers_j, count), jnp.int32),
            jax.ShapeDtypeStruct((count // group, group * size, group * layers_j * size), BF16),
        ] + [table] * (2 * number),
        in_specs=[smem, smem, smem, smem, vmem, vmem],
        out_specs=[smem, vmem] + [vmem] * (2 * number),
        scratch_shapes=[pltpu.SMEM((layers_h + layers_j, count), jnp.int32)],
        compiler_params=pltpu.CompilerParams(vmem_limit_bytes=60 * 2**20),
        cost_estimate=pl.CostEstimate(flops=1, bytes_accessed=1, transcendentals=0),
        name="operator_tables",
    )(ham_cols, jump_cols, controls, controls_next, ham_blocks, jump_blocks)
    return (2 * layers_h, layers_k, layers_j), rows, jump_row, *tables


class Step:
    def __init__(self, rows, counts, size, plus, minus, jump):
        self.rows, self.counts, self.size = rows, counts, size
        self.plus, self.minus, self.jump = plus, minus, jump
        self.group = jump.shape[1] // size

    def take(self, ref, kind, c, cols):
        first = sum(self.counts[:kind])
        return [
            ref[pl.ds(pl.multiple_of(self.rows[first + k, c], self.size), self.size), cols]
            for k in range(self.counts[kind])
        ]

    def ham(self, table, c, ham_ref, decay_ref, cols):
        met = jnp.concatenate(self.take(ham_ref, 0, c, cols) + self.take(decay_ref, 1, c, cols), axis=0)
        return jnp.dot(table[c], met, preferred_element_type=F32)

    def pull(self, q, ref, cols):
        met = jnp.concatenate(sum((self.take(ref, 2, q * self.group + v, cols) for v in range(self.group)), []), axis=0)
        return jnp.dot(self.jump[q], met, preferred_element_type=F32)

    def flat(self, kind, table, q, cols, *refs):
        if kind == "pull":
            return [self.pull(q, *refs, cols)]
        return [self.ham(table, q * self.group + v, *refs, cols) for v in range(self.group)]


def turn_whole(source, target, tile):
    n = source.shape[0] // tile

    @pl.loop(0, n)
    def _(i):
        near = pl.ds(pl.multiple_of(i * tile, tile), tile)
        for j in range(n):
            far = pl.ds(j * tile, tile)
            target[far, near] = source[near, far].T


def load_all(copies, sems):
    copies = [pltpu.make_async_copy(source, target, sems.at[k]) for k, (source, target) in enumerate(copies)]
    for copy in copies:
        copy.start()
    for copy in copies:
        copy.wait()


def part_of(first, k, tile):
    return pl.ds(pl.multiple_of(first + k * tile, tile), tile)


def assemble_first(place, near, near_pair, far, far_pair, c_ref, d_ref, stage, other, sems, tile):
    half, width = far.shape
    here, there = place[2], half - place[2]
    own, pair = place[3], width - place[3]

    def cols(first):
        return pl.ds(pl.multiple_of(first, width), width)

    copies = [
        (far, other.at[pl.ds(0, half), cols(own)]),
        (far_pair, other.at[pl.ds(0, half), cols(pair)]),
    ]
    for k in range(2):
        copies.append((near.at[0, k], stage.at[:, cols(k * half + own)]))
        copies.append((near_pair.at[0, k], stage.at[:, cols(k * half + pair)]))
    load_all(copies, sems)

    def mixed(rows, j):
        real = stage[rows, pl.ds(j * tile, tile)].astype(F32)
        imag = stage[rows, pl.ds(half + j * tile, tile)].astype(F32)
        return (real + imag).astype(BF16), (real - imag).astype(BF16)

    @pl.loop(0, half // tile)
    def _(i):
        here_i, there_i = part_of(here, i, tile), part_of(there, i, tile)
        for j in range(half // tile):
            here_j, there_j = part_of(here, j, tile), part_of(there, j, tile)
            total, less = mixed(there_i, j)
            c_ref[there_i, here_j] = total
            d_ref[there_i, here_j] = less
            c_ref[here_j, there_i] = less.T
            d_ref[here_j, there_i] = total.T
            block = other[part_of(0, i, tile), pl.ds(j * tile, tile)]
            c_ref[there_i, there_j] = block
            d_ref[there_j, there_i] = block.T
            total, less = mixed(here_i, j)
            c_ref[here_i, here_j] = total
            d_ref[here_i, here_j] = less


def assemble_next(place, pieces, c_ref, d_ref, stage, other, sems, tile):
    half, width = pieces[0].shape
    here, there = place[2], half - place[2]
    copies = []
    for (near, upper, lower, far), core in ((pieces[:4], place[3]), (pieces[4:], width - place[3])):
        low = pl.ds(pl.multiple_of(core, width), width)
        high = pl.ds(pl.multiple_of(half + core, width), width)
        rows = pl.ds(0, half)
        copies += [(near, other.at[rows, low]), (far, other.at[rows, high])]
        top = upper.shape[1]
        for k, to in enumerate((low, high)):
            copies.append((upper.at[k], stage.at[pl.ds(0, top), to]))
            copies.append((lower.at[k], stage.at[pl.ds(top, half - top), to]))
    load_all(copies, sems)

    @pl.loop(0, half // tile)
    def _(i):
        rows = part_of(0, i, tile)
        here_i, there_i = part_of(here, i, tile), part_of(there, i, tile)
        for j in range(half // tile):
            here_j, there_j = part_of(here, j, tile), part_of(there, j, tile)
            real = stage[rows, pl.ds(j * tile, tile)].astype(F32)
            imag = stage[rows, pl.ds(half + j * tile, tile)].astype(F32)
            total, less = (real + imag).astype(BF16), (real - imag).astype(BF16)
            c_ref[there_i, here_j] = total
            d_ref[there_i, here_j] = less
            c_ref[here_j, there_i] = less.T
            d_ref[here_j, there_i] = total.T
            block = other[rows, pl.ds(j * tile, tile)]
            c_ref[here_i, here_j] = block
            d_ref[here_j, here_i] = block.T
            block = other[rows, pl.ds(half + j * tile, tile)]
            c_ref[there_i, there_j] = block
            d_ref[there_j, there_i] = block.T


def put_turned(step, target, cols, to, first, count, kind, table, *refs):
    rows = sum((step.flat(kind, table, first + v, cols, *refs) for v in range(count)), [])
    target[cols, to] = jnp.concatenate([piece.astype(BF16) for piece in rows], axis=0).T


def whole_step(step, c_ref, d_ref, r_ref, x_ref, c_new, d_new, tile):
    n = c_ref.shape[0]
    size = step.size
    count = tile // (step.group * size)

    @pl.loop(0, n // tile)
    def _(g):
        to = part_of(0, g, tile)

        @pl.loop(0, n // tile, unroll=8)
        def _(s):
            cols = part_of(0, s, tile)
            put_turned(step, r_ref, cols, to, g * count, count, "ham", step.minus, c_ref, d_ref)
            put_turned(step, x_ref, cols, to, g * count, count, "pull", None, d_ref)

    @pl.loop(0, n // tile)
    def _(g):
        @pl.loop(0, n // tile, unroll=8)
        def _(s):
            cols = part_of(0, s, tile)
            made = []
            for q in range(count):
                pulled = step.pull(g * count + q, x_ref, cols)
                for v in range(step.group):
                    c = (g * count + q) * step.group + v
                    own = pl.ds(pl.multiple_of(c * size, size), size)
                    change = step.ham(step.plus, c, d_ref, c_ref, cols) + pulled[v * size : (v + 1) * size]
                    change = change + r_ref[own, cols].astype(F32)
                    made.append((c_ref[own, cols].astype(F32) + time_step * change).astype(BF16))
                    c_new[own, cols] = made[-1]
            d_new[cols, part_of(0, g, tile)] = jnp.concatenate(made, axis=0).T


def own_step(step, start, width, c_ref, d_ref, turned, tile, base, out):
    n = c_ref.shape[0]
    part = min(tile, width)
    size = step.size
    deep = step.group * size
    count = part // deep
    kinds = (
        ("ham", step.minus, c_ref, d_ref),
        ("ham", step.plus, d_ref, c_ref),
        ("pull", None, d_ref),
        ("pull", None, c_ref),
    )

    @pl.loop(0, width // part)
    def _(g):
        @pl.loop(0, n // tile, unroll=4)
        def _(s):
            for k, kind in enumerate(kinds):
                to = part_of(k * width, g, part)
                put_turned(step, turned, part_of(0, s, tile), to, start // deep + g * count, count, *kind)

    @pl.loop(0, n // deep, unroll=4)
    def _(q):
        for s in range(width // part):
            cols = pl.ds(pl.multiple_of(start + s * part, part), part)
            to = pl.ds(s * part, part)
            of = [pl.ds(k * width + s * part, part) for k in range(4)]
            pulled = [step.pull(q, turned, of[k]) for k in (2, 3)]
            for v in range(step.group):
                c = q * step.group + v
                own = pl.ds(pl.multiple_of(c * size, size), size)
                here = slice(v * size, (v + 1) * size)
                change = step.ham(step.plus, c, d_ref, c_ref, cols) + pulled[0][here]
                second = step.ham(step.minus, c, c_ref, d_ref, cols) + pulled[1][here]
                change = change + turned[own, of[0]].astype(F32)
                second = second + turned[own, of[1]].astype(F32)
                real, imag = base(own, cols, to)
                out[0, 0, own, to] = (real + 0.5 * time_step * (change + second)).astype(BF16)
                out[0, 1, own, to] = (imag + 0.5 * time_step * (change - second)).astype(BF16)


def fill_whole(piece, c_ref, d_ref, sems, tile):
    load_all([(piece, c_ref)], sems)
    turn_whole(c_ref, d_ref, tile)


def inner_kernel(counts, tile, number, rows, place, terminal, jump, plus, minus, *refs):
    pieces, refs = refs[:number], refs[number:]
    out, c_ref, d_ref, stage, turned, sems = refs
    n, width = out.shape[2], out.shape[3]
    if number == 1:
        fill_whole(pieces[0], c_ref, d_ref, sems, tile)
        load_all([(terminal.at[0, k], stage.at[:, pl.ds(k * width, width)]) for k in range(2)], sems)
        starts = (0, width)
    else:
        assemble_first(place, terminal, *pieces, c_ref, d_ref, stage, turned, sems, tile)
        starts = (place[3], place[3] + 2 * width)
    step = Step(rows, counts, plus.shape[1], plus, minus, jump)

    def base(own, _, cols):
        part = cols.size
        return [
            stage[own, pl.ds(pl.multiple_of(first + cols.start, part), part)].astype(F32) for first in starts
        ]

    own_step(step, place[0], width, c_ref, d_ref, turned, tile, base, out)


def start_kernel(counts, tile, number, rows, place, terminal, jump, plus, minus, plus_two, minus_two, *refs):
    pieces, refs = refs[:number], refs[number:]
    out, c_ref, d_ref, r_ref, x_ref, c_new, d_new, sems = refs
    size = plus.shape[1]

    @pl.when(place[1] == 1)
    def _():
        load_all([(terminal, out)], sems)

    @pl.when(place[1] == 0)
    def _():
        if number == 1:
            fill_whole(pieces[0], c_ref, d_ref, sems, tile)
        else:
            assemble_next(place, pieces, c_ref, d_ref, r_ref, x_ref, sems, tile)
        whole_step(Step(rows, counts, size, plus, minus, jump), c_ref, d_ref, r_ref, x_ref, c_new, d_new, tile)

        def base(own, cols, _):
            first, second = c_new[own, cols].astype(F32), d_new[own, cols].astype(F32)
            return 0.5 * (first + second), 0.5 * (first - second)

        step = Step(rows, counts, size, plus_two, minus_two, jump)
        own_step(step, place[0], out.shape[3], c_new, d_new, r_ref, tile, base, out)


def swapped(block, bit):
    return lax.ppermute(block, "row", [(i, i ^ bit) for i in range(lax.axis_size("row"))])


def on_device(terminal, controls, ham_blocks, ham_cols, jump_blocks, jump_cols):
    n, width = terminal.shape[2], terminal.shape[3]
    tile = 256
    row = lax.axis_index("row")
    here = row // 2 * 2 * width
    controls_next = shifted_down(controls, "tm")
    is_last = lax.axis_index("tm") == lax.axis_size("tm") - 1
    place = jnp.stack([row * width, is_last.astype(jnp.int32), here, row % 2 * width]).astype(jnp.int32)
    operators = (ham_blocks, ham_cols, jump_blocks, jump_cols)

    smem = pl.BlockSpec(memory_space=pltpu.SMEM)
    vmem = pl.BlockSpec(memory_space=pltpu.VMEM)
    anywhere = pl.BlockSpec(memory_space=pl.ANY)
    square = pltpu.VMEM((n, n), BF16)

    def step_call(kernel, name, squares, rows, tables, pieces):
        return pl.pallas_call(
            functools.partial(kernel, counts, tile, len(pieces)),
            out_shape=jax.ShapeDtypeStruct(terminal.shape, BF16),
            in_specs=[smem, smem, anywhere] + [vmem] * len(tables) + [anywhere] * len(pieces),
            out_specs=vmem,
            scratch_shapes=[square] * squares + [pltpu.SemaphoreType.DMA((12,))],
            compiler_params=pltpu.CompilerParams(vmem_limit_bytes=60 * 2**20),
            cost_estimate=pl.CostEstimate(flops=1, bytes_accessed=1, transcendentals=0),
            name=name,
        )(rows, place, terminal, *tables, *pieces)

    counts, rows, *tables = operator_tables(((0, 1), (1, 1), (1, 0)), *operators, controls, controls_next)
    first, second = tables[:3], tables[:1] + tables[3:]
    if lax.axis_size("row") == 4:
        near_pair = swapped(terminal, 1)
        halves = terminal.reshape(2, 2, 2 * width, width)
        chip, top = row // 2, 5 * width // 4

        def cut(first, count, which, low, high):
            return lax.dynamic_slice(halves, (first, which, low, 0), (count, 1, high - low, width))[:, 0]

        mixed = (cut(0, 1, chip, 0, 2 * width)[0].astype(F32) + cut(1, 1, chip, 0, 2 * width)[0].astype(F32)).astype(BF16)
        near = shifted_down(mixed, "tm")
        across, controls_next = lax.optimization_barrier((mixed, controls_next))
        far = swapped(across, 2)
        upper = shifted_down(cut(0, 2, 1 - chip, 0, top), "tm")
        lower = shifted_down(cut(0, 2, 1 - chip, top, 2 * width), "tm")
        far, rows = lax.optimization_barrier((far, rows))
        far_pair = swapped(far, 1)
        rows, mixed = lax.optimization_barrier((rows, near))
        far_next = swapped(mixed, 2)
        new_fpoint = step_call(inner_kernel, "inner_point", 4, rows, first, [near_pair, far, far_pair])
        mixed_pair = swapped(mixed, 1)
        upper, far_next, mixed_pair, new_fpoint = lax.optimization_barrier((upper, far_next, mixed_pair, new_fpoint))
        pieces = [mixed, upper, lower, far_next]
        pieces += [mixed_pair] + [swapped(piece, 1) for piece in pieces[1:]]
    else:
        mixed = (terminal[0, 0].astype(F32) + terminal[0, 1].astype(F32)).astype(BF16)

        def gathered(piece):
            return [lax.all_gather(piece, "row", axis=1, tiled=True)]

        new_fpoint = step_call(inner_kernel, "inner_point", 4, rows, first, gathered(mixed))
        pieces = gathered(shifted_down(mixed, "tm"))
    new_cpoint = step_call(start_kernel, "left_end", 6, rows, second, pieces)
    return (new_cpoint, new_fpoint)


def solution(mesh):
    in_specs = (P(("grp", "tm"), None, None, "row"), P(("grp", "tm"), None), P(), P(), P(), P())
    out_specs = (P(("grp", "tm"), None, None, "row"), P(("grp", "tm"), None, None, "row"))
    return jax.shard_map(
        on_device, mesh=mesh, in_specs=in_specs, out_specs=out_specs, check_vma=False
    )
```

```python
import functools

import jax
import jax.numpy as jnp
from jax import lax
from jax.experimental import pallas as pl
from jax.experimental.pallas import tpu as pltpu
from jax.sharding import PartitionSpec as P

time_step = 0.2
F32 = jnp.float32
BF16 = jnp.bfloat16


def shifted_down(block, axis):
    route = [(i, i - 1) for i in range(1, lax.axis_size(axis))]
    return lax.ppermute(block, axis, route)


def group_of(layers_j, size):
    return max(256 // (layers_j * size), 1)


def table_kernel(which, ham_cols, jump_cols, controls, controls_next, ham, jump, rows, jump_row, *refs):
    layers_h, count = ham_cols.shape
    layers_j = jump_cols.shape[0]
    size = ham.shape[-1]
    crossed = [(k, other) for k in range(layers_j) for other in range(layers_j) if k != other]
    *tables, came = refs
    group = jump_row.shape[1] // size
    first_k = 2 * layers_h
    first_j = first_k + 1 + len(crossed)

    @pl.loop(0, count, unroll=4)
    def _(b):
        for k in range(layers_h):
            rows[k, b] = ham_cols[k, b] * size
            rows[layers_h + k, ham_cols[k, b]] = b * size
            came[k, ham_cols[k, b]] = b
        for k in range(layers_j):
            rows[first_j + k, jump_cols[k, b]] = b * size
            came[layers_h + k, jump_cols[k, b]] = b

    def block_row(q, v):
        c = q * group + v
        came_h = [came[k, c] for k in range(layers_h)]
        came_j = [came[layers_h + k, c] for k in range(layers_j)]
        rows[first_k, c] = c * size
        for at, (k, other) in enumerate(crossed):
            rows[first_k + 1 + at, c] = jump_cols[other, came_j[k]] * size

        def ham_row(term):
            parts = [ham[term, c, k].astype(F32) for k in range(layers_h)]
            parts += [ham[term, came_h[k], k].astype(F32).T for k in range(layers_h)]
            return jnp.concatenate(parts, axis=1)

        stored = [[jump[came_j[k], other] for other in range(layers_j)] for k in range(layers_j)]
        turned = [stored[k][k].astype(F32).T.astype(BF16) for k in range(layers_j)]
        empty = [jnp.zeros_like(piece) for piece in turned]
        jump_row[q, v * size : (v + 1) * size, :] = jnp.concatenate(empty * v + turned + empty * (group - 1 - v), axis=1)
        square = sum(jnp.dot(turned[k], stored[k][k], preferred_element_type=F32) for k in range(layers_j))
        blocks = [square] + [jnp.dot(turned[k], stored[k][other], preferred_element_type=F32) for k, other in crossed]
        decay = -0.5 * jnp.concatenate(blocks, axis=1)
        drift, steer = ham_row(0), ham_row(1)
        for at, (later, fine) in enumerate(which):
            amplitude = (controls, controls_next)[later][0, fine]
            coeffs = drift + amplitude * steer
            tables[2 * at][c] = jnp.concatenate([coeffs, decay], axis=1).astype(BF16)
            tables[2 * at + 1][c] = jnp.concatenate([-coeffs, decay], axis=1).astype(BF16)

    @pl.loop(0, count // group, unroll=2)
    def _(q):
        for v in range(group):
            block_row(q, v)


def operator_tables(which, ham_blocks, ham_cols, jump_blocks, jump_cols, controls, controls_next):
    layers_h, count = ham_cols.shape
    layers_j = jump_cols.shape[0]
    size = ham_blocks.shape[-1]
    layers_k = 1 + layers_j * (layers_j - 1)
    smem = pl.BlockSpec(memory_space=pltpu.SMEM)
    vmem = pl.BlockSpec(memory_space=pltpu.VMEM)
    table = jax.ShapeDtypeStruct((count, size, (2 * layers_h + layers_k) * size), BF16)
    number = len(which)
    group = group_of(layers_j, size)
    rows, jump_row, *tables = pl.pallas_call(
        functools.partial(table_kernel, which),
        out_shape=[
            jax.ShapeDtypeStruct((2 * layers_h + layers_k + layers_j, count), jnp.int32),
            jax.ShapeDtypeStruct((count // group, group * size, group * layers_j * size), BF16),
        ] + [table] * (2 * number),
        in_specs=[smem, smem, smem, smem, vmem, vmem],
        out_specs=[smem, vmem] + [vmem] * (2 * number),
        scratch_shapes=[pltpu.SMEM((layers_h + layers_j, count), jnp.int32)],
        compiler_params=pltpu.CompilerParams(vmem_limit_bytes=60 * 2**20),
        cost_estimate=pl.CostEstimate(flops=1, bytes_accessed=1, transcendentals=0),
        name="operator_tables",
    )(ham_cols, jump_cols, controls, controls_next, ham_blocks, jump_blocks)
    return (2 * layers_h, layers_k, layers_j), rows, jump_row, *tables


class Step:
    def __init__(self, rows, counts, size, plus, minus, jump):
        self.rows, self.counts, self.size = rows, counts, size
        self.plus, self.minus, self.jump = plus, minus, jump
        self.group = jump.shape[1] // size

    def take(self, ref, kind, c, cols):
        first = sum(self.counts[:kind])
        return [
            ref[pl.ds(pl.multiple_of(self.rows[first + k, c], self.size), self.size), cols]
            for k in range(self.counts[kind])
        ]

    def ham(self, table, c, ham_ref, decay_ref, cols):
        met = jnp.concatenate(self.take(ham_ref, 0, c, cols) + self.take(decay_ref, 1, c, cols), axis=0)
        return jnp.dot(table[c], met, preferred_element_type=F32)

    def pull(self, q, ref, cols):
        met = jnp.concatenate(sum((self.take(ref, 2, q * self.group + v, cols) for v in range(self.group)), []), axis=0)
        return jnp.dot(self.jump[q], met, preferred_element_type=F32)

    def flat(self, kind, table, q, cols, *refs):
        if kind == "pull":
            return [self.pull(q, *refs, cols)]
        return [self.ham(table, q * self.group + v, *refs, cols) for v in range(self.group)]


def turn_whole(source, target, tile):
    n = source.shape[0] // tile

    @pl.loop(0, n)
    def _(i):
        near = pl.ds(pl.multiple_of(i * tile, tile), tile)
        for j in range(n):
            far = pl.ds(j * tile, tile)
            target[far, near] = source[near, far].T


def load_all(copies, sems):
    copies = [pltpu.make_async_copy(source, target, sems.at[k]) for k, (source, target) in enumerate(copies)]
    for copy in copies:
        copy.start()
    for copy in copies:
        copy.wait()


def part_of(first, k, tile):
    return pl.ds(pl.multiple_of(first + k * tile, tile), tile)


def assemble_first(place, near, near_pair, far, far_pair, c_ref, d_ref, stage, other, sems, tile):
    half, width = far.shape
    here, there = place[2], half - place[2]
    own, pair = place[3], width - place[3]

    def cols(first):
        return pl.ds(pl.multiple_of(first, width), width)

    copies = [
        (far, other.at[pl.ds(0, half), cols(own)]),
        (far_pair, other.at[pl.ds(0, half), cols(pair)]),
    ]
    for k in range(2):
        copies.append((near.at[0, k], stage.at[:, cols(k * half + own)]))
        copies.append((near_pair.at[0, k], stage.at[:, cols(k * half + pair)]))
    load_all(copies, sems)

    def mixed(rows, j):
        real = stage[rows, pl.ds(j * tile, tile)].astype(F32)
        imag = stage[rows, pl.ds(half + j * tile, tile)].astype(F32)
        return (real + imag).astype(BF16), (real - imag).astype(BF16)

    @pl.loop(0, half // tile)
    def _(i):
        here_i, there_i = part_of(here, i, tile), part_of(there, i, tile)
        for j in range(half // tile):
            here_j, there_j = part_of(here, j, tile), part_of(there, j, tile)
            total, less = mixed(there_i, j)
            c_ref[there_i, here_j] = total
            d_ref[there_i, here_j] = less
            c_ref[here_j, there_i] = less.T
            d_ref[here_j, there_i] = total.T
            block = other[part_of(0, i, tile), pl.ds(j * tile, tile)]
            c_ref[there_i, there_j] = block
            d_ref[there_j, there_i] = block.T
            total, less = mixed(here_i, j)
            c_ref[here_i, here_j] = total
            d_ref[here_i, here_j] = less


def assemble_next(place, pieces, c_ref, d_ref, stage, other, sems, tile):
    half, width = pieces[0].shape
    here, there = place[2], half - place[2]
    copies = []
    for (near, upper, lower, far), core in ((pieces[:4], place[3]), (pieces[4:], width - place[3])):
        low = pl.ds(pl.multiple_of(core, width), width)
        high = pl.ds(pl.multiple_of(half + core, width), width)
        rows = pl.ds(0, half)
        copies += [(near, other.at[rows, low]), (far, other.at[rows, high])]
        top = upper.shape[1]
        for k, to in enumerate((low, high)):
            copies.append((upper.at[k], stage.at[pl.ds(0, top), to]))
            copies.append((lower.at[k], stage.at[pl.ds(top, half - top), to]))
    load_all(copies, sems)

    @pl.loop(0, half // tile)
    def _(i):
        rows = part_of(0, i, tile)
        here_i, there_i = part_of(here, i, tile), part_of(there, i, tile)
        for j in range(half // tile):
            here_j, there_j = part_of(here, j, tile), part_of(there, j, tile)
            real = stage[rows, pl.ds(j * tile, tile)].astype(F32)
            imag = stage[rows, pl.ds(half + j * tile, tile)].astype(F32)
            total, less = (real + imag).astype(BF16), (real - imag).astype(BF16)
            c_ref[there_i, here_j] = total
            d_ref[there_i, here_j] = less
            c_ref[here_j, there_i] = less.T
            d_ref[here_j, there_i] = total.T
            block = other[rows, pl.ds(j * tile, tile)]
            c_ref[here_i, here_j] = block
            d_ref[here_j, here_i] = block.T
            block = other[rows, pl.ds(half + j * tile, tile)]
            c_ref[there_i, there_j] = block
            d_ref[there_j, there_i] = block.T


def put_turned(step, target, cols, to, first, count, kind, table, *refs):
    rows = sum((step.flat(kind, table, first + v, cols, *refs) for v in range(count)), [])
    target[cols, to] = jnp.concatenate([piece.astype(BF16) for piece in rows], axis=0).T


def whole_step(step, c_ref, d_ref, r_ref, x_ref, c_new, d_new, tile):
    n = c_ref.shape[0]
    size = step.size
    count = tile // (step.group * size)

    @pl.loop(0, n // tile)
    def _(g):
        to = part_of(0, g, tile)

        @pl.loop(0, n // tile, unroll=8)
        def _(s):
            cols = part_of(0, s, tile)
            put_turned(step, r_ref, cols, to, g * count, count, "ham", step.minus, c_ref, d_ref)
            put_turned(step, x_ref, cols, to, g * count, count, "pull", None, d_ref)

    @pl.loop(0, n // tile)
    def _(g):
        @pl.loop(0, n // tile, unroll=8)
        def _(s):
            cols = part_of(0, s, tile)
            made = []
            for q in range(count):
                pulled = step.pull(g * count + q, x_ref, cols)
                for v in range(step.group):
                    c = (g * count + q) * step.group + v
                    own = pl.ds(pl.multiple_of(c * size, size), size)
                    change = step.ham(step.plus, c, d_ref, c_ref, cols) + pulled[v * size : (v + 1) * size]
                    change = change + r_ref[own, cols].astype(F32)
                    made.append((c_ref[own, cols].astype(F32) + time_step * change).astype(BF16))
                    c_new[own, cols] = made[-1]
            d_new[cols, part_of(0, g, tile)] = jnp.concatenate(made, axis=0).T


def own_step(step, start, width, c_ref, d_ref, turned, tile, base, out):
    n = c_ref.shape[0]
    part = min(tile, width)
    size = step.size
    deep = step.group * size
    count = part // deep
    kinds = (
        ("ham", step.minus, c_ref, d_ref),
        ("ham", step.plus, d_ref, c_ref),
        ("pull", None, d_ref),
        ("pull", None, c_ref),
    )

    @pl.loop(0, width // part)
    def _(g):
        @pl.loop(0, n // tile, unroll=8)
        def _(s):
            for k, kind in enumerate(kinds):
                to = part_of(k * width, g, part)
                put_turned(step, turned, part_of(0, s, tile), to, start // deep + g * count, count, *kind)

    @pl.loop(0, n // deep, unroll=8)
    def _(q):
        for s in range(width // part):
            cols = pl.ds(pl.multiple_of(start + s * part, part), part)
            to = pl.ds(s * part, part)
            of = [pl.ds(k * width + s * part, part) for k in range(4)]
            pulled = [step.pull(q, turned, of[k]) for k in (2, 3)]
            for v in range(step.group):
                c = q * step.group + v
                own = pl.ds(pl.multiple_of(c * size, size), size)
                here = slice(v * size, (v + 1) * size)
                change = step.ham(step.plus, c, d_ref, c_ref, cols) + pulled[0][here]
                second = step.ham(step.minus, c, c_ref, d_ref, cols) + pulled[1][here]
                change = change + turned[own, of[0]].astype(F32)
                second = second + turned[own, of[1]].astype(F32)
                real, imag = base(own, cols, to)
                out[0, 0, own, to] = (real + 0.5 * time_step * (change + second)).astype(BF16)
                out[0, 1, own, to] = (imag + 0.5 * time_step * (change - second)).astype(BF16)


def fill_whole(piece, c_ref, d_ref, sems, tile):
    load_all([(piece, c_ref)], sems)
    turn_whole(c_ref, d_ref, tile)


def inner_kernel(counts, tile, number, rows, place, terminal, jump, plus, minus, *refs):
    pieces, refs = refs[:number], refs[number:]
    out, c_ref, d_ref, stage, turned, sems = refs
    n, width = out.shape[2], out.shape[3]
    if number == 1:
        fill_whole(pieces[0], c_ref, d_ref, sems, tile)
        load_all([(terminal.at[0, k], stage.at[:, pl.ds(k * width, width)]) for k in range(2)], sems)
        starts = (0, width)
    else:
        assemble_first(place, terminal, *pieces, c_ref, d_ref, stage, turned, sems, tile)
        starts = (place[3], place[3] + 2 * width)
    step = Step(rows, counts, plus.shape[1], plus, minus, jump)

    def base(own, _, cols):
        part = cols.size
        return [
            stage[own, pl.ds(pl.multiple_of(first + cols.start, part), part)].astype(F32) for first in starts
        ]

    own_step(step, place[0], width, c_ref, d_ref, turned, tile, base, out)


def start_kernel(counts, tile, number, rows, place, terminal, jump, plus, minus, plus_two, minus_two, *refs):
    pieces, refs = refs[:number], refs[number:]
    out, c_ref, d_ref, r_ref, x_ref, c_new, d_new, sems = refs
    size = plus.shape[1]

    @pl.when(place[1] == 1)
    def _():
        load_all([(terminal, out)], sems)

    @pl.when(place[1] == 0)
    def _():
        if number == 1:
            fill_whole(pieces[0], c_ref, d_ref, sems, tile)
        else:
            assemble_next(place, pieces, c_ref, d_ref, r_ref, x_ref, sems, tile)
        whole_step(Step(rows, counts, size, plus, minus, jump), c_ref, d_ref, r_ref, x_ref, c_new, d_new, tile)

        def base(own, cols, _):
            first, second = c_new[own, cols].astype(F32), d_new[own, cols].astype(F32)
            return 0.5 * (first + second), 0.5 * (first - second)

        step = Step(rows, counts, size, plus_two, minus_two, jump)
        own_step(step, place[0], out.shape[3], c_new, d_new, r_ref, tile, base, out)


def swapped(block, bit):
    return lax.ppermute(block, "row", [(i, i ^ bit) for i in range(lax.axis_size("row"))])


def on_device(terminal, controls, ham_blocks, ham_cols, jump_blocks, jump_cols):
    n, width = terminal.shape[2], terminal.shape[3]
    tile = 256
    row = lax.axis_index("row")
    here = row // 2 * 2 * width
    controls_next = shifted_down(controls, "tm")
    is_last = lax.axis_index("tm") == lax.axis_size("tm") - 1
    place = jnp.stack([row * width, is_last.astype(jnp.int32), here, row % 2 * width]).astype(jnp.int32)
    operators = (ham_blocks, ham_cols, jump_blocks, jump_cols)

    smem = pl.BlockSpec(memory_space=pltpu.SMEM)
    vmem = pl.BlockSpec(memory_space=pltpu.VMEM)
    anywhere = pl.BlockSpec(memory_space=pl.ANY)
    square = pltpu.VMEM((n, n), BF16)

    def step_call(kernel, name, squares, rows, tables, pieces):
        return pl.pallas_call(
            functools.partial(kernel, counts, tile, len(pieces)),
            out_shape=jax.ShapeDtypeStruct(terminal.shape, BF16),
            in_specs=[smem, smem, anywhere] + [vmem] * len(tables) + [anywhere] * len(pieces),
            out_specs=vmem,
            scratch_shapes=[square] * squares + [pltpu.SemaphoreType.DMA((12,))],
            compiler_params=pltpu.CompilerParams(vmem_limit_bytes=60 * 2**20),
            cost_estimate=pl.CostEstimate(flops=1, bytes_accessed=1, transcendentals=0),
            name=name,
        )(rows, place, terminal, *tables, *pieces)

    counts, rows, *tables = operator_tables(((0, 1), (1, 1), (1, 0)), *operators, controls, controls_next)
    first, second = tables[:3], tables[:1] + tables[3:]
    if lax.axis_size("row") == 4:
        near_pair = swapped(terminal, 1)
        halves = terminal.reshape(2, 2, 2 * width, width)
        chip, top = row // 2, 5 * width // 4

        def cut(first, count, which, low, high):
            return lax.dynamic_slice(halves, (first, which, low, 0), (count, 1, high - low, width))[:, 0]

        mixed = (cut(0, 1, chip, 0, 2 * width)[0].astype(F32) + cut(1, 1, chip, 0, 2 * width)[0].astype(F32)).astype(BF16)
        near = shifted_down(mixed, "tm")
        across, controls_next = lax.optimization_barrier((mixed, controls_next))
        far = swapped(across, 2)
        upper = shifted_down(cut(0, 2, 1 - chip, 0, top), "tm")
        lower = shifted_down(cut(0, 2, 1 - chip, top, 2 * width), "tm")
        far, rows = lax.optimization_barrier((far, rows))
        far_pair = swapped(far, 1)
        rows, mixed = lax.optimization_barrier((rows, near))
        far_next = swapped(mixed, 2)
        new_fpoint = step_call(inner_kernel, "inner_point", 4, rows, first, [near_pair, far, far_pair])
        mixed_pair = swapped(mixed, 1)
        upper, far_next, mixed_pair, new_fpoint = lax.optimization_barrier((upper, far_next, mixed_pair, new_fpoint))
        pieces = [mixed, upper, lower, far_next]
        pieces += [mixed_pair] + [swapped(piece, 1) for piece in pieces[1:]]
    else:
        mixed = (terminal[0, 0].astype(F32) + terminal[0, 1].astype(F32)).astype(BF16)

        def gathered(piece):
            return [lax.all_gather(piece, "row", axis=1, tiled=True)]

        new_fpoint = step_call(inner_kernel, "inner_point", 4, rows, first, gathered(mixed))
        pieces = gathered(shifted_down(mixed, "tm"))
    new_cpoint = step_call(start_kernel, "left_end", 6, rows, second, pieces)
    return (new_cpoint, new_fpoint)


def solution(mesh):
    in_specs = (P(("grp", "tm"), None, None, "row"), P(("grp", "tm"), None), P(), P(), P(), P())
    out_specs = (P(("grp", "tm"), None, None, "row"), P(("grp", "tm"), None, None, "row"))
    return jax.shard_map(
        on_device, mesh=mesh, in_specs=in_specs, out_specs=out_specs, check_vma=False
    )
```

```python
import functools

import jax
import jax.numpy as jnp
from jax import lax
from jax.experimental import pallas as pl
from jax.experimental.pallas import tpu as pltpu
from jax.sharding import PartitionSpec as P

time_step = 0.2
F32 = jnp.float32
BF16 = jnp.bfloat16


def shifted_down(block, axis):
    route = [(i, i - 1) for i in range(1, lax.axis_size(axis))]
    return lax.ppermute(block, axis, route)


def group_of(layers_j, size):
    return max(256 // (layers_j * size), 1)


def table_kernel(which, ham_cols, jump_cols, controls, controls_next, ham, jump, rows, jump_row, *refs):
    layers_h, count = ham_cols.shape
    layers_j = jump_cols.shape[0]
    size = ham.shape[-1]
    crossed = [(k, other) for k in range(layers_j) for other in range(layers_j) if k != other]
    *tables, came = refs
    group = jump_row.shape[1] // size
    first_k = 2 * layers_h
    first_j = first_k + 1 + len(crossed)

    @pl.loop(0, count, unroll=4)
    def _(b):
        for k in range(layers_h):
            rows[k, b] = ham_cols[k, b] * size
            rows[layers_h + k, ham_cols[k, b]] = b * size
            came[k, ham_cols[k, b]] = b
        for k in range(layers_j):
            rows[first_j + k, jump_cols[k, b]] = b * size
            came[layers_h + k, jump_cols[k, b]] = b

    def block_row(q, v):
        c = q * group + v
        came_h = [came[k, c] for k in range(layers_h)]
        came_j = [came[layers_h + k, c] for k in range(layers_j)]
        rows[first_k, c] = c * size
        for at, (k, other) in enumerate(crossed):
            rows[first_k + 1 + at, c] = jump_cols[other, came_j[k]] * size

        def ham_row(term):
            parts = [ham[term, c, k].astype(F32) for k in range(layers_h)]
            parts += [ham[term, came_h[k], k].astype(F32).T for k in range(layers_h)]
            return jnp.concatenate(parts, axis=1)

        stored = [[jump[came_j[k], other] for other in range(layers_j)] for k in range(layers_j)]
        turned = [stored[k][k].astype(F32).T.astype(BF16) for k in range(layers_j)]
        empty = [jnp.zeros_like(piece) for piece in turned]
        jump_row[q, v * size : (v + 1) * size, :] = jnp.concatenate(empty * v + turned + empty * (group - 1 - v), axis=1)
        square = sum(jnp.dot(turned[k], stored[k][k], preferred_element_type=F32) for k in range(layers_j))
        blocks = [square] + [jnp.dot(turned[k], stored[k][other], preferred_element_type=F32) for k, other in crossed]
        decay = -0.5 * jnp.concatenate(blocks, axis=1)
        drift, steer = ham_row(0), ham_row(1)
        for at, (later, fine) in enumerate(which):
            amplitude = (controls, controls_next)[later][0, fine]
            coeffs = drift + amplitude * steer
            tables[2 * at][c] = jnp.concatenate([coeffs, decay], axis=1).astype(BF16)
            tables[2 * at + 1][c] = jnp.concatenate([-coeffs, decay], axis=1).astype(BF16)

    @pl.loop(0, count // group, unroll=2)
    def _(q):
        for v in range(group):
            block_row(q, v)


def operator_tables(which, ham_blocks, ham_cols, jump_blocks, jump_cols, controls, controls_next):
    layers_h, count = ham_cols.shape
    layers_j = jump_cols.shape[0]
    size = ham_blocks.shape[-1]
    layers_k = 1 + layers_j * (layers_j - 1)
    smem = pl.BlockSpec(memory_space=pltpu.SMEM)
    vmem = pl.BlockSpec(memory_space=pltpu.VMEM)
    table = jax.ShapeDtypeStruct((count, size, (2 * layers_h + layers_k) * size), BF16)
    number = len(which)
    group = group_of(layers_j, size)
    rows, jump_row, *tables = pl.pallas_call(
        functools.partial(table_kernel, which),
        out_shape=[
            jax.ShapeDtypeStruct((2 * layers_h + layers_k + layers_j, count), jnp.int32),
            jax.ShapeDtypeStruct((count // group, group * size, group * layers_j * size), BF16),
        ] + [table] * (2 * number),
        in_specs=[smem, smem, smem, smem, vmem, vmem],
        out_specs=[smem, vmem] + [vmem] * (2 * number),
        scratch_shapes=[pltpu.SMEM((layers_h + layers_j, count), jnp.int32)],
        compiler_params=pltpu.CompilerParams(vmem_limit_bytes=60 * 2**20),
        cost_estimate=pl.CostEstimate(flops=1, bytes_accessed=1, transcendentals=0),
        name="operator_tables",
    )(ham_cols, jump_cols, controls, controls_next, ham_blocks, jump_blocks)
    return (2 * layers_h, layers_k, layers_j), rows, jump_row, *tables


class Step:
    def __init__(self, rows, counts, size, plus, minus, jump):
        self.rows, self.counts, self.size = rows, counts, size
        self.plus, self.minus, self.jump = plus, minus, jump
        self.group = jump.shape[1] // size

    def take(self, ref, kind, c, cols):
        first = sum(self.counts[:kind])
        return [
            ref[pl.ds(pl.multiple_of(self.rows[first + k, c], self.size), self.size), cols]
            for k in range(self.counts[kind])
        ]

    def ham(self, table, c, ham_ref, decay_ref, cols):
        met = jnp.concatenate(self.take(ham_ref, 0, c, cols) + self.take(decay_ref, 1, c, cols), axis=0)
        return jnp.dot(table[c], met, preferred_element_type=F32)

    def pull(self, q, ref, cols):
        met = jnp.concatenate(sum((self.take(ref, 2, q * self.group + v, cols) for v in range(self.group)), []), axis=0)
        return jnp.dot(self.jump[q], met, preferred_element_type=F32)

    def flat(self, kind, table, q, cols, *refs):
        if kind == "pull":
            return [self.pull(q, *refs, cols)]
        return [self.ham(table, q * self.group + v, *refs, cols) for v in range(self.group)]


def turn_whole(source, target, tile):
    n = source.shape[0] // tile

    @pl.loop(0, n)
    def _(i):
        near = pl.ds(pl.multiple_of(i * tile, tile), tile)
        for j in range(n):
            far = pl.ds(j * tile, tile)
            target[far, near] = source[near, far].T


def load_all(copies, sems):
    copies = [pltpu.make_async_copy(source, target, sems.at[k]) for k, (source, target) in enumerate(copies)]
    for copy in copies:
        copy.start()
    for copy in copies:
        copy.wait()


def part_of(first, k, tile):
    return pl.ds(pl.multiple_of(first + k * tile, tile), tile)


def assemble_first(place, near, near_pair, far, far_pair, c_ref, d_ref, stage, other, sems, tile):
    half, width = far.shape
    here, there = place[2], half - place[2]
    own, pair = place[3], width - place[3]

    def cols(first):
        return pl.ds(pl.multiple_of(first, width), width)

    copies = [
        (far, other.at[pl.ds(0, half), cols(own)]),
        (far_pair, other.at[pl.ds(0, half), cols(pair)]),
    ]
    for k in range(2):
        copies.append((near.at[0, k], stage.at[:, cols(k * half + own)]))
        copies.append((near_pair.at[0, k], stage.at[:, cols(k * half + pair)]))
    load_all(copies, sems)

    def mixed(rows, j):
        real = stage[rows, pl.ds(j * tile, tile)].astype(F32)
        imag = stage[rows, pl.ds(half + j * tile, tile)].astype(F32)
        return (real + imag).astype(BF16), (real - imag).astype(BF16)

    @pl.loop(0, half // tile, unroll=2)
    def _(i):
        here_i, there_i = part_of(here, i, tile), part_of(there, i, tile)
        for j in range(half // tile):
            here_j, there_j = part_of(here, j, tile), part_of(there, j, tile)
            total, less = mixed(there_i, j)
            c_ref[there_i, here_j] = total
            d_ref[there_i, here_j] = less
            c_ref[here_j, there_i] = less.T
            d_ref[here_j, there_i] = total.T
            block = other[part_of(0, i, tile), pl.ds(j * tile, tile)]
            c_ref[there_i, there_j] = block
            d_ref[there_j, there_i] = block.T
            total, less = mixed(here_i, j)
            c_ref[here_i, here_j] = total
            d_ref[here_i, here_j] = less


def assemble_next(place, pieces, c_ref, d_ref, stage, other, sems, tile):
    half, width = pieces[0].shape
    here, there = place[2], half - place[2]
    copies = []
    for (near, upper, lower, far), core in ((pieces[:4], place[3]), (pieces[4:], width - place[3])):
        low = pl.ds(pl.multiple_of(core, width), width)
        high = pl.ds(pl.multiple_of(half + core, width), width)
        rows = pl.ds(0, half)
        copies += [(near, other.at[rows, low]), (far, other.at[rows, high])]
        top = upper.shape[1]
        for k, to in enumerate((low, high)):
            copies.append((upper.at[k], stage.at[pl.ds(0, top), to]))
            copies.append((lower.at[k], stage.at[pl.ds(top, half - top), to]))
    load_all(copies, sems)

    @pl.loop(0, half // tile, unroll=2)
    def _(i):
        rows = part_of(0, i, tile)
        here_i, there_i = part_of(here, i, tile), part_of(there, i, tile)
        for j in range(half // tile):
            here_j, there_j = part_of(here, j, tile), part_of(there, j, tile)
            real = stage[rows, pl.ds(j * tile, tile)].astype(F32)
            imag = stage[rows, pl.ds(half + j * tile, tile)].astype(F32)
            total, less = (real + imag).astype(BF16), (real - imag).astype(BF16)
            c_ref[there_i, here_j] = total
            d_ref[there_i, here_j] = less
            c_ref[here_j, there_i] = less.T
            d_ref[here_j, there_i] = total.T
            block = other[rows, pl.ds(j * tile, tile)]
            c_ref[here_i, here_j] = block
            d_ref[here_j, here_i] = block.T
            block = other[rows, pl.ds(half + j * tile, tile)]
            c_ref[there_i, there_j] = block
            d_ref[there_j, there_i] = block.T


def put_turned(step, target, cols, to, first, count, kind, table, *refs):
    rows = sum((step.flat(kind, table, first + v, cols, *refs) for v in range(count)), [])
    target[cols, to] = jnp.concatenate([piece.astype(BF16) for piece in rows], axis=0).T


def whole_step(step, c_ref, d_ref, r_ref, x_ref, c_new, d_new, tile):
    n = c_ref.shape[0]
    size = step.size
    count = tile // (step.group * size)

    @pl.loop(0, n // tile)
    def _(g):
        to = part_of(0, g, tile)

        @pl.loop(0, n // tile, unroll=8)
        def _(s):
            cols = part_of(0, s, tile)
            put_turned(step, r_ref, cols, to, g * count, count, "ham", step.minus, c_ref, d_ref)
            put_turned(step, x_ref, cols, to, g * count, count, "pull", None, d_ref)

    @pl.loop(0, n // tile)
    def _(g):
        @pl.loop(0, n // tile, unroll=8)
        def _(s):
            cols = part_of(0, s, tile)
            made = []
            for q in range(count):
                pulled = step.pull(g * count + q, x_ref, cols)
                for v in range(step.group):
                    c = (g * count + q) * step.group + v
                    own = pl.ds(pl.multiple_of(c * size, size), size)
                    change = step.ham(step.plus, c, d_ref, c_ref, cols) + pulled[v * size : (v + 1) * size]
                    change = change + r_ref[own, cols].astype(F32)
                    made.append((c_ref[own, cols].astype(F32) + time_step * change).astype(BF16))
                    c_new[own, cols] = made[-1]
            d_new[cols, part_of(0, g, tile)] = jnp.concatenate(made, axis=0).T


def own_step(step, start, width, c_ref, d_ref, turned, tile, base, out):
    n = c_ref.shape[0]
    part = min(tile, width)
    size = step.size
    deep = step.group * size
    count = part // deep
    kinds = (
        ("ham", step.minus, c_ref, d_ref),
        ("ham", step.plus, d_ref, c_ref),
        ("pull", None, d_ref),
        ("pull", None, c_ref),
    )

    @pl.loop(0, width // part)
    def _(g):
        @pl.loop(0, n // tile, unroll=8)
        def _(s):
            for k, kind in enumerate(kinds):
                to = part_of(k * width, g, part)
                put_turned(step, turned, part_of(0, s, tile), to, start // deep + g * count, count, *kind)

    @pl.loop(0, n // deep, unroll=8)
    def _(q):
        for s in range(width // part):
            cols = pl.ds(pl.multiple_of(start + s * part, part), part)
            to = pl.ds(s * part, part)
            of = [pl.ds(k * width + s * part, part) for k in range(4)]
            pulled = [step.pull(q, turned, of[k]) for k in (2, 3)]
            for v in range(step.group):
                c = q * step.group + v
                own = pl.ds(pl.multiple_of(c * size, size), size)
                here = slice(v * size, (v + 1) * size)
                change = step.ham(step.plus, c, d_ref, c_ref, cols) + pulled[0][here]
                second = step.ham(step.minus, c, c_ref, d_ref, cols) + pulled[1][here]
                change = change + turned[own, of[0]].astype(F32)
                second = second + turned[own, of[1]].astype(F32)
                real, imag = base(own, cols, to)
                out[0, 0, own, to] = (real + 0.5 * time_step * (change + second)).astype(BF16)
                out[0, 1, own, to] = (imag + 0.5 * time_step * (change - second)).astype(BF16)


def fill_whole(piece, c_ref, d_ref, sems, tile):
    load_all([(piece, c_ref)], sems)
    turn_whole(c_ref, d_ref, tile)


def inner_kernel(counts, tile, number, rows, place, terminal, jump, plus, minus, *refs):
    pieces, refs = refs[:number], refs[number:]
    out, c_ref, d_ref, stage, turned, sems = refs
    n, width = out.shape[2], out.shape[3]
    if number == 1:
        fill_whole(pieces[0], c_ref, d_ref, sems, tile)
        load_all([(terminal.at[0, k], stage.at[:, pl.ds(k * width, width)]) for k in range(2)], sems)
        starts = (0, width)
    else:
        assemble_first(place, terminal, *pieces, c_ref, d_ref, stage, turned, sems, tile)
        starts = (place[3], place[3] + 2 * width)
    step = Step(rows, counts, plus.shape[1], plus, minus, jump)

    def base(own, _, cols):
        part = cols.size
        return [
            stage[own, pl.ds(pl.multiple_of(first + cols.start, part), part)].astype(F32) for first in starts
        ]

    own_step(step, place[0], width, c_ref, d_ref, turned, tile, base, out)


def start_kernel(counts, tile, number, rows, place, terminal, jump, plus, minus, plus_two, minus_two, *refs):
    pieces, refs = refs[:number], refs[number:]
    out, c_ref, d_ref, r_ref, x_ref, c_new, d_new, sems = refs
    size = plus.shape[1]

    @pl.when(place[1] == 1)
    def _():
        load_all([(terminal, out)], sems)

    @pl.when(place[1] == 0)
    def _():
        if number == 1:
            fill_whole(pieces[0], c_ref, d_ref, sems, tile)
        else:
            assemble_next(place, pieces, c_ref, d_ref, r_ref, x_ref, sems, tile)
        whole_step(Step(rows, counts, size, plus, minus, jump), c_ref, d_ref, r_ref, x_ref, c_new, d_new, tile)

        def base(own, cols, _):
            first, second = c_new[own, cols].astype(F32), d_new[own, cols].astype(F32)
            return 0.5 * (first + second), 0.5 * (first - second)

        step = Step(rows, counts, size, plus_two, minus_two, jump)
        own_step(step, place[0], out.shape[3], c_new, d_new, r_ref, tile, base, out)


def swapped(block, bit):
    return lax.ppermute(block, "row", [(i, i ^ bit) for i in range(lax.axis_size("row"))])


def on_device(terminal, controls, ham_blocks, ham_cols, jump_blocks, jump_cols):
    n, width = terminal.shape[2], terminal.shape[3]
    tile = 256
    row = lax.axis_index("row")
    here = row // 2 * 2 * width
    controls_next = shifted_down(controls, "tm")
    is_last = lax.axis_index("tm") == lax.axis_size("tm") - 1
    place = jnp.stack([row * width, is_last.astype(jnp.int32), here, row % 2 * width]).astype(jnp.int32)
    operators = (ham_blocks, ham_cols, jump_blocks, jump_cols)

    smem = pl.BlockSpec(memory_space=pltpu.SMEM)
    vmem = pl.BlockSpec(memory_space=pltpu.VMEM)
    anywhere = pl.BlockSpec(memory_space=pl.ANY)
    square = pltpu.VMEM((n, n), BF16)

    def step_call(kernel, name, squares, rows, tables, pieces):
        return pl.pallas_call(
            functools.partial(kernel, counts, tile, len(pieces)),
            out_shape=jax.ShapeDtypeStruct(terminal.shape, BF16),
            in_specs=[smem, smem, anywhere] + [vmem] * len(tables) + [anywhere] * len(pieces),
            out_specs=vmem,
            scratch_shapes=[square] * squares + [pltpu.SemaphoreType.DMA((12,))],
            compiler_params=pltpu.CompilerParams(vmem_limit_bytes=60 * 2**20),
            cost_estimate=pl.CostEstimate(flops=1, bytes_accessed=1, transcendentals=0),
            name=name,
        )(rows, place, terminal, *tables, *pieces)

    counts, rows, *tables = operator_tables(((0, 1), (1, 1), (1, 0)), *operators, controls, controls_next)
    first, second = tables[:3], tables[:1] + tables[3:]
    if lax.axis_size("row") == 4:
        near_pair = swapped(terminal, 1)
        halves = terminal.reshape(2, 2, 2 * width, width)
        chip, top = row // 2, 5 * width // 4

        def cut(first, count, which, low, high):
            return lax.dynamic_slice(halves, (first, which, low, 0), (count, 1, high - low, width))[:, 0]

        mixed = (cut(0, 1, chip, 0, 2 * width)[0].astype(F32) + cut(1, 1, chip, 0, 2 * width)[0].astype(F32)).astype(BF16)
        near = shifted_down(mixed, "tm")
        across, controls_next = lax.optimization_barrier((mixed, controls_next))
        far = swapped(across, 2)
        upper = shifted_down(cut(0, 2, 1 - chip, 0, top), "tm")
        lower = shifted_down(cut(0, 2, 1 - chip, top, 2 * width), "tm")
        far, rows = lax.optimization_barrier((far, rows))
        far_pair = swapped(far, 1)
        rows, mixed = lax.optimization_barrier((rows, near))
        far_next = swapped(mixed, 2)
        new_fpoint = step_call(inner_kernel, "inner_point", 4, rows, first, [near_pair, far, far_pair])
        mixed_pair = swapped(mixed, 1)
        upper, far_next, mixed_pair, new_fpoint = lax.optimization_barrier((upper, far_next, mixed_pair, new_fpoint))
        pieces = [mixed, upper, lower, far_next]
        pieces += [mixed_pair] + [swapped(piece, 1) for piece in pieces[1:]]
    else:
        mixed = (terminal[0, 0].astype(F32) + terminal[0, 1].astype(F32)).astype(BF16)

        def gathered(piece):
            return [lax.all_gather(piece, "row", axis=1, tiled=True)]

        new_fpoint = step_call(inner_kernel, "inner_point", 4, rows, first, gathered(mixed))
        pieces = gathered(shifted_down(mixed, "tm"))
    new_cpoint = step_call(start_kernel, "left_end", 6, rows, second, pieces)
    return (new_cpoint, new_fpoint)


def solution(mesh):
    in_specs = (P(("grp", "tm"), None, None, "row"), P(("grp", "tm"), None), P(), P(), P(), P())
    out_specs = (P(("grp", "tm"), None, None, "row"), P(("grp", "tm"), None, None, "row"))
    return jax.shard_map(
        on_device, mesh=mesh, in_specs=in_specs, out_specs=out_specs, check_vma=False
    )
```
